32 devices in a mesh: groups: 1, seq: 16 (over z, y, x), chan: 2 (over core).
Axes of the slice: x: 2, y: 2, z: 4, core: 2. Of those that a mesh axis runs over, the one named last changes fastest.
Arguments:
- q_proj: bfloat16 [4096, 2048], P('chan', ('groups', 'seq')), may hold values from -6 to 6
- k_proj: bfloat16 [4096, 2048], P('chan', ('groups', 'seq')), may hold values from -6 to 6
- value_projection: bfloat16 [4096, 2048], P('chan', ('groups', 'seq')), may hold values from -6 to 6
- residues: float32 [4096, 16], P(('chan', 'seq')), may hold values from -1.5 to 1.5
- rates: float32 [4096, 16], P(('chan', 'seq')), may hold values from 9.765625e-06 to 0.03
- direct_gain: float32 [4096], P('chan'), may hold values from 0.5 to 1.5
Outputs:
- mixed: bfloat16 [4096, 2048], P('chan', ('groups', 'seq'))
The draws below stay inside these ranges and needn't reach their ends.
All inputs are finite; a program needn't handle non-finite values.
Results may differ from the reference program's by a relative error of at most 0.001.
Values sent between devices are 32-bit elements; how exact they have to be, the bound alone decides.
No kernel may reach another device: no remote copies, remote signals or barrier semaphores. Data moves between devices by JAX's collectives and lax.ppermute only.
A program may use at most 64 MiB of HBM per device.

```python
import math
import jax
import jax.numpy as jnp
from jax import lax

D = 4096
ORDER = 16
SEQUENCE_LENGTH = 2048


def steps_of(rng, extent, split, smallest, high):
    factor_of = 1.0
    for dim, blocks in split:
        draws = jax.random.uniform(jax.random.fold_in(jax.random.fold_in(rng, 6), dim), (blocks,), jnp.float32, smallest / len(split), high / len(split))
        factor_of = factor_of * jnp.repeat(jnp.exp(draws), extent[dim] // blocks).reshape((-1,) + (1,) * (len(extent) - 1 - dim))
    return factor_of


def normal_values(rng, extent, scale, most, cuts=(), held_as=jnp.bfloat16):
    values = jax.random.normal(rng, extent, jnp.float32) * scale
    if len(cuts) > 0:
        values = steps_of(rng, extent, cuts, -0.22, 0.18) * values
    return jnp.clip(values, min=-most, max=most).astype(held_as)


def setup_inputs(seed: int = 0, part: int = 0) -> dict:
    keys = jax.random.split(jax.random.key(seed), 7)
    part_keys = jax.random.split(jax.random.fold_in(keys[6], part), 7)
    return {
        "q_proj": normal_values(part_keys[0], (D, SEQUENCE_LENGTH), 1.0, 6.0, ((0, 2), (1, 16))),
        "k_proj": normal_values(part_keys[1], (D, SEQUENCE_LENGTH), 1.0, 6.0, ((0, 2), (1, 16))),
        "value_projection": normal_values(part_keys[2], (D, SEQUENCE_LENGTH), 1.0, 6.0, ((0, 2), (1, 16))),
        "residues": normal_values(keys[3], (D, ORDER), 0.25, 1.5, ((0, 32),), jnp.float32),
        "rates": jnp.clip(jnp.exp(math.log(0.03) - 8.030084 * jax.random.uniform(keys[4], (D, ORDER), jnp.float32) ** steps_of(keys[4], (D, ORDER), ((0, 32),), -0.2, 0.2)), 9.765624781721272e-06, 0.03),
        "direct_gain": jnp.clip(0.5 + 1.0 * jax.random.uniform(keys[5], (D,), jnp.float32) ** steps_of(keys[5], (D,), ((0, 2),), -0.2, 0.2), 0.5, 1.5),
    }


def reference(q_proj, k_proj, value_projection, residues, rates, direct_gain):
    gated = k_proj.astype(jnp.float32) * value_projection.astype(jnp.float32)
    weights = residues * jnp.sqrt(-jnp.expm1(-2.0 * rates))
    steps_all = jnp.arange(SEQUENCE_LENGTH).astype(jnp.float32)
    group = 32
    length = 2 * SEQUENCE_LENGTH

    def one_group(pieces):
        signal, weight_matrix, decay = pieces
        decay_powers = jnp.exp(-decay[:, :, None] * steps_all[None, None, :])
        filter_taps = jnp.einsum('nh,nhp->np', weight_matrix, decay_powers, precision=lax.Precision.HIGHEST)
        spectrum = jnp.fft.rfft(signal, n=length) * jnp.fft.rfft(filter_taps, n=length)
        return jnp.fft.irfft(spectrum, n=length)[:, :SEQUENCE_LENGTH].astype(jnp.float32)
    conv = lax.map(one_group, (gated.reshape(D // group, group, SEQUENCE_LENGTH), weights.reshape(D // group, group, ORDER), rates.reshape(D // group, group, ORDER)))
    conv = conv.reshape(D, SEQUENCE_LENGTH)
    mixed = q_proj.astype(jnp.float32) * (conv + direct_gain[:, None] * gated)
    return mixed.astype(jnp.bfloat16)
```

```python
import functools
import jax
import jax.numpy as jnp
from jax import lax
from jax.experimental import pallas as pl
from jax.experimental.pallas import tpu as pltpu
from jax.sharding import PartitionSpec as P

LANES = 128
SUBLANES = 8
UNROLL = 8
VMEM_LIMIT = 32 * 1024 * 1024


def prepare_kernel(chunks, k_ref, v_ref, series_ref):
    length = k_ref.shape[1]
    for chunk in range(chunks):
        rows = pl.ds(chunk * LANES, LANES)
        gated = k_ref[rows, :].astype(jnp.float32) * v_ref[rows, :].astype(jnp.float32)
        series_ref[pl.ds(chunk, length, stride=chunks), :] = gated.T


def mode_rows(ref, base, order, per_chunk, chunks, half):
    first = half * SUBLANES * per_chunk + base
    return [ref[pl.ds(first + r, SUBLANES, stride=per_chunk), :] for r in range(order)]


def state_kernel(chunks, order, params_ref, series_ref, state_ref):
    length = series_ref.shape[0] // chunks
    for half in range(chunks // SUBLANES):
        decay = [jnp.exp(-rate) for rate in mode_rows(params_ref, 0, order, 2 * order, chunks, half)]

        def steps(i, state):
            state = list(state)
            for u in range(UNROLL):
                row = pl.multiple_of((i * UNROLL + u) * chunks + half * SUBLANES, SUBLANES)
                x = series_ref[pl.ds(row, SUBLANES), :]
                for r in range(order):
                    state[r] = decay[r] * state[r] + x
            return tuple(state)

        zero = jnp.zeros((SUBLANES, LANES), jnp.float32)
        state = lax.fori_loop(0, length // UNROLL, steps, (zero,) * order)
        for r in range(order):
            state_ref[pl.ds(half * SUBLANES * order + r, SUBLANES, stride=order), :] = state[r]


def prefix_kernel(length, rate_ref, ends_ref, starts_ref):
    span_decay = jnp.exp(-float(length) * rate_ref[...])
    carry = jnp.zeros(rate_ref.shape, jnp.float32)
    for block in range(ends_ref.shape[0]):
        starts_ref[block] = carry
        carry = span_decay * carry + ends_ref[block]


def tree_sum(terms):
    terms = list(terms)
    while len(terms) > 1:
        terms = [terms[i] + terms[i + 1] if i + 1 < len(terms) else terms[i] for i in range(0, len(terms), 2)]
    return terms[0]


def output_kernel(chunks, order, params_ref, series_ref, carry_ref, gain_ref, q_ref, out_ref, conv_ref):
    length = series_ref.shape[0] // chunks
    for half in range(chunks // SUBLANES):
        decay = [jnp.exp(-rate) for rate in mode_rows(params_ref, 0, order, 2 * order, chunks, half)]
        weight = mode_rows(params_ref, order, order, 2 * order, chunks, half)
        carry = mode_rows(carry_ref, 0, order, order, chunks, half)
        gain = gain_ref[pl.ds(half * SUBLANES, SUBLANES), :]

        def steps(i, state):
            state = list(state)
            for u in range(UNROLL):
                row = pl.multiple_of((i * UNROLL + u) * chunks + half * SUBLANES, SUBLANES)
                x = series_ref[pl.ds(row, SUBLANES), :]
                for r in range(order):
                    state[r] = decay[r] * state[r] + x
                terms = [weight[r] * state[r] for r in range(order)]
                conv_ref[pl.ds(row, SUBLANES), :] = tree_sum(terms + [gain * x])
            return tuple(state)

        lax.fori_loop(0, length // UNROLL, steps, tuple(carry))
    for chunk in range(chunks):
        rows = pl.ds(chunk * LANES, LANES)
        conv = conv_ref[pl.ds(chunk, length, stride=chunks), :].T
        out_ref[rows, :] = (q_ref[rows, :].astype(jnp.float32) * conv).astype(jnp.bfloat16)


def call(kernel, out_shape, *args, scratch=(), flops=0):
    in_bytes = sum(a.size * a.dtype.itemsize for a in args)
    vmem = pl.BlockSpec(memory_space=pltpu.VMEM)
    return pl.pallas_call(
        kernel,
        out_shape=out_shape,
        in_specs=[vmem] * len(args),
        out_specs=vmem,
        scratch_shapes=list(scratch),
        compiler_params=pltpu.CompilerParams(vmem_limit_bytes=VMEM_LIMIT),
        cost_estimate=pl.CostEstimate(flops=flops, bytes_accessed=in_bytes, transcendentals=0),
    )(*args)


def to_chunks(pieces):
    owners, rows, own = pieces.shape
    if own == LANES:
        return pieces
    if own < LANES:
        group = LANES // own
        return pieces.reshape(owners // group, group, rows, own).swapaxes(1, 2).reshape(-1, rows, LANES)
    return pieces.reshape(owners, rows, own // LANES, LANES).swapaxes(1, 2).reshape(-1, rows, LANES)


def from_chunks(pieces, owners):
    chunks, rows, _ = pieces.shape
    own = chunks * LANES // owners
    if own == LANES:
        return pieces
    if own < LANES:
        group = LANES // own
        return pieces.reshape(chunks, rows, group, own).swapaxes(1, 2).reshape(owners, rows, own)
    return pieces.reshape(owners, own // LANES, rows, LANES).swapaxes(1, 2).reshape(owners, rows, own)


def shards(blocks, q_proj, k_proj, value_projection, residues, rates, direct_gain):
    channels, length = q_proj.shape
    order = residues.shape[1]
    chunks = channels // LANES
    f32 = jnp.float32

    weights = residues * jnp.sqrt(-jnp.expm1(-2.0 * rates))
    own_rates = rates.T
    packed = jnp.concatenate([own_rates, weights.T], axis=0)
    gathered = lax.all_gather(packed, "seq", axis=0)
    params = to_chunks(gathered).reshape(chunks * 2 * order, LANES)

    series = call(
        functools.partial(prepare_kernel, chunks),
        jax.ShapeDtypeStruct((length * chunks, LANES), f32),
        k_proj,
        value_projection,
        flops=channels * length,
    )
    ends = call(
        functools.partial(state_kernel, chunks, order),
        jax.ShapeDtypeStruct((chunks * order, LANES), f32),
        params,
        series,
        flops=2 * order * channels * length,
    )
    ends = from_chunks(ends.reshape(chunks, order, LANES), blocks)
    ends = lax.all_to_all(ends, "seq", split_axis=0, concat_axis=0, tiled=True)
    starts = call(
        functools.partial(prefix_kernel, length),
        jax.ShapeDtypeStruct(ends.shape, f32),
        own_rates,
        ends,
    )
    starts = lax.all_to_all(starts, "seq", split_axis=0, concat_axis=0, tiled=True)
    carry = to_chunks(starts).reshape(chunks * order, LANES)
    return call(
        functools.partial(output_kernel, chunks, order),
        jax.ShapeDtypeStruct((channels, length), jnp.bfloat16),
        params,
        series,
        carry,
        direct_gain.reshape(chunks, LANES),
        q_proj,
        scratch=[pltpu.VMEM((length * chunks, LANES), f32)],
        flops=4 * order * channels * length,
    )


def solution(mesh):
    return jax.shard_map(
        functools.partial(shards, mesh.shape["seq"]),
        mesh=mesh,
        in_specs=(
            P("chan", ("groups", "seq")),
            P("chan", ("groups", "seq")),
            P("chan", ("groups", "seq")),
            P(("chan", "seq"), None),
            P(("chan", "seq"), None),
            P("chan"),
        ),
        out_specs=P("chan", ("groups", "seq")),
        check_vma=False,
    )
```

```python
import functools
import jax
import jax.numpy as jnp
from jax import lax
from jax.experimental import pallas as pl
from jax.experimental.pallas import tpu as pltpu
from jax.sharding import PartitionSpec as P

LANES = 128
SUBLANES = 8
UNROLL = 8
MOST_PERMUTES = 16
VMEM_LIMIT = 32 * 1024 * 1024


def prepare_kernel(chunks, k_ref, v_ref, series_ref):
    length = k_ref.shape[1]
    for chunk in range(chunks):
        rows = pl.ds(chunk * LANES, LANES)
        gated = k_ref[rows, :].astype(jnp.float32) * v_ref[rows, :].astype(jnp.float32)
        series_ref[pl.ds(chunk, length, stride=chunks), :] = gated.T


def mode_rows(ref, base, order, per_chunk, chunks, half):
    first = half * SUBLANES * per_chunk + base
    return [ref[pl.ds(first + r, SUBLANES, stride=per_chunk), :] for r in range(order)]


def state_kernel(chunks, order, pieces, *refs):
    piece_refs, (series_ref, params_ref, state_ref) = refs[:pieces], refs[pieces:]
    length = series_ref.shape[0] // chunks
    rows = piece_refs[0].shape[0]
    me = lax.axis_index("seq") if pieces > 1 else 0
    for shift, piece_ref in enumerate(piece_refs):
        owner = lax.rem(me + pieces - shift, pieces)
        params_ref[pl.ds(pl.multiple_of(owner * rows, SUBLANES), rows), :] = piece_ref[...]
    for half in range(chunks // SUBLANES):
        decay = [jnp.exp(-rate) for rate in mode_rows(params_ref, 0, order, 2 * order, chunks, half)]

        def steps(i, state):
            state = list(state)
            for u in range(UNROLL):
                row = pl.multiple_of((i * UNROLL + u) * chunks + half * SUBLANES, SUBLANES)
                x = series_ref[pl.ds(row, SUBLANES), :]
                for r in range(order):
                    state[r] = decay[r] * state[r] + x
            return tuple(state)

        zero = jnp.zeros((SUBLANES, LANES), jnp.float32)
        state = lax.fori_loop(0, length // UNROLL, steps, (zero,) * order)
        for r in range(order):
            state_ref[pl.ds(half * SUBLANES * order + r, SUBLANES, stride=order), :] = state[r]


def prefix_kernel(length, rate_ref, ends_ref, starts_ref):
    span_decay = jnp.exp(-float(length) * rate_ref[...])
    carry = jnp.zeros(rate_ref.shape, jnp.float32)
    for block in range(ends_ref.shape[0]):
        starts_ref[block] = carry
        carry = span_decay * carry + ends_ref[block]


def tree_sum(terms):
    terms = list(terms)
    while len(terms) > 1:
        terms = [terms[i] + terms[i + 1] if i + 1 < len(terms) else terms[i] for i in range(0, len(terms), 2)]
    return terms[0]


def output_kernel(chunks, order, params_ref, series_ref, carry_ref, gain_ref, q_ref, out_ref, conv_ref):
    length = series_ref.shape[0] // chunks
    for half in range(chunks // SUBLANES):
        decay = [jnp.exp(-rate) for rate in mode_rows(params_ref, 0, order, 2 * order, chunks, half)]
        weight = mode_rows(params_ref, order, order, 2 * order, chunks, half)
        carry = mode_rows(carry_ref, 0, order, order, chunks, half)
        gain = gain_ref[pl.ds(half * SUBLANES, SUBLANES), :]

        def steps(i, state):
            state = list(state)
            for u in range(UNROLL):
                row = pl.multiple_of((i * UNROLL + u) * chunks + half * SUBLANES, SUBLANES)
                x = series_ref[pl.ds(row, SUBLANES), :]
                for r in range(order):
                    state[r] = decay[r] * state[r] + x
                terms = [weight[r] * state[r] for r in range(order)]
                conv_ref[pl.ds(row, SUBLANES), :] = tree_sum(terms + [gain * x])
            return tuple(state)

        lax.fori_loop(0, length // UNROLL, steps, tuple(carry))
    for chunk in range(chunks):
        rows = pl.ds(chunk * LANES, LANES)
        conv = conv_ref[pl.ds(chunk, length, stride=chunks), :].T
        out_ref[rows, :] = (q_ref[rows, :].astype(jnp.float32) * conv).astype(jnp.bfloat16)


def call(kernel, out_shape, *args, scratch=(), flops=0):
    in_bytes = sum(a.size * a.dtype.itemsize for a in args)
    vmem = pl.BlockSpec(memory_space=pltpu.VMEM)
    return pl.pallas_call(
        kernel,
        out_shape=out_shape,
        in_specs=[vmem] * len(args),
        out_specs=jax.tree.map(lambda _: vmem, out_shape),
        scratch_shapes=list(scratch),
        compiler_params=pltpu.CompilerParams(vmem_limit_bytes=VMEM_LIMIT),
        cost_estimate=pl.CostEstimate(flops=flops, bytes_accessed=in_bytes, transcendentals=0),
    )(*args)


def to_chunks(pieces):
    owners, rows, own = pieces.shape
    if own == LANES:
        return pieces
    if own < LANES:
        group = LANES // own
        return pieces.reshape(owners // group, group, rows, own).swapaxes(1, 2).reshape(-1, rows, LANES)
    return pieces.reshape(owners, rows, own // LANES, LANES).swapaxes(1, 2).reshape(-1, rows, LANES)


def from_chunks(pieces, owners):
    chunks, rows, _ = pieces.shape
    own = chunks * LANES // owners
    if own == LANES:
        return pieces
    if own < LANES:
        group = LANES // own
        return pieces.reshape(chunks, rows, group, own).swapaxes(1, 2).reshape(owners, rows, own)
    return pieces.reshape(owners, own // LANES, rows, LANES).swapaxes(1, 2).reshape(owners, rows, own)


def shards(blocks, q_proj, k_proj, value_projection, residues, rates, direct_gain):
    channels, length = q_proj.shape
    order = residues.shape[1]
    chunks = channels // LANES
    f32 = jnp.float32

    weights = residues * jnp.sqrt(-jnp.expm1(-2.0 * rates))
    own_rates = rates.T
    packed = jnp.concatenate([own_rates, weights.T], axis=0)
    if blocks <= MOST_PERMUTES and blocks == chunks:
        pieces = [packed]
        for shift in range(1, blocks):
            pairs = [(i, (i + shift) % blocks) for i in range(blocks)]
            pieces.append(lax.ppermute(packed, "seq", pairs))
    else:
        gathered = lax.all_gather(packed, "seq", axis=0)
        pieces = [to_chunks(gathered).reshape(chunks * 2 * order, LANES)]

    series = call(
        functools.partial(prepare_kernel, chunks),
        jax.ShapeDtypeStruct((length * chunks, LANES), f32),
        k_proj,
        value_projection,
        flops=channels * length,
    )
    params, ends = call(
        functools.partial(state_kernel, chunks, order, len(pieces)),
        (
            jax.ShapeDtypeStruct((chunks * 2 * order, LANES), f32),
            jax.ShapeDtypeStruct((chunks * order, LANES), f32),
        ),
        *pieces,
        series,
        flops=2 * order * channels * length,
    )
    ends = from_chunks(ends.reshape(chunks, order, LANES), blocks)
    ends = lax.all_to_all(ends, "seq", split_axis=0, concat_axis=0, tiled=True)
    starts = call(
        functools.partial(prefix_kernel, length),
        jax.ShapeDtypeStruct(ends.shape, f32),
        own_rates,
        ends,
    )
    starts = lax.all_to_all(starts, "seq", split_axis=0, concat_axis=0, tiled=True)
    carry = to_chunks(starts).reshape(chunks * order, LANES)
    return call(
        functools.partial(output_kernel, chunks, order),
        jax.ShapeDtypeStruct((channels, length), jnp.bfloat16),
        params,
        series,
        carry,
        direct_gain.reshape(chunks, LANES),
        q_proj,
        scratch=[pltpu.VMEM((length * chunks, LANES), f32)],
        flops=4 * order * channels * length,
    )


def solution(mesh):
    return jax.shard_map(
        functools.partial(shards, mesh.shape["seq"]),
        mesh=mesh,
        in_specs=(
            P("chan", ("groups", "seq")),
            P("chan", ("groups", "seq")),
            P("chan", ("groups", "seq")),
            P(("chan", "seq"), None),
            P(("chan", "seq"), None),
            P("chan"),
        ),
        out_specs=P("chan", ("groups", "seq")),
        check_vma=False,
    )
```

```python
import functools
import jax
import jax.numpy as jnp
from jax import lax
from jax.experimental import pallas as pl
from jax.experimental.pallas import tpu as pltpu
from jax.sharding import PartitionSpec as P

LANES = 128
SUBLANES = 8
UNROLL = 8
VMEM_LIMIT = 32 * 1024 * 1024


def prepare_kernel(chunks, k_ref, v_ref, series_ref):
    length = k_ref.shape[1]
    for chunk in range(chunks):
        rows = pl.ds(chunk * LANES, LANES)
        gated = k_ref[rows, :].astype(jnp.float32) * v_ref[rows, :].astype(jnp.float32)
        series_ref[pl.ds(chunk, length, stride=chunks), :] = gated.T


def mode_rows(ref, base, order, per_chunk, chunks, half):
    first = half * SUBLANES * per_chunk + base
    return [ref[pl.ds(first + r, SUBLANES, stride=per_chunk), :] for r in range(order)]


def state_kernel(chunks, order, params_ref, series_ref, state_ref):
    length = series_ref.shape[0] // chunks
    for half in range(chunks // SUBLANES):
        decay = [jnp.exp(-rate) for rate in mode_rows(params_ref, 0, order, 2 * order, chunks, half)]

        def steps(i, state):
            state = list(state)
            for u in range(UNROLL):
                row = pl.multiple_of((i * UNROLL + u) * chunks + half * SUBLANES, SUBLANES)
                x = series_ref[pl.ds(row, SUBLANES), :]
                for r in range(order):
                    state[r] = decay[r] * state[r] + x
            return tuple(state)

        zero = jnp.zeros((SUBLANES, LANES), jnp.float32)
        state = lax.fori_loop(0, length // UNROLL, steps, (zero,) * order)
        for r in range(order):
            state_ref[pl.ds(half * SUBLANES * order + r, SUBLANES, stride=order), :] = state[r]


def prefix_kernel(length, rate_ref, ends_ref, starts_ref):
    span_decay = jnp.exp(-float(length) * rate_ref[...])
    carry = jnp.zeros(rate_ref.shape, jnp.float32)
    for block in range(ends_ref.shape[0]):
        starts_ref[block] = carry
        carry = span_decay * carry + ends_ref[block]


def tree_sum(terms):
    terms = list(terms)
    while len(terms) > 1:
        terms = [terms[i] + terms[i + 1] if i + 1 < len(terms) else terms[i] for i in range(0, len(terms), 2)]
    return terms[0]


def output_kernel(chunks, order, params_ref, series_ref, carry_ref, gain_ref, q_ref, out_ref, conv_ref):
    length = series_ref.shape[0] // chunks
    for half in range(chunks // SUBLANES):
        decay = [jnp.exp(-rate) for rate in mode_rows(params_ref, 0, order, 2 * order, chunks, half)]
        weight = mode_rows(params_ref, order, order, 2 * order, chunks, half)
        carry = mode_rows(carry_ref, 0, order, order, chunks, half)
        gain = gain_ref[pl.ds(half * SUBLANES, SUBLANES), :]

        def steps(i, state):
            state = list(state)
            for u in range(UNROLL):
                row = pl.multiple_of((i * UNROLL + u) * chunks + half * SUBLANES, SUBLANES)
                x = series_ref[pl.ds(row, SUBLANES), :]
                for r in range(order):
                    state[r] = decay[r] * state[r] + x
                terms = [weight[r] * state[r] for r in range(order)]
                conv_ref[pl.ds(row, SUBLANES), :] = tree_sum(terms + [gain * x])
            return tuple(state)

        lax.fori_loop(0, length // UNROLL, steps, tuple(carry))
    for chunk in range(chunks):
        rows = pl.ds(chunk * LANES, LANES)
        conv = conv_ref[pl.ds(chunk, length, stride=chunks), :].T
        out_ref[rows, :] = (q_ref[rows, :].astype(jnp.float32) * conv).astype(jnp.bfloat16)


def call(kernel, out_shape, *args, scratch=(), flops=0):
    in_bytes = sum(a.size * a.dtype.itemsize for a in args)
    vmem = pl.BlockSpec(memory_space=pltpu.VMEM)
    return pl.pallas_call(
        kernel,
        out_shape=out_shape,
        in_specs=[vmem] * len(args),
        out_specs=jax.tree.map(lambda _: vmem, out_shape),
        scratch_shapes=list(scratch),
        compiler_params=pltpu.CompilerParams(vmem_limit_bytes=VMEM_LIMIT),
        cost_estimate=pl.CostEstimate(flops=flops, bytes_accessed=in_bytes, transcendentals=0),
    )(*args)


def to_chunks(pieces):
    owners, rows, own = pieces.shape
    if own == LANES:
        return pieces
    if own < LANES:
        group = LANES // own
        return pieces.reshape(owners // group, group, rows, own).swapaxes(1, 2).reshape(-1, rows, LANES)
    return pieces.reshape(owners, rows, own // LANES, LANES).swapaxes(1, 2).reshape(-1, rows, LANES)


def from_chunks(pieces, owners):
    chunks, rows, _ = pieces.shape
    own = chunks * LANES // owners
    if own == LANES:
        return pieces
    if own < LANES:
        group = LANES // own
        return pieces.reshape(chunks, rows, group, own).swapaxes(1, 2).reshape(owners, rows, own)
    return pieces.reshape(owners, own // LANES, rows, LANES).swapaxes(1, 2).reshape(owners, rows, own)


def shards(blocks, q_proj, k_proj, value_projection, residues, rates, direct_gain):
    channels, length = q_proj.shape
    order = residues.shape[1]
    chunks = channels // LANES
    f32 = jnp.float32

    weights = residues * jnp.sqrt(-jnp.expm1(-2.0 * rates))
    own_rates = rates.T
    packed = jnp.concatenate([own_rates, weights.T], axis=0)
    copies = jnp.broadcast_to(packed[None], (blocks,) + packed.shape)
    gathered = lax.all_to_all(copies, "seq", split_axis=0, concat_axis=0, tiled=True)
    params = to_chunks(gathered).reshape(chunks * 2 * order, LANES)

    series = call(
        functools.partial(prepare_kernel, chunks),
        jax.ShapeDtypeStruct((length * chunks, LANES), f32),
        k_proj,
        value_projection,
        flops=channels * length,
    )
    ends = call(
        functools.partial(state_kernel, chunks, order),
        jax.ShapeDtypeStruct((chunks * order, LANES), f32),
        params,
        series,
        flops=2 * order * channels * length,
    )
    ends = from_chunks(ends.reshape(chunks, order, LANES), blocks)
    ends = lax.all_to_all(ends, "seq", split_axis=0, concat_axis=0, tiled=True)
    starts = call(
        functools.partial(prefix_kernel, length),
        jax.ShapeDtypeStruct(ends.shape, f32),
        own_rates,
        ends,
    )
    starts = lax.all_to_all(starts, "seq", split_axis=0, concat_axis=0, tiled=True)
    carry = to_chunks(starts).reshape(chunks * order, LANES)
    return call(
        functools.partial(output_kernel, chunks, order),
        jax.ShapeDtypeStruct((channels, length), jnp.bfloat16),
        params,
        series,
        carry,
        direct_gain.reshape(chunks, LANES),
        q_proj,
        scratch=[pltpu.VMEM((length * chunks, LANES), f32)],
        flops=4 * order * channels * length,
    )


def solution(mesh):
    return jax.shard_map(
        functools.partial(shards, mesh.shape["seq"]),
        mesh=mesh,
        in_specs=(
            P("chan", ("groups", "seq")),
            P("chan", ("groups", "seq")),
            P("chan", ("groups", "seq")),
            P(("chan", "seq"), None),
            P(("chan", "seq"), None),
            P("chan"),
        ),
        out_specs=P("chan", ("groups", "seq")),
        check_vma=False,
    )
```

```python
import functools
import jax
import jax.numpy as jnp
from jax import lax
from jax.experimental import pallas as pl
from jax.experimental.pallas import tpu as pltpu
from jax.sharding import PartitionSpec as P

LANES = 128
SUBLANES = 8
UNROLL = 8
MEMBERS = 4
VMEM_LIMIT = 32 * 1024 * 1024


def prepare_kernel(places, k_ref, v_ref, series_ref):
    length = k_ref.shape[1]
    chunks = len(places)
    for chunk, place in enumerate(places):
        rows = pl.ds(place * LANES, LANES)
        gated = k_ref[rows, :].astype(jnp.float32) * v_ref[rows, :].astype(jnp.float32)
        series_ref[pl.ds(chunk, length, stride=chunks), :] = gated.T


def mode_rows(ref, base, order, per_chunk, chunks, half):
    first = half * SUBLANES * per_chunk + base
    return [ref[pl.ds(first + r, SUBLANES, stride=per_chunk), :] for r in range(order)]


def state_kernel(chunks, order, params_ref, series_ref, state_ref):
    length = series_ref.shape[0] // chunks
    for half in range(chunks // SUBLANES):
        decay = [jnp.exp(-rate) for rate in mode_rows(params_ref, 0, order, 2 * order, chunks, half)]

        def steps(i, state):
            state = list(state)
            for u in range(UNROLL):
                row = pl.multiple_of((i * UNROLL + u) * chunks + half * SUBLANES, SUBLANES)
                x = series_ref[pl.ds(row, SUBLANES), :]
                for r in range(order):
                    state[r] = decay[r] * state[r] + x
            return tuple(state)

        zero = jnp.zeros((SUBLANES, LANES), jnp.float32)
        state = lax.fori_loop(0, length // UNROLL, steps, (zero,) * order)
        for r in range(order):
            state_ref[pl.ds(half * SUBLANES * order + r, SUBLANES, stride=order), :] = state[r]


def prefix_kernel(length, rate_ref, ends_ref, starts_ref):
    span_decay = jnp.exp(-float(length) * rate_ref[...])
    carry = jnp.zeros(rate_ref.shape, jnp.float32)
    for block in range(ends_ref.shape[0]):
        starts_ref[block] = carry
        carry = span_decay * carry + ends_ref[block]


def plane_kernel(length, rate_ref, ends_ref, totals_ref):
    order = ends_ref.shape[2]
    span_decay = jnp.exp(-float(length) * rate_ref[:, :order, :])
    total = ends_ref[0]
    for block in range(1, ends_ref.shape[0]):
        total = span_decay * total + ends_ref[block]
    for plane in range(totals_ref.shape[0]):
        totals_ref[plane] = total


def planes_kernel(length, rate_ref, ends_ref, totals_ref, starts_ref):
    members, _, order, _ = ends_ref.shape
    mine = lax.axis_index("seq") // members
    rate = rate_ref[:, :order, :]
    plane_decay = jnp.exp(-float(length * members) * rate)
    carry = jnp.zeros(rate.shape, jnp.float32)
    for plane in range(totals_ref.shape[0] - 1):
        carry = jnp.where(plane < mine, plane_decay * carry + totals_ref[plane], carry)
    span_decay = jnp.exp(-float(length) * rate)
    for block in range(members):
        starts_ref[block] = carry
        if block + 1 < members:
            carry = span_decay * carry + ends_ref[block]


def tree_sum(terms):
    terms = list(terms)
    while len(terms) > 1:
        terms = [terms[i] + terms[i + 1] if i + 1 < len(terms) else terms[i] for i in range(0, len(terms), 2)]
    return terms[0]


def output_kernel(places, order, params_ref, series_ref, carry_ref, gain_ref, q_ref, out_ref, conv_ref):
    chunks = len(places)
    length = series_ref.shape[0] // chunks
    for half in range(chunks // SUBLANES):
        decay = [jnp.exp(-rate) for rate in mode_rows(params_ref, 0, order, 2 * order, chunks, half)]
        weight = mode_rows(params_ref, order, order, 2 * order, chunks, half)
        carry = mode_rows(carry_ref, 0, order, order, chunks, half)
        own = places[half * SUBLANES : (half + 1) * SUBLANES]
        gain = jnp.concatenate([gain_ref[pl.ds(place, 1), :] for place in own], axis=0)

        def steps(i, state):
            state = list(state)
            for u in range(UNROLL):
                row = pl.multiple_of((i * UNROLL + u) * chunks + half * SUBLANES, SUBLANES)
                x = series_ref[pl.ds(row, SUBLANES), :]
                for r in range(order):
                    state[r] = decay[r] * state[r] + x
                terms = [weight[r] * state[r] for r in range(order)]
                conv_ref[pl.ds(row, SUBLANES), :] = tree_sum(terms + [gain * x])
            return tuple(state)

        lax.fori_loop(0, length // UNROLL, steps, tuple(carry))
    for chunk, place in enumerate(places):
        rows = pl.ds(place * LANES, LANES)
        conv = conv_ref[pl.ds(chunk, length, stride=chunks), :].T
        out_ref[rows, :] = (q_ref[rows, :].astype(jnp.float32) * conv).astype(jnp.bfloat16)


def call(kernel, out_shape, *args, scratch=(), flops=0):
    in_bytes = sum(a.size * a.dtype.itemsize for a in args)
    vmem = pl.BlockSpec(memory_space=pltpu.VMEM)
    return pl.pallas_call(
        kernel,
        out_shape=out_shape,
        in_specs=[vmem] * len(args),
        out_specs=jax.tree.map(lambda _: vmem, out_shape),
        scratch_shapes=list(scratch),
        compiler_params=pltpu.CompilerParams(vmem_limit_bytes=VMEM_LIMIT),
        cost_estimate=pl.CostEstimate(flops=flops, bytes_accessed=in_bytes, transcendentals=0),
    )(*args)


def to_chunks(pieces):
    owners, rows, own = pieces.shape
    if own == LANES:
        return pieces
    if own < LANES:
        group = LANES // own
        return pieces.reshape(owners // group, group, rows, own).swapaxes(1, 2).reshape(-1, rows, LANES)
    return pieces.reshape(owners, rows, own // LANES, LANES).swapaxes(1, 2).reshape(-1, rows, LANES)


def from_chunks(pieces, owners):
    chunks, rows, _ = pieces.shape
    own = chunks * LANES // owners
    if own == LANES:
        return pieces
    if own < LANES:
        group = LANES // own
        return pieces.reshape(chunks, rows, group, own).swapaxes(1, 2).reshape(owners, rows, own)
    return pieces.reshape(owners, own // LANES, rows, LANES).swapaxes(1, 2).reshape(owners, rows, own)


def all_to_all(pieces, groups=None):
    return lax.all_to_all(pieces, "seq", split_axis=0, concat_axis=0, axis_index_groups=groups, tiled=True)


def copies(array, count):
    return jnp.broadcast_to(array[None], (count,) + array.shape)


def shards(blocks, q_proj, k_proj, value_projection, residues, rates, direct_gain):
    channels, length = q_proj.shape
    own, order = residues.shape
    chunks = channels // LANES
    f32 = jnp.float32
    two_level = own == LANES and blocks % MEMBERS == 0
    planes = blocks // MEMBERS
    if two_level:
        lines = [[plane * MEMBERS + member for plane in range(planes)] for member in range(MEMBERS)]
        layers = [[plane * MEMBERS + member for member in range(MEMBERS)] for plane in range(planes)]
        places = [plane * MEMBERS + member for member in range(MEMBERS) for plane in range(planes)]
    else:
        places = list(range(chunks))

    weights = residues * jnp.sqrt(-jnp.expm1(-2.0 * rates))
    own_rates = rates.T
    packed = jnp.concatenate([own_rates, weights.T], axis=0)
    if two_level:
        line_params = all_to_all(copies(packed, planes), lines)
        params = all_to_all(copies(line_params, MEMBERS), layers)
    else:
        params = to_chunks(all_to_all(copies(packed, blocks)))
    params = params.reshape(chunks * 2 * order, LANES)

    series = call(
        functools.partial(prepare_kernel, places),
        jax.ShapeDtypeStruct((length * chunks, LANES), f32),
        k_proj,
        value_projection,
        flops=channels * length,
    )
    ends = call(
        functools.partial(state_kernel, chunks, order),
        jax.ShapeDtypeStruct((chunks * order, LANES), f32),
        params,
        series,
        flops=2 * order * channels * length,
    )
    ends = ends.reshape(chunks, order, LANES)
    if two_level:
        ends = all_to_all(ends.reshape(MEMBERS, planes, order, LANES), layers)
        totals = call(
            functools.partial(plane_kernel, length),
            jax.ShapeDtypeStruct((planes, planes, order, LANES), f32),
            line_params,
            ends,
        )
        totals = all_to_all(totals, lines)
        starts = call(
            functools.partial(planes_kernel, length),
            jax.ShapeDtypeStruct(ends.shape, f32),
            line_params,
            ends,
            totals,
        )
        carry = all_to_all(starts, layers)
    else:
        ends = all_to_all(from_chunks(ends, blocks))
        starts = call(
            functools.partial(prefix_kernel, length),
            jax.ShapeDtypeStruct(ends.shape, f32),
            own_rates,
            ends,
        )
        carry = to_chunks(all_to_all(starts))
    return call(
        functools.partial(output_kernel, places, order),
        jax.ShapeDtypeStruct((channels, length), jnp.bfloat16),
        params,
        series,
        carry.reshape(chunks * order, LANES),
        direct_gain.reshape(chunks, LANES),
        q_proj,
        scratch=[pltpu.VMEM((length * chunks, LANES), f32)],
        flops=4 * order * channels * length,
    )


def solution(mesh):
    return jax.shard_map(
        functools.partial(shards, mesh.shape["seq"]),
        mesh=mesh,
        in_specs=(
            P("chan", ("groups", "seq")),
            P("chan", ("groups", "seq")),
            P("chan", ("groups", "seq")),
            P(("chan", "seq"), None),
            P(("chan", "seq"), None),
            P("chan"),
        ),
        out_specs=P("chan", ("groups", "seq")),
        check_vma=False,
    )
```

```python
import functools
import jax
import jax.numpy as jnp
from jax import lax
from jax.experimental import pallas as pl
from jax.experimental.pallas import tpu as pltpu
from jax.sharding import PartitionSpec as P

LANES = 128
SUBLANES = 8
UNROLL = 8
VMEM_LIMIT = 32 * 1024 * 1024


def prepare_kernel(chunks, k_ref, v_ref, series_ref):
    length = k_ref.shape[1]
    for chunk in range(chunks):
        rows = pl.ds(chunk * LANES, LANES)
        gated = k_ref[rows, :].astype(jnp.float32) * v_ref[rows, :].astype(jnp.float32)
        series_ref[pl.ds(chunk, length, stride=chunks), :] = gated.T


def mode_rows(ref, base, order, per_chunk, chunks, half):
    first = half * SUBLANES * per_chunk + base
    return [ref[pl.ds(first + r, SUBLANES, stride=per_chunk), :] for r in range(order)]


def state_kernel(chunks, order, params_ref, series_ref, state_ref):
    length = series_ref.shape[0] // chunks
    for half in range(chunks // SUBLANES):
        decay = [jnp.exp(-rate) for rate in mode_rows(params_ref, 0, order, 2 * order, chunks, half)]

        def steps(i, state):
            state = list(state)
            for u in range(UNROLL):
                row = pl.multiple_of((i * UNROLL + u) * chunks + half * SUBLANES, SUBLANES)
                x = series_ref[pl.ds(row, SUBLANES), :]
                for r in range(order):
                    state[r] = decay[r] * state[r] + x
            return tuple(state)

        zero = jnp.zeros((SUBLANES, LANES), jnp.float32)
        state = lax.fori_loop(0, length // UNROLL, steps, (zero,) * order)
        for r in range(order):
            state_ref[pl.ds(half * SUBLANES * order + r, SUBLANES, stride=order), :] = state[r]


def prefix_kernel(length, rate_ref, ends_ref, starts_ref):
    span_decay = jnp.exp(-float(length) * rate_ref[...])
    carry = jnp.zeros(rate_ref.shape, jnp.float32)
    for block in range(ends_ref.shape[0]):
        starts_ref[block] = carry
        carry = span_decay * carry + ends_ref[block]


def tree_sum(terms):
    terms = list(terms)
    while len(terms) > 1:
        terms = [terms[i] + terms[i + 1] if i + 1 < len(terms) else terms[i] for i in range(0, len(terms), 2)]
    return terms[0]


def one_minus_exp(y):
    series = jnp.ones_like(y)
    for k in range(11, 1, -1):
        series = 1.0 - (y * (1.0 / k)) * series
    return jnp.where(y < 0.5, y * series, 1.0 - jnp.exp(-y))


def local_kernel(chunks, order, gathered_ref, series_ref, gain_ref, conv_ref, weight_ref):
    length = series_ref.shape[0] // chunks
    for half in range(chunks // SUBLANES):
        rate = mode_rows(gathered_ref, 0, order, 2 * order, chunks, half)
        residue = mode_rows(gathered_ref, order, order, 2 * order, chunks, half)
        decay = [jnp.exp(-rate[r]) for r in range(order)]
        weight = [residue[r] * jnp.sqrt(one_minus_exp(2.0 * rate[r])) for r in range(order)]
        for r in range(order):
            weight_ref[pl.ds(half * SUBLANES * order + r, SUBLANES, stride=order), :] = weight[r]
        gain = gain_ref[pl.ds(half * SUBLANES, SUBLANES), :]

        def steps(i, state):
            state = list(state)
            for u in range(UNROLL):
                row = pl.multiple_of((i * UNROLL + u) * chunks + half * SUBLANES, SUBLANES)
                x = series_ref[pl.ds(row, SUBLANES), :]
                for r in range(order):
                    state[r] = decay[r] * state[r] + x
                terms = [weight[r] * state[r] for r in range(order)]
                conv_ref[pl.ds(row, SUBLANES), :] = tree_sum(terms + [gain * x])
            return tuple(state)

        zero = jnp.zeros((SUBLANES, LANES), jnp.float32)
        lax.fori_loop(0, length // UNROLL, steps, (zero,) * order)


def output_kernel(chunks, order, gathered_ref, weight_ref, carry_ref, local_ref, q_ref, out_ref, conv_ref):
    length = local_ref.shape[0] // chunks
    for half in range(chunks // SUBLANES):
        decay = [jnp.exp(-rate) for rate in mode_rows(gathered_ref, 0, order, 2 * order, chunks, half)]
        weight = mode_rows(weight_ref, 0, order, order, chunks, half)
        carry = mode_rows(carry_ref, 0, order, order, chunks, half)

        def steps(i, fading):
            fading = list(fading)
            for u in range(UNROLL):
                row = pl.multiple_of((i * UNROLL + u) * chunks + half * SUBLANES, SUBLANES)
                fading = [decay[r] * fading[r] for r in range(order)]
                conv_ref[pl.ds(row, SUBLANES), :] = tree_sum(fading + [local_ref[pl.ds(row, SUBLANES), :]])
            return tuple(fading)

        lax.fori_loop(0, length // UNROLL, steps, tuple(weight[r] * carry[r] for r in range(order)))
        for chunk in range(half * SUBLANES, (half + 1) * SUBLANES):
            rows = pl.ds(chunk * LANES, LANES)
            conv = conv_ref[pl.ds(chunk, length, stride=chunks), :].T
            out_ref[rows, :] = (q_ref[rows, :].astype(jnp.float32) * conv).astype(jnp.bfloat16)


def call(kernel, out_shape, *args, scratch=(), flops=0):
    in_bytes = sum(a.size * a.dtype.itemsize for a in args)
    vmem = pl.BlockSpec(memory_space=pltpu.VMEM)
    return pl.pallas_call(
        kernel,
        out_shape=out_shape,
        in_specs=[vmem] * len(args),
        out_specs=jax.tree.map(lambda _: vmem, out_shape),
        scratch_shapes=list(scratch),
        compiler_params=pltpu.CompilerParams(vmem_limit_bytes=VMEM_LIMIT),
        cost_estimate=pl.CostEstimate(flops=flops, bytes_accessed=in_bytes, transcendentals=0),
    )(*args)


def to_chunks(pieces):
    owners, rows, own = pieces.shape
    if own == LANES:
        return pieces
    if own < LANES:
        group = LANES // own
        return pieces.reshape(owners // group, group, rows, own).swapaxes(1, 2).reshape(-1, rows, LANES)
    return pieces.reshape(owners, rows, own // LANES, LANES).swapaxes(1, 2).reshape(-1, rows, LANES)


def from_chunks(pieces, owners):
    chunks, rows, _ = pieces.shape
    own = chunks * LANES // owners
    if own == LANES:
        return pieces
    if own < LANES:
        group = LANES // own
        return pieces.reshape(chunks, rows, group, own).swapaxes(1, 2).reshape(owners, rows, own)
    return pieces.reshape(owners, own // LANES, rows, LANES).swapaxes(1, 2).reshape(owners, rows, own)


def shards(blocks, q_proj, k_proj, value_projection, residues, rates, direct_gain):
    channels, length = q_proj.shape
    order = residues.shape[1]
    chunks = channels // LANES
    f32 = jnp.float32

    own_rates = rates.T
    packed = jnp.concatenate([own_rates, residues.T], axis=0)
    copies = jnp.broadcast_to(packed[None], (blocks,) + packed.shape)
    gathered = lax.all_to_all(copies, "seq", split_axis=0, concat_axis=0, tiled=True)
    params = to_chunks(gathered).reshape(chunks * 2 * order, LANES)

    series = call(
        functools.partial(prepare_kernel, chunks),
        jax.ShapeDtypeStruct((length * chunks, LANES), f32),
        k_proj,
        value_projection,
        flops=channels * length,
    )
    ends = call(
        functools.partial(state_kernel, chunks, order),
        jax.ShapeDtypeStruct((chunks * order, LANES), f32),
        params,
        series,
        flops=2 * order * channels * length,
    )
    local_series, ends = lax.optimization_barrier((series, ends))
    ends = from_chunks(ends.reshape(chunks, order, LANES), blocks)
    local, weights = call(
        functools.partial(local_kernel, chunks, order),
        (
            jax.ShapeDtypeStruct((length * chunks, LANES), f32),
            jax.ShapeDtypeStruct((chunks * order, LANES), f32),
        ),
        params,
        local_series,
        direct_gain.reshape(chunks, LANES),
        flops=4 * order * channels * length,
    )
    ends = lax.all_to_all(ends, "seq", split_axis=0, concat_axis=0, tiled=True)
    starts = call(
        functools.partial(prefix_kernel, length),
        jax.ShapeDtypeStruct(ends.shape, f32),
        own_rates,
        ends,
    )
    starts = lax.all_to_all(starts, "seq", split_axis=0, concat_axis=0, tiled=True)
    carry = to_chunks(starts).reshape(chunks * order, LANES)
    return call(
        functools.partial(output_kernel, chunks, order),
        jax.ShapeDtypeStruct((channels, length), jnp.bfloat16),
        params,
        weights,
        carry,
        local,
        q_proj,
        scratch=[pltpu.VMEM((length * chunks, LANES), f32)],
        flops=2 * order * channels * length,
    )


def solution(mesh):
    return jax.shard_map(
        functools.partial(shards, mesh.shape["seq"]),
        mesh=mesh,
        in_specs=(
            P("chan", ("groups", "seq")),
            P("chan", ("groups", "seq")),
            P("chan", ("groups", "seq")),
            P(("chan", "seq"), None),
            P(("chan", "seq"), None),
            P("chan"),
        ),
        out_specs=P("chan", ("groups", "seq")),
        check_vma=False,
    )
```

```python
import functools
import jax
import jax.numpy as jnp
from jax import lax
from jax.experimental import pallas as pl
from jax.experimental.pallas import tpu as pltpu
from jax.sharding import PartitionSpec as P

LANES = 128
SUBLANES = 8
UNROLL = 8
VMEM_LIMIT = 32 * 1024 * 1024


def mode_rows(ref, base, order, per_chunk, chunks, half):
    first = half * SUBLANES * per_chunk + base
    return [ref[pl.ds(first + r, SUBLANES, stride=per_chunk), :] for r in range(order)]


def state_kernel(chunks, order, params_ref, k_ref, v_ref, series_ref, state_ref):
    length = k_ref.shape[1]
    for chunk in range(chunks):
        rows = pl.ds(chunk * LANES, LANES)
        gated = k_ref[rows, :].astype(jnp.float32) * v_ref[rows, :].astype(jnp.float32)
        series_ref[pl.ds(chunk, length, stride=chunks), :] = gated.T
    for half in range(chunks // SUBLANES):
        decay = [jnp.exp(-rate) for rate in mode_rows(params_ref, 0, order, 2 * order, chunks, half)]

        def steps(i, state):
            state = list(state)
            for u in range(UNROLL):
                row = pl.multiple_of((i * UNROLL + u) * chunks + half * SUBLANES, SUBLANES)
                x = series_ref[pl.ds(row, SUBLANES), :]
                for r in range(order):
                    state[r] = decay[r] * state[r] + x
            return tuple(state)

        zero = jnp.zeros((SUBLANES, LANES), jnp.float32)
        state = lax.fori_loop(0, length // UNROLL, steps, (zero,) * order)
        for r in range(order):
            state_ref[pl.ds(half * SUBLANES * order + r, SUBLANES, stride=order), :] = state[r]


def prefix_kernel(length, rate_ref, ends_ref, starts_ref):
    span_decay = jnp.exp(-float(length) * rate_ref[...])
    carry = jnp.zeros(rate_ref.shape, jnp.float32)
    for block in range(ends_ref.shape[0]):
        starts_ref[block] = carry
        carry = span_decay * carry + ends_ref[block]


def tree_sum(terms):
    terms = list(terms)
    while len(terms) > 1:
        terms = [terms[i] + terms[i + 1] if i + 1 < len(terms) else terms[i] for i in range(0, len(terms), 2)]
    return terms[0]


def one_minus_exp(y):
    series = jnp.ones_like(y)
    for k in range(11, 1, -1):
        series = 1.0 - (y * (1.0 / k)) * series
    return jnp.where(y < 0.5, y * series, 1.0 - jnp.exp(-y))


def output_kernel(chunks, order, params_ref, series_ref, carry_ref, gain_ref, q_ref, out_ref, conv_ref):
    length = series_ref.shape[0] // chunks
    for half in range(chunks // SUBLANES):
        rate = mode_rows(params_ref, 0, order, 2 * order, chunks, half)
        residue = mode_rows(params_ref, order, order, 2 * order, chunks, half)
        decay = [jnp.exp(-rate[r]) for r in range(order)]
        weight = [residue[r] * jnp.sqrt(one_minus_exp(2.0 * rate[r])) for r in range(order)]
        carry = mode_rows(carry_ref, 0, order, order, chunks, half)
        gain = gain_ref[pl.ds(half * SUBLANES, SUBLANES), :]

        def steps(i, state):
            state = list(state)
            for u in range(UNROLL):
                row = pl.multiple_of((i * UNROLL + u) * chunks + half * SUBLANES, SUBLANES)
                x = series_ref[pl.ds(row, SUBLANES), :]
                for r in range(order):
                    state[r] = decay[r] * state[r] + x
                terms = [weight[r] * state[r] for r in range(order)]
                conv_ref[pl.ds(row, SUBLANES), :] = tree_sum(terms + [gain * x])
            return tuple(state)

        lax.fori_loop(0, length // UNROLL, steps, tuple(carry))
        for chunk in range(half * SUBLANES, (half + 1) * SUBLANES):
            rows = pl.ds(chunk * LANES, LANES)
            conv = conv_ref[pl.ds(chunk, length, stride=chunks), :].T
            out_ref[rows, :] = (q_ref[rows, :].astype(jnp.float32) * conv).astype(jnp.bfloat16)


def call(kernel, out_shape, *args, scratch=(), flops=0):
    in_bytes = sum(a.size * a.dtype.itemsize for a in args)
    vmem = pl.BlockSpec(memory_space=pltpu.VMEM)
    return pl.pallas_call(
        kernel,
        out_shape=out_shape,
        in_specs=[vmem] * len(args),
        out_specs=jax.tree.map(lambda _: vmem, out_shape),
        scratch_shapes=list(scratch),
        compiler_params=pltpu.CompilerParams(vmem_limit_bytes=VMEM_LIMIT),
        cost_estimate=pl.CostEstimate(flops=flops, bytes_accessed=in_bytes, transcendentals=0),
    )(*args)


def to_chunks(pieces):
    owners, rows, own = pieces.shape
    if own == LANES:
        return pieces
    if own < LANES:
        group = LANES // own
        return pieces.reshape(owners // group, group, rows, own).swapaxes(1, 2).reshape(-1, rows, LANES)
    return pieces.reshape(owners, rows, own // LANES, LANES).swapaxes(1, 2).reshape(-1, rows, LANES)


def from_chunks(pieces, owners):
    chunks, rows, _ = pieces.shape
    own = chunks * LANES // owners
    if own == LANES:
        return pieces
    if own < LANES:
        group = LANES // own
        return pieces.reshape(chunks, rows, group, own).swapaxes(1, 2).reshape(owners, rows, own)
    return pieces.reshape(owners, own // LANES, rows, LANES).swapaxes(1, 2).reshape(owners, rows, own)


def shards(blocks, q_proj, k_proj, value_projection, residues, rates, direct_gain):
    channels, length = q_proj.shape
    order = residues.shape[1]
    chunks = channels // LANES
    f32 = jnp.float32

    own_rates = rates.T
    packed = jnp.concatenate([own_rates, residues.T], axis=0)
    copies = jnp.broadcast_to(packed[None], (blocks,) + packed.shape)
    gathered = lax.all_to_all(copies, "seq", split_axis=0, concat_axis=0, tiled=True)
    params = to_chunks(gathered).reshape(chunks * 2 * order, LANES)

    series, ends = call(
        functools.partial(state_kernel, chunks, order),
        (
            jax.ShapeDtypeStruct((length * chunks, LANES), f32),
            jax.ShapeDtypeStruct((chunks * order, LANES), f32),
        ),
        params,
        k_proj,
        value_projection,
        flops=2 * order * channels * length,
    )
    ends = from_chunks(ends.reshape(chunks, order, LANES), blocks)
    ends = lax.all_to_all(ends, "seq", split_axis=0, concat_axis=0, tiled=True)
    starts = call(
        functools.partial(prefix_kernel, length),
        jax.ShapeDtypeStruct(ends.shape, f32),
        own_rates,
        ends,
    )
    starts = lax.all_to_all(starts, "seq", split_axis=0, concat_axis=0, tiled=True)
    carry = to_chunks(starts).reshape(chunks * order, LANES)
    return call(
        functools.partial(output_kernel, chunks, order),
        jax.ShapeDtypeStruct((channels, length), jnp.bfloat16),
        params,
        series,
        carry,
        direct_gain.reshape(chunks, LANES),
        q_proj,
        scratch=[pltpu.VMEM((length * chunks, LANES), f32)],
        flops=4 * order * channels * length,
    )


def solution(mesh):
    return jax.shard_map(
        functools.partial(shards, mesh.shape["seq"]),
        mesh=mesh,
        in_specs=(
            P("chan", ("groups", "seq")),
            P("chan", ("groups", "seq")),
            P("chan", ("groups", "seq")),
            P(("chan", "seq"), None),
            P(("chan", "seq"), None),
            P("chan"),
        ),
        out_specs=P("chan", ("groups", "seq")),
        check_vma=False,
    )
```

```python
import functools
import jax
import jax.numpy as jnp
from jax import lax
from jax.experimental import pallas as pl
from jax.experimental.pallas import tpu as pltpu
from jax.sharding import PartitionSpec as P

LANES = 128
SUBLANES = 8
UNROLL = 8
VMEM_LIMIT = 32 * 1024 * 1024


def half_rows(half, per_chunk, interleaved):
    if interleaved:
        return half * per_chunk, 2 * per_chunk
    return half * SUBLANES * per_chunk, per_chunk


def mode_rows(ref, base, order, per_chunk, half, interleaved):
    first, stride = half_rows(half, per_chunk, interleaved)
    return [ref[pl.ds(first + base + r, SUBLANES, stride=stride), :] for r in range(order)]


def state_kernel(chunks, order, interleaved, params_ref, k_ref, v_ref, series_ref, state_ref):
    length = k_ref.shape[1]
    for chunk in range(chunks):
        rows = pl.ds(chunk * LANES, LANES)
        gated = k_ref[rows, :].astype(jnp.float32) * v_ref[rows, :].astype(jnp.float32)
        series_ref[pl.ds(chunk, length, stride=chunks), :] = gated.T
    for half in range(chunks // SUBLANES):
        decay = [jnp.exp(-rate) for rate in mode_rows(params_ref, 0, order, 2 * order, half, interleaved)]

        def steps(i, state):
            state = list(state)
            for u in range(UNROLL):
                row = pl.multiple_of((i * UNROLL + u) * chunks + half * SUBLANES, SUBLANES)
                x = series_ref[pl.ds(row, SUBLANES), :]
                for r in range(order):
                    state[r] = decay[r] * state[r] + x
            return tuple(state)

        zero = jnp.zeros((SUBLANES, LANES), jnp.float32)
        state = lax.fori_loop(0, length // UNROLL, steps, (zero,) * order)
        first, stride = half_rows(half, order, interleaved)
        for r in range(order):
            state_ref[pl.ds(first + r, SUBLANES, stride=stride), :] = state[r]


def copies_kernel(members, own_ref, other_ref, copies_ref):
    own, other = own_ref[...], other_ref[...]
    lower = jnp.broadcast_to(lax.axis_index("seq") < members, own.shape)
    pair = (jnp.where(lower, own, other), jnp.where(lower, other, own))
    for member in range(members):
        for half in range(2):
            copies_ref[member, half] = pair[half]


def span_decay(length, order, rate_ref):
    rate = rate_ref[0, :, :order, :] if len(rate_ref.shape) == 4 else rate_ref[...]
    return jnp.exp(-float(length) * rate)


def total_kernel(length, rate_ref, ends_ref, total_ref):
    decay = span_decay(length, ends_ref.shape[-2], rate_ref)
    total = ends_ref[0]
    for block in range(1, ends_ref.shape[0]):
        total = decay * total + ends_ref[block]
    total_ref[...] = total


def prefix_kernel(length, rate_ref, ends_ref, carry_ref, starts_ref):
    decay = span_decay(length, ends_ref.shape[-2], rate_ref)
    carry = carry_ref[...]
    for block in range(ends_ref.shape[0]):
        starts_ref[block] = carry
        carry = decay * carry + ends_ref[block]


def tree_sum(terms):
    terms = list(terms)
    while len(terms) > 1:
        terms = [terms[i] + terms[i + 1] if i + 1 < len(terms) else terms[i] for i in range(0, len(terms), 2)]
    return terms[0]


def one_minus_exp(y):
    series = jnp.ones_like(y)
    for k in range(11, 1, -1):
        series = 1.0 - (y * (1.0 / k)) * series
    return jnp.where(y < 0.5, y * series, 1.0 - jnp.exp(-y))


def output_kernel(chunks, order, interleaved, params_ref, series_ref, carry_ref, gain_ref, q_ref, out_ref, conv_ref):
    length = series_ref.shape[0] // chunks
    for half in range(chunks // SUBLANES):
        rate = mode_rows(params_ref, 0, order, 2 * order, half, interleaved)
        residue = mode_rows(params_ref, order, order, 2 * order, half, interleaved)
        decay = [jnp.exp(-rate[r]) for r in range(order)]
        weight = [residue[r] * jnp.sqrt(one_minus_exp(2.0 * rate[r])) for r in range(order)]
        carry = mode_rows(carry_ref, 0, order, order, half, interleaved)
        gain = gain_ref[pl.ds(half * SUBLANES, SUBLANES), :]

        def steps(i, state):
            state = list(state)
            for u in range(UNROLL):
                row = pl.multiple_of((i * UNROLL + u) * chunks + half * SUBLANES, SUBLANES)
                x = series_ref[pl.ds(row, SUBLANES), :]
                for r in range(order):
                    state[r] = decay[r] * state[r] + x
                terms = [weight[r] * state[r] for r in range(order)]
                conv_ref[pl.ds(row, SUBLANES), :] = tree_sum(terms + [gain * x])
            return tuple(state)

        lax.fori_loop(0, length // UNROLL, steps, tuple(carry))
        for chunk in range(half * SUBLANES, (half + 1) * SUBLANES):
            rows = pl.ds(chunk * LANES, LANES)
            conv = conv_ref[pl.ds(chunk, length, stride=chunks), :].T
            out_ref[rows, :] = (q_ref[rows, :].astype(jnp.float32) * conv).astype(jnp.bfloat16)


def call(kernel, out_shape, *args, scratch=(), flops=0):
    in_bytes = sum(a.size * a.dtype.itemsize for a in args)
    vmem = pl.BlockSpec(memory_space=pltpu.VMEM)
    return pl.pallas_call(
        kernel,
        out_shape=out_shape,
        in_specs=[vmem] * len(args),
        out_specs=jax.tree.map(lambda _: vmem, out_shape),
        scratch_shapes=list(scratch),
        compiler_params=pltpu.CompilerParams(vmem_limit_bytes=VMEM_LIMIT),
        cost_estimate=pl.CostEstimate(flops=flops, bytes_accessed=in_bytes, transcendentals=0),
    )(*args)


def to_chunks(pieces):
    owners, rows, own = pieces.shape
    if own == LANES:
        return pieces
    if own < LANES:
        group = LANES // own
        return pieces.reshape(owners // group, group, rows, own).swapaxes(1, 2).reshape(-1, rows, LANES)
    return pieces.reshape(owners, rows, own // LANES, LANES).swapaxes(1, 2).reshape(-1, rows, LANES)


def from_chunks(pieces, owners):
    chunks, rows, _ = pieces.shape
    own = chunks * LANES // owners
    if own == LANES:
        return pieces
    if own < LANES:
        group = LANES // own
        return pieces.reshape(chunks, rows, group, own).swapaxes(1, 2).reshape(owners, rows, own)
    return pieces.reshape(owners, own // LANES, rows, LANES).swapaxes(1, 2).reshape(owners, rows, own)


def all_to_all(pieces, groups=None):
    return lax.all_to_all(pieces, "seq", split_axis=0, concat_axis=0, axis_index_groups=groups, tiled=True)


def shards(blocks, q_proj, k_proj, value_projection, residues, rates, direct_gain):
    channels, length = q_proj.shape
    order = residues.shape[1]
    chunks = channels // LANES
    f32 = jnp.float32

    own_rates = rates.T
    packed = jnp.concatenate([own_rates, residues.T], axis=0)
    members = blocks // 2
    halves = blocks == chunks and members == SUBLANES
    if halves:
        groups = [list(range(members)), list(range(members, blocks))]
        other = lax.ppermute(packed, "seq", [(i, (i + members) % blocks) for i in range(blocks)])
        copies = call(
            functools.partial(copies_kernel, members),
            jax.ShapeDtypeStruct((members, 2) + packed.shape, f32),
            packed,
            other,
        )
        params = all_to_all(copies, groups)
    else:
        copies = jnp.broadcast_to(packed[None], (blocks,) + packed.shape)
        params = to_chunks(all_to_all(copies))
    params = params.reshape(chunks * 2 * order, LANES)

    series, ends = call(
        functools.partial(state_kernel, chunks, order, halves),
        (
            jax.ShapeDtypeStruct((length * chunks, LANES), f32),
            jax.ShapeDtypeStruct((chunks * order, LANES), f32),
        ),
        params,
        k_proj,
        value_projection,
        flops=2 * order * channels * length,
    )
    if halves:
        ends = all_to_all(ends.reshape(members, 2, order, LANES), groups)
        total = call(
            functools.partial(total_kernel, length),
            jax.ShapeDtypeStruct(ends.shape[1:], f32),
            copies,
            ends,
        )
        before = lax.ppermute(total, "seq", [(i, i + members) for i in range(members)])
        rates_here = copies
    else:
        ends = all_to_all(from_chunks(ends.reshape(chunks, order, LANES), blocks))
        before = jnp.zeros(ends.shape[1:], f32)
        rates_here = own_rates
    starts = call(
        functools.partial(prefix_kernel, length),
        jax.ShapeDtypeStruct(ends.shape, f32),
        rates_here,
        ends,
        before,
    )
    if halves:
        carry = all_to_all(starts, groups)
    else:
        carry = to_chunks(all_to_all(starts))
    carry = carry.reshape(chunks * order, LANES)
    return call(
        functools.partial(output_kernel, chunks, order, halves),
        jax.ShapeDtypeStruct((channels, length), jnp.bfloat16),
        params,
        series,
        carry,
        direct_gain.reshape(chunks, LANES),
        q_proj,
        scratch=[pltpu.VMEM((length * chunks, LANES), f32)],
        flops=4 * order * channels * length,
    )


def solution(mesh):
    return jax.shard_map(
        functools.partial(shards, mesh.shape["seq"]),
        mesh=mesh,
        in_specs=(
            P("chan", ("groups", "seq")),
            P("chan", ("groups", "seq")),
            P("chan", ("groups", "seq")),
            P(("chan", "seq"), None),
            P(("chan", "seq"), None),
            P("chan"),
        ),
        out_specs=P("chan", ("groups", "seq")),
        check_vma=False,
    )
```

```python
import functools
import jax
import jax.numpy as jnp
from jax import lax
from jax.experimental import pallas as pl
from jax.experimental.pallas import tpu as pltpu
from jax.sharding import PartitionSpec as P

LANES = 128
SUBLANES = 8
UNROLL = 8
VMEM_LIMIT = 32 * 1024 * 1024


def prepare_kernel(chunks, k_ref, v_ref, series_ref):
    length = k_ref.shape[1]
    for chunk in range(chunks):
        rows = pl.ds(chunk * LANES, LANES)
        gated = k_ref[rows, :].astype(jnp.float32) * v_ref[rows, :].astype(jnp.float32)
        series_ref[pl.ds(chunk, length, stride=chunks), :] = gated.T


def mode_rows(ref, base, order, per_chunk, chunks, half):
    first = half * SUBLANES * per_chunk + base
    return [ref[pl.ds(first + r, SUBLANES, stride=per_chunk), :] for r in range(order)]


def state_kernel(chunks, order, params_ref, series_ref, state_ref):
    length = series_ref.shape[0] // chunks
    for half in range(chunks // SUBLANES):
        decay = [jnp.exp(-rate) for rate in mode_rows(params_ref, 0, order, 2 * order, chunks, half)]

        def steps(i, state):
            state = list(state)
            for u in range(UNROLL):
                row = pl.multiple_of((i * UNROLL + u) * chunks + half * SUBLANES, SUBLANES)
                x = series_ref[pl.ds(row, SUBLANES), :]
                for r in range(order):
                    state[r] = decay[r] * state[r] + x
            return tuple(state)

        zero = jnp.zeros((SUBLANES, LANES), jnp.float32)
        state = lax.fori_loop(0, length // UNROLL, steps, (zero,) * order)
        for r in range(order):
            state_ref[pl.ds(half * SUBLANES * order + r, SUBLANES, stride=order), :] = state[r]


def prefix_kernel(length, rate_ref, ends_ref, starts_ref):
    span_decay = jnp.exp(-float(length) * rate_ref[...])
    carry = jnp.zeros(rate_ref.shape, jnp.float32)
    for block in range(ends_ref.shape[0]):
        starts_ref[block] = carry
        carry = span_decay * carry + ends_ref[block]


def tree_sum(terms):
    terms = list(terms)
    while len(terms) > 1:
        terms = [terms[i] + terms[i + 1] if i + 1 < len(terms) else terms[i] for i in range(0, len(terms), 2)]
    return terms[0]


def one_minus_exp(y):
    series = jnp.ones_like(y)
    for k in range(11, 1, -1):
        series = 1.0 - (y * (1.0 / k)) * series
    return jnp.where(y < 0.5, y * series, 1.0 - jnp.exp(-y))


def local_kernel(chunks, order, gathered_ref, series_ref, gain_ref, conv_ref, weight_ref):
    length = series_ref.shape[0] // chunks
    for half in range(chunks // SUBLANES):
        rate = mode_rows(gathered_ref, 0, order, 2 * order, chunks, half)
        residue = mode_rows(gathered_ref, order, order, 2 * order, chunks, half)
        decay = [jnp.exp(-rate[r]) for r in range(order)]
        weight = [residue[r] * jnp.sqrt(one_minus_exp(2.0 * rate[r])) for r in range(order)]
        for r in range(order):
            weight_ref[pl.ds(half * SUBLANES * order + r, SUBLANES, stride=order), :] = weight[r]
        gain = gain_ref[pl.ds(half * SUBLANES, SUBLANES), :]

        def steps(i, state):
            state = list(state)
            for u in range(UNROLL):
                row = pl.multiple_of((i * UNROLL + u) * chunks + half * SUBLANES, SUBLANES)
                x = series_ref[pl.ds(row, SUBLANES), :]
                for r in range(order):
                    state[r] = decay[r] * state[r] + x
                terms = [weight[r] * state[r] for r in range(order)]
                conv_ref[pl.ds(row, SUBLANES), :] = tree_sum(terms + [gain * x])
            return tuple(state)

        zero = jnp.zeros((SUBLANES, LANES), jnp.float32)
        lax.fori_loop(0, length // UNROLL, steps, (zero,) * order)


def output_kernel(
    chunks, order, gathered_ref, weight_ref, carry_ref, local_ref, q_ref, out_ref, conv_ref, gated_ref, sems
):
    length = local_ref.shape[0] // chunks
    tokens = length // SUBLANES

    def leave(chunk):
        rows = pl.ds(pl.multiple_of(chunk * LANES, LANES), LANES)
        return pltpu.make_async_copy(gated_ref.at[rows, :], out_ref.at[rows, :], sems.at[chunk])

    def finish(chunk):
        rows = pl.ds(pl.multiple_of(chunk * LANES, LANES), LANES)
        conv = conv_ref[pl.ds(chunk, length, stride=chunks), :].T
        gated_ref[rows, :] = (q_ref[rows, :].astype(jnp.float32) * conv).astype(jnp.bfloat16)
        leave(chunk).start()

    for half in range(chunks // SUBLANES):
        decay = [jnp.exp(-rate) for rate in mode_rows(gathered_ref, 0, order, 2 * order, chunks, half)]
        weight = mode_rows(weight_ref, 0, order, order, chunks, half)
        carry = mode_rows(carry_ref, 0, order, order, chunks, half)

        def steps(i, fading):
            fading = list(fading)
            for u in range(tokens):
                row = pl.multiple_of((i * tokens + u) * chunks + half * SUBLANES, SUBLANES)
                fading = [decay[r] * fading[r] for r in range(order)]
                conv_ref[pl.ds(row, SUBLANES), :] = tree_sum(fading + [local_ref[pl.ds(row, SUBLANES), :]])
            if half > 0:
                finish((half - 1) * SUBLANES + i)
            return tuple(fading)

        lax.fori_loop(0, SUBLANES, steps, tuple(weight[r] * carry[r] for r in range(order)))
    for chunk in range(chunks - SUBLANES, chunks):
        finish(chunk)
    for chunk in range(chunks):
        leave(chunk).wait()


def copies_kernel(rate_hbm, residue_hbm, copies_ref, rate_ref, residue_ref, sems):
    pairs = ((rate_hbm, rate_ref), (residue_hbm, residue_ref))
    loads = [pltpu.make_async_copy(source, target, sems.at[i]) for i, (source, target) in enumerate(pairs)]
    for load in loads:
        load.start()
    for load in loads:
        load.wait()
    order = rate_ref.shape[0]
    for copy in range(copies_ref.shape[0]):
        copies_ref[copy, :order] = rate_ref[...]
        copies_ref[copy, order:] = residue_ref[...]


def call(kernel, out_shape, *args, in_space=pltpu.VMEM, out_space=pltpu.VMEM, scratch=(), flops=0):
    in_bytes = sum(a.size * a.dtype.itemsize for a in args)
    in_spec = pl.BlockSpec(memory_space=in_space)
    out_spec = pl.BlockSpec(memory_space=out_space)
    return pl.pallas_call(
        kernel,
        out_shape=out_shape,
        in_specs=[in_spec] * len(args),
        out_specs=jax.tree.map(lambda _: out_spec, out_shape),
        scratch_shapes=list(scratch),
        compiler_params=pltpu.CompilerParams(vmem_limit_bytes=VMEM_LIMIT),
        cost_estimate=pl.CostEstimate(flops=flops, bytes_accessed=in_bytes, transcendentals=0),
    )(*args)


def to_chunks(pieces):
    owners, rows, own = pieces.shape
    if own == LANES:
        return pieces
    if own < LANES:
        group = LANES // own
        return pieces.reshape(owners // group, group, rows, own).swapaxes(1, 2).reshape(-1, rows, LANES)
    return pieces.reshape(owners, rows, own // LANES, LANES).swapaxes(1, 2).reshape(-1, rows, LANES)


def from_chunks(pieces, owners):
    chunks, rows, _ = pieces.shape
    own = chunks * LANES // owners
    if own == LANES:
        return pieces
    if own < LANES:
        group = LANES // own
        return pieces.reshape(chunks, rows, group, own).swapaxes(1, 2).reshape(owners, rows, own)
    return pieces.reshape(owners, own // LANES, rows, LANES).swapaxes(1, 2).reshape(owners, rows, own)


def shards(blocks, q_proj, k_proj, value_projection, residues, rates, direct_gain):
    channels, length = q_proj.shape
    order = residues.shape[1]
    chunks = channels // LANES
    f32 = jnp.float32

    own_rates = rates.T
    copies = call(
        copies_kernel,
        pltpu.VMEM((blocks, 2 * order, rates.shape[0]), f32),
        own_rates,
        residues.T,
        in_space=pltpu.HBM,
        scratch=[pltpu.VMEM(own_rates.shape, f32)] * 2 + [pltpu.SemaphoreType.DMA((2,))],
    )
    gathered = lax.all_to_all(copies, "seq", split_axis=0, concat_axis=0, tiled=True)
    params = to_chunks(gathered).reshape(chunks * 2 * order, LANES)

    series = call(
        functools.partial(prepare_kernel, chunks),
        jax.ShapeDtypeStruct((length * chunks, LANES), f32),
        k_proj,
        value_projection,
        flops=channels * length,
    )
    ends = call(
        functools.partial(state_kernel, chunks, order),
        jax.ShapeDtypeStruct((chunks * order, LANES), f32),
        params,
        series,
        flops=2 * order * channels * length,
    )
    local_series, ends = lax.optimization_barrier((series, ends))
    ends = from_chunks(ends.reshape(chunks, order, LANES), blocks)
    local, weights = call(
        functools.partial(local_kernel, chunks, order),
        (
            jax.ShapeDtypeStruct((length * chunks, LANES), f32),
            jax.ShapeDtypeStruct((chunks * order, LANES), f32),
        ),
        params,
        local_series,
        direct_gain.reshape(chunks, LANES),
        flops=4 * order * channels * length,
    )
    ends = lax.all_to_all(ends, "seq", split_axis=0, concat_axis=0, tiled=True)
    starts = call(
        functools.partial(prefix_kernel, length),
        pltpu.VMEM(ends.shape, f32),
        own_rates,
        ends,
    )
    starts = lax.all_to_all(starts, "seq", split_axis=0, concat_axis=0, tiled=True)
    carry = to_chunks(starts).reshape(chunks * order, LANES)
    return call(
        functools.partial(output_kernel, chunks, order),
        jax.ShapeDtypeStruct((channels, length), jnp.bfloat16),
        params,
        weights,
        carry,
        local,
        q_proj,
        out_space=pl.ANY,
        scratch=[
            pltpu.VMEM((length * chunks, LANES), f32),
            pltpu.VMEM((channels, length), jnp.bfloat16),
            pltpu.SemaphoreType.DMA((chunks,)),
        ],
        flops=2 * order * channels * length,
    )


def solution(mesh):
    return jax.shard_map(
        functools.partial(shards, mesh.shape["seq"]),
        mesh=mesh,
        in_specs=(
            P("chan", ("groups", "seq")),
            P("chan", ("groups", "seq")),
            P("chan", ("groups", "seq")),
            P(("chan", "seq"), None),
            P(("chan", "seq"), None),
            P("chan"),
        ),
        out_specs=P("chan", ("groups", "seq")),
        check_vma=False,
    )
```

```python
import functools
import jax
import jax.numpy as jnp
from jax import lax
from jax.experimental import pallas as pl
from jax.experimental.pallas import tpu as pltpu
from jax.sharding import PartitionSpec as P

LANES = 128
SUBLANES = 8
UNROLL = 8
VMEM_LIMIT = 32 * 1024 * 1024


def prepare_kernel(chunks, k_ref, v_ref, series_ref):
    length = k_ref.shape[1]
    for chunk in range(chunks):
        rows = pl.ds(chunk * LANES, LANES)
        gated = k_ref[rows, :].astype(jnp.float32) * v_ref[rows, :].astype(jnp.float32)
        series_ref[pl.ds(chunk, length, stride=chunks), :] = gated.T


def mode_rows(ref, base, order, per_chunk, chunks, half):
    first = half * SUBLANES * per_chunk + base
    return [ref[pl.ds(first + r, SUBLANES, stride=per_chunk), :] for r in range(order)]


def state_kernel(chunks, order, params_ref, series_ref, state_ref):
    length = series_ref.shape[0] // chunks
    for half in range(chunks // SUBLANES):
        decay = [jnp.exp(-rate) for rate in mode_rows(params_ref, 0, order, 2 * order, chunks, half)]

        def steps(i, state):
            state = list(state)
            for u in range(UNROLL):
                row = pl.multiple_of((i * UNROLL + u) * chunks + half * SUBLANES, SUBLANES)
                x = series_ref[pl.ds(row, SUBLANES), :]
                for r in range(order):
                    state[r] = decay[r] * state[r] + x
            return tuple(state)

        zero = jnp.zeros((SUBLANES, LANES), jnp.float32)
        state = lax.fori_loop(0, length // UNROLL, steps, (zero,) * order)
        for r in range(order):
            state_ref[pl.ds(half * SUBLANES * order + r, SUBLANES, stride=order), :] = state[r]


def prefix_kernel(length, rate_ref, ends_ref, starts_ref):
    span_decay = jnp.exp(-float(length) * rate_ref[...])
    carry = jnp.zeros(rate_ref.shape, jnp.float32)
    for block in range(ends_ref.shape[0]):
        starts_ref[block] = carry
        carry = span_decay * carry + ends_ref[block]


def tree_sum(terms):
    terms = list(terms)
    while len(terms) > 1:
        terms = [terms[i] + terms[i + 1] if i + 1 < len(terms) else terms[i] for i in range(0, len(terms), 2)]
    return terms[0]


def one_minus_exp(y):
    series = jnp.ones_like(y)
    for k in range(11, 1, -1):
        series = 1.0 - (y * (1.0 / k)) * series
    return jnp.where(y < 0.5, y * series, 1.0 - jnp.exp(-y))


def leaving(chunk, gated_ref, out_ref, sems):
    rows = pl.ds(chunk * LANES, LANES)
    return pltpu.make_async_copy(gated_ref.at[rows, :], out_ref.at[rows, :], sems.at[chunk])


def finish(chunk, chunks, conv_ref, q_ref, gated_ref, out_ref, sems):
    length = conv_ref.shape[0] // chunks
    rows = pl.ds(chunk * LANES, LANES)
    conv = conv_ref[pl.ds(chunk, length, stride=chunks), :].T
    gated_ref[rows, :] = (q_ref[rows, :].astype(jnp.float32) * conv).astype(jnp.bfloat16)
    leaving(chunk, gated_ref, out_ref, sems).start()


def local_kernel(
    chunks, order, gathered_ref, series_ref, gain_ref, q_ref, conv_ref, weight_ref, out_ref, gated_ref, sems
):
    length = series_ref.shape[0] // chunks
    for half in range(chunks // SUBLANES):
        rate = mode_rows(gathered_ref, 0, order, 2 * order, chunks, half)
        residue = mode_rows(gathered_ref, order, order, 2 * order, chunks, half)
        decay = [jnp.exp(-rate[r]) for r in range(order)]
        weight = [residue[r] * jnp.sqrt(one_minus_exp(2.0 * rate[r])) for r in range(order)]
        for r in range(order):
            weight_ref[pl.ds(half * SUBLANES * order + r, SUBLANES, stride=order), :] = weight[r]
        gain = gain_ref[pl.ds(half * SUBLANES, SUBLANES), :]

        def steps(i, state):
            state = list(state)
            for u in range(UNROLL):
                row = pl.multiple_of((i * UNROLL + u) * chunks + half * SUBLANES, SUBLANES)
                x = series_ref[pl.ds(row, SUBLANES), :]
                for r in range(order):
                    state[r] = decay[r] * state[r] + x
                terms = [weight[r] * state[r] for r in range(order)]
                conv_ref[pl.ds(row, SUBLANES), :] = tree_sum(terms + [gain * x])
            return tuple(state)

        zero = jnp.zeros((SUBLANES, LANES), jnp.float32)
        lax.fori_loop(0, length // UNROLL, steps, (zero,) * order)

    @pl.when(lax.axis_index("seq") == 0)
    def _():
        for chunk in range(chunks):
            finish(chunk, chunks, conv_ref, q_ref, gated_ref, out_ref, sems)
        for chunk in range(chunks):
            leaving(chunk, gated_ref, out_ref, sems).wait()


def output_kernel(
    chunks, order, gathered_ref, weight_ref, carry_ref, local_ref, q_ref, _, out_ref, conv_ref, gated_ref, sems
):
    length = local_ref.shape[0] // chunks
    tokens = length // SUBLANES

    @pl.when(lax.axis_index("seq") > 0)
    def _():
        for half in range(chunks // SUBLANES):
            decay = [jnp.exp(-rate) for rate in mode_rows(gathered_ref, 0, order, 2 * order, chunks, half)]
            weight = mode_rows(weight_ref, 0, order, order, chunks, half)
            carry = mode_rows(carry_ref, 0, order, order, chunks, half)

            def steps(i, fading):
                fading = list(fading)
                for u in range(tokens):
                    row = (i * tokens + u) * chunks + half * SUBLANES
                    if not isinstance(row, int):
                        row = pl.multiple_of(row, SUBLANES)
                    fading = [decay[r] * fading[r] for r in range(order)]
                    conv_ref[pl.ds(row, SUBLANES), :] = tree_sum(fading + [local_ref[pl.ds(row, SUBLANES), :]])
                return tuple(fading)

            fading = tuple(weight[r] * carry[r] for r in range(order))
            if half == 0:
                lax.fori_loop(0, SUBLANES, steps, fading)
            else:
                for i in range(SUBLANES):
                    fading = steps(i, fading)
                    finish((half - 1) * SUBLANES + i, chunks, conv_ref, q_ref, gated_ref, out_ref, sems)
        for chunk in range(chunks - SUBLANES, chunks):
            finish(chunk, chunks, conv_ref, q_ref, gated_ref, out_ref, sems)
        for chunk in range(chunks):
            leaving(chunk, gated_ref, out_ref, sems).wait()


def call(kernel, out_shape, *args, out_spaces=None, aliases=None, scratch=(), flops=0):
    in_bytes = sum(a.size * a.dtype.itemsize for a in args)
    vmem = pl.BlockSpec(memory_space=pltpu.VMEM)
    in_specs = [vmem] * len(args)
    for i in aliases or {}:
        in_specs[i] = pl.BlockSpec(memory_space=pl.ANY)
    out_spaces = out_spaces or jax.tree.map(lambda _: pltpu.VMEM, out_shape)
    return pl.pallas_call(
        kernel,
        out_shape=out_shape,
        in_specs=in_specs,
        out_specs=jax.tree.map(lambda space: pl.BlockSpec(memory_space=space), out_spaces),
        scratch_shapes=list(scratch),
        input_output_aliases=aliases or {},
        compiler_params=pltpu.CompilerParams(vmem_limit_bytes=VMEM_LIMIT),
        cost_estimate=pl.CostEstimate(flops=flops, bytes_accessed=in_bytes, transcendentals=0),
    )(*args)


def to_chunks(pieces):
    owners, rows, own = pieces.shape
    if own == LANES:
        return pieces
    if own < LANES:
        group = LANES // own
        return pieces.reshape(owners // group, group, rows, own).swapaxes(1, 2).reshape(-1, rows, LANES)
    return pieces.reshape(owners, rows, own // LANES, LANES).swapaxes(1, 2).reshape(-1, rows, LANES)


def from_chunks(pieces, owners):
    chunks, rows, _ = pieces.shape
    own = chunks * LANES // owners
    if own == LANES:
        return pieces
    if own < LANES:
        group = LANES // own
        return pieces.reshape(chunks, rows, group, own).swapaxes(1, 2).reshape(owners, rows, own)
    return pieces.reshape(owners, own // LANES, rows, LANES).swapaxes(1, 2).reshape(owners, rows, own)


def shards(blocks, q_proj, k_proj, value_projection, residues, rates, direct_gain):
    channels, length = q_proj.shape
    order = residues.shape[1]
    chunks = channels // LANES
    f32 = jnp.float32

    own_rates = rates.T
    copies_of = (blocks, 2, order, rates.shape[0])
    first = lax.broadcasted_iota(jnp.int32, copies_of, 1) == 0
    copies = jnp.where(first, own_rates, residues.T).reshape(blocks, 2 * order, -1)
    gathered = lax.all_to_all(copies, "seq", split_axis=0, concat_axis=0, tiled=True)
    params = to_chunks(gathered).reshape(chunks * 2 * order, LANES)

    series = call(
        functools.partial(prepare_kernel, chunks),
        jax.ShapeDtypeStruct((length * chunks, LANES), f32),
        k_proj,
        value_projection,
        flops=channels * length,
    )
    ends = call(
        functools.partial(state_kernel, chunks, order),
        jax.ShapeDtypeStruct((chunks * order, LANES), f32),
        params,
        series,
        flops=2 * order * channels * length,
    )
    local_series, ends = lax.optimization_barrier((series, ends))
    ends = from_chunks(ends.reshape(chunks, order, LANES), blocks)
    out_shape = jax.ShapeDtypeStruct((channels, length), jnp.bfloat16)
    out_scratch = [pltpu.VMEM(out_shape.shape, out_shape.dtype), pltpu.SemaphoreType.DMA((chunks,))]
    local, weights, out = call(
        functools.partial(local_kernel, chunks, order),
        (
            jax.ShapeDtypeStruct((length * chunks, LANES), f32),
            jax.ShapeDtypeStruct((chunks * order, LANES), f32),
            out_shape,
        ),
        params,
        local_series,
        direct_gain.reshape(chunks, LANES),
        q_proj,
        out_spaces=(pltpu.VMEM, pltpu.VMEM, pl.ANY),
        scratch=out_scratch,
        flops=4 * order * channels * length,
    )
    ends = lax.all_to_all(ends, "seq", split_axis=0, concat_axis=0, tiled=True)
    starts = call(
        functools.partial(prefix_kernel, length),
        jax.ShapeDtypeStruct(ends.shape, f32),
        own_rates,
        ends,
    )
    starts = lax.all_to_all(starts, "seq", split_axis=0, concat_axis=0, tiled=True)
    carry = to_chunks(starts).reshape(chunks * order, LANES)
    return call(
        functools.partial(output_kernel, chunks, order),
        out_shape,
        params,
        weights,
        carry,
        local,
        q_proj,
        out,
        out_spaces=pl.ANY,
        aliases={5: 0},
        scratch=[pltpu.VMEM((length * chunks, LANES), f32)] + out_scratch,
        flops=2 * order * channels * length,
    )


def solution(mesh):
    return jax.shard_map(
        functools.partial(shards, mesh.shape["seq"]),
        mesh=mesh,
        in_specs=(
            P("chan", ("groups", "seq")),
            P("chan", ("groups", "seq")),
            P("chan", ("groups", "seq")),
            P(("chan", "seq"), None),
            P(("chan", "seq"), None),
            P("chan"),
        ),
        out_specs=P("chan", ("groups", "seq")),
        check_vma=False,
    )
```

```python
import functools
import jax
import jax.numpy as jnp
from jax import lax
from jax.experimental import pallas as pl
from jax.experimental.pallas import tpu as pltpu
from jax.sharding import PartitionSpec as P

LANES = 128
SUBLANES = 8
UNROLL = 8
VMEM_LIMIT = 32 * 1024 * 1024


def prepare_kernel(chunks, k_ref, v_ref, series_ref):
    length = k_ref.shape[1]
    for chunk in range(chunks):
        rows = pl.ds(chunk * LANES, LANES)
        gated = k_ref[rows, :].astype(jnp.float32) * v_ref[rows, :].astype(jnp.float32)
        series_ref[pl.ds(chunk, length, stride=chunks), :] = gated.T


def mode_rows(ref, base, order, per_chunk, chunks, half):
    first = half * SUBLANES * per_chunk + base
    return [ref[pl.ds(first + r, SUBLANES, stride=per_chunk), :] for r in range(order)]


def state_kernel(chunks, order, params_ref, series_ref, state_ref):
    length = series_ref.shape[0] // chunks
    for half in range(chunks // SUBLANES):
        decay = [jnp.exp(-rate) for rate in mode_rows(params_ref, 0, order, 2 * order, chunks, half)]

        def steps(i, state):
            state = list(state)
            for u in range(UNROLL):
                row = pl.multiple_of((i * UNROLL + u) * chunks + half * SUBLANES, SUBLANES)
                x = series_ref[pl.ds(row, SUBLANES), :]
                for r in range(order):
                    state[r] = decay[r] * state[r] + x
            return tuple(state)

        zero = jnp.zeros((SUBLANES, LANES), jnp.float32)
        state = lax.fori_loop(0, length // UNROLL, steps, (zero,) * order)
        for r in range(order):
            state_ref[pl.ds(half * SUBLANES * order + r, SUBLANES, stride=order), :] = state[r]


def prefix_kernel(length, rate_ref, ends_ref, starts_ref):
    span_decay = jnp.exp(-float(length) * rate_ref[...])
    carry = jnp.zeros(rate_ref.shape, jnp.float32)
    for block in range(ends_ref.shape[0]):
        starts_ref[block] = carry
        carry = span_decay * carry + ends_ref[block]


def tree_sum(terms):
    terms = list(terms)
    while len(terms) > 1:
        terms = [terms[i] + terms[i + 1] if i + 1 < len(terms) else terms[i] for i in range(0, len(terms), 2)]
    return terms[0]


def one_minus_exp(y):
    series = jnp.ones_like(y)
    for k in range(11, 1, -1):
        series = 1.0 - (y * (1.0 / k)) * series
    return jnp.where(y < 0.5, y * series, 1.0 - jnp.exp(-y))


def leaving(chunk, gated_ref, out_ref, sems):
    rows = pl.ds(chunk * LANES, LANES)
    return pltpu.make_async_copy(gated_ref.at[rows, :], out_ref.at[rows, :], sems.at[chunk])


def finish(chunk, chunks, conv_ref, q_ref, gated_ref, out_ref, sems):
    length = conv_ref.shape[0] // chunks
    rows = pl.ds(chunk * LANES, LANES)
    conv = conv_ref[pl.ds(chunk, length, stride=chunks), :].T
    gated_ref[rows, :] = (q_ref[rows, :].astype(jnp.float32) * conv).astype(jnp.bfloat16)
    leaving(chunk, gated_ref, out_ref, sems).start()


def local_kernel(
    chunks, order, gathered_ref, series_ref, gain_ref, q_ref, conv_ref, weight_ref, out_ref, gated_ref, sems
):
    length = series_ref.shape[0] // chunks
    for half in range(chunks // SUBLANES):
        rate = mode_rows(gathered_ref, 0, order, 2 * order, chunks, half)
        residue = mode_rows(gathered_ref, order, order, 2 * order, chunks, half)
        decay = [jnp.exp(-rate[r]) for r in range(order)]
        weight = [residue[r] * jnp.sqrt(one_minus_exp(2.0 * rate[r])) for r in range(order)]
        for r in range(order):
            weight_ref[pl.ds(half * SUBLANES * order + r, SUBLANES, stride=order), :] = weight[r]
        gain = gain_ref[pl.ds(half * SUBLANES, SUBLANES), :]

        def steps(i, state):
            state = list(state)
            for u in range(UNROLL):
                row = pl.multiple_of((i * UNROLL + u) * chunks + half * SUBLANES, SUBLANES)
                x = series_ref[pl.ds(row, SUBLANES), :]
                for r in range(order):
                    state[r] = decay[r] * state[r] + x
                terms = [weight[r] * state[r] for r in range(order)]
                conv_ref[pl.ds(row, SUBLANES), :] = tree_sum(terms + [gain * x])
            return tuple(state)

        zero = jnp.zeros((SUBLANES, LANES), jnp.float32)
        lax.fori_loop(0, length // UNROLL, steps, (zero,) * order)

    @pl.when(lax.axis_index("seq") == 0)
    def _():
        for chunk in range(chunks):
            finish(chunk, chunks, conv_ref, q_ref, gated_ref, out_ref, sems)
        for chunk in range(chunks):
            leaving(chunk, gated_ref, out_ref, sems).wait()


def output_kernel(
    chunks, order, gathered_ref, weight_ref, carry_ref, local_ref, q_ref, _, out_ref, conv_ref, gated_ref, sems
):
    length = local_ref.shape[0] // chunks
    tokens = length // SUBLANES

    @pl.when(lax.axis_index("seq") > 0)
    def _():
        for half in range(chunks // SUBLANES):
            decay = [jnp.exp(-rate) for rate in mode_rows(gathered_ref, 0, order, 2 * order, chunks, half)]
            weight = mode_rows(weight_ref, 0, order, order, chunks, half)
            carry = mode_rows(carry_ref, 0, order, order, chunks, half)

            def steps(i, fading):
                fading = list(fading)
                for u in range(tokens):
                    row = (i * tokens + u) * chunks + half * SUBLANES
                    if not isinstance(row, int):
                        row = pl.multiple_of(row, SUBLANES)
                    fading = [decay[r] * fading[r] for r in range(order)]
                    conv_ref[pl.ds(row, SUBLANES), :] = tree_sum(fading + [local_ref[pl.ds(row, SUBLANES), :]])
                return tuple(fading)

            fading = tuple(weight[r] * carry[r] for r in range(order))
            if half == 0:
                lax.fori_loop(0, SUBLANES, steps, fading)
            else:
                for i in range(SUBLANES):
                    fading = steps(i, fading)
                    finish((half - 1) * SUBLANES + i, chunks, conv_ref, q_ref, gated_ref, out_ref, sems)
        for chunk in range(chunks - SUBLANES, chunks):
            finish(chunk, chunks, conv_ref, q_ref, gated_ref, out_ref, sems)
        for chunk in range(chunks):
            leaving(chunk, gated_ref, out_ref, sems).wait()


def copies_kernel(rate_ref, residue_ref, copies_ref, sems):
    order = rate_ref.shape[0]
    copies = []
    for piece in range(copies_ref.shape[0]):
        for part, source in enumerate((rate_ref, residue_ref)):
            target = copies_ref.at[piece, pl.ds(part * order, order)]
            copies.append(pltpu.make_async_copy(source, target, sems.at[piece, part]))
    for copy in copies:
        copy.start()
    for copy in copies:
        copy.wait()


def call(kernel, out_shape, *args, in_spaces=None, out_spaces=None, aliases=None, scratch=(), flops=0):
    in_bytes = sum(a.size * a.dtype.itemsize for a in args)
    in_spaces = in_spaces or [pl.ANY if i in (aliases or {}) else pltpu.VMEM for i in range(len(args))]
    out_spaces = out_spaces or jax.tree.map(lambda _: pltpu.VMEM, out_shape)
    return pl.pallas_call(
        kernel,
        out_shape=out_shape,
        in_specs=[pl.BlockSpec(memory_space=space) for space in in_spaces],
        out_specs=jax.tree.map(lambda space: pl.BlockSpec(memory_space=space), out_spaces),
        scratch_shapes=list(scratch),
        input_output_aliases=aliases or {},
        compiler_params=pltpu.CompilerParams(vmem_limit_bytes=VMEM_LIMIT),
        cost_estimate=pl.CostEstimate(flops=flops, bytes_accessed=in_bytes, transcendentals=0),
    )(*args)


def to_chunks(pieces):
    owners, rows, own = pieces.shape
    if own == LANES:
        return pieces
    if own < LANES:
        group = LANES // own
        return pieces.reshape(owners // group, group, rows, own).swapaxes(1, 2).reshape(-1, rows, LANES)
    return pieces.reshape(owners, rows, own // LANES, LANES).swapaxes(1, 2).reshape(-1, rows, LANES)


def from_chunks(pieces, owners):
    chunks, rows, _ = pieces.shape
    own = chunks * LANES // owners
    if own == LANES:
        return pieces
    if own < LANES:
        group = LANES // own
        return pieces.reshape(chunks, rows, group, own).swapaxes(1, 2).reshape(owners, rows, own)
    return pieces.reshape(owners, own // LANES, rows, LANES).swapaxes(1, 2).reshape(owners, rows, own)


def shards(blocks, q_proj, k_proj, value_projection, residues, rates, direct_gain):
    channels, length = q_proj.shape
    order = residues.shape[1]
    chunks = channels // LANES
    f32 = jnp.float32

    own_rates = rates.T
    in_hbm = [pltpu.with_memory_space_constraint(array, pltpu.HBM) for array in (own_rates, residues.T)]
    copies = call(
        copies_kernel,
        jax.ShapeDtypeStruct((blocks, 2 * order, rates.shape[0]), f32),
        *in_hbm,
        in_spaces=[pl.ANY] * 2,
        out_spaces=pl.ANY,
        scratch=[pltpu.SemaphoreType.DMA((blocks, 2))],
    )
    gathered = lax.all_to_all(copies, "seq", split_axis=0, concat_axis=0, tiled=True)
    params = to_chunks(gathered).reshape(chunks * 2 * order, LANES)

    series = call(
        functools.partial(prepare_kernel, chunks),
        jax.ShapeDtypeStruct((length * chunks, LANES), f32),
        k_proj,
        value_projection,
        flops=channels * length,
    )
    ends = call(
        functools.partial(state_kernel, chunks, order),
        jax.ShapeDtypeStruct((chunks * order, LANES), f32),
        params,
        series,
        flops=2 * order * channels * length,
    )
    local_series, ends = lax.optimization_barrier((series, ends))
    ends = from_chunks(ends.reshape(chunks, order, LANES), blocks)
    out_shape = jax.ShapeDtypeStruct((channels, length), jnp.bfloat16)
    out_scratch = [pltpu.VMEM(out_shape.shape, out_shape.dtype), pltpu.SemaphoreType.DMA((chunks,))]
    local, weights, out = call(
        functools.partial(local_kernel, chunks, order),
        (
            jax.ShapeDtypeStruct((length * chunks, LANES), f32),
            jax.ShapeDtypeStruct((chunks * order, LANES), f32),
            out_shape,
        ),
        params,
        local_series,
        direct_gain.reshape(chunks, LANES),
        q_proj,
        out_spaces=(pltpu.VMEM, pltpu.VMEM, pl.ANY),
        scratch=out_scratch,
        flops=4 * order * channels * length,
    )
    ends = lax.all_to_all(ends, "seq", split_axis=0, concat_axis=0, tiled=True)
    starts = call(
        functools.partial(prefix_kernel, length),
        jax.ShapeDtypeStruct(ends.shape, f32),
        own_rates,
        ends,
    )
    starts = lax.all_to_all(starts, "seq", split_axis=0, concat_axis=0, tiled=True)
    carry = to_chunks(starts).reshape(chunks * order, LANES)
    return call(
        functools.partial(output_kernel, chunks, order),
        out_shape,
        params,
        weights,
        carry,
        local,
        q_proj,
        out,
        out_spaces=pl.ANY,
        aliases={5: 0},
        scratch=[pltpu.VMEM((length * chunks, LANES), f32)] + out_scratch,
        flops=2 * order * channels * length,
    )


def solution(mesh):
    return jax.shard_map(
        functools.partial(shards, mesh.shape["seq"]),
        mesh=mesh,
        in_specs=(
            P("chan", ("groups", "seq")),
            P("chan", ("groups", "seq")),
            P("chan", ("groups", "seq")),
            P(("chan", "seq"), None),
            P(("chan", "seq"), None),
            P("chan"),
        ),
        out_specs=P("chan", ("groups", "seq")),
        check_vma=False,
    )
```

```python
import functools
import jax
import jax.numpy as jnp
from jax import lax
from jax.experimental import pallas as pl
from jax.experimental.pallas import tpu as pltpu
from jax.sharding import PartitionSpec as P

LANES = 128
SUBLANES = 8
UNROLL = 8
VMEM_LIMIT = 32 * 1024 * 1024


def prepare_kernel(places, k_ref, v_ref, series_ref):
    chunks, length = len(places), k_ref.shape[1]
    for chunk, place in enumerate(places):
        rows = pl.ds(place * LANES, LANES)
        gated = k_ref[rows, :].astype(jnp.float32) * v_ref[rows, :].astype(jnp.float32)
        series_ref[pl.ds(chunk, length, stride=chunks), :] = gated.T


def mode_rows(ref, base, order, per_chunk, chunks, half):
    first = half * SUBLANES * per_chunk + base
    return [ref[pl.ds(first + r, SUBLANES, stride=per_chunk), :] for r in range(order)]


def state_kernel(chunks, order, params_ref, series_ref, state_ref):
    length = series_ref.shape[0] // chunks
    for half in range(chunks // SUBLANES):
        decay = [jnp.exp(-rate) for rate in mode_rows(params_ref, 0, order, 2 * order, chunks, half)]

        def steps(i, state):
            state = list(state)
            for u in range(UNROLL):
                row = pl.multiple_of((i * UNROLL + u) * chunks + half * SUBLANES, SUBLANES)
                x = series_ref[pl.ds(row, SUBLANES), :]
                for r in range(order):
                    state[r] = decay[r] * state[r] + x
            return tuple(state)

        zero = jnp.zeros((SUBLANES, LANES), jnp.float32)
        state = lax.fori_loop(0, length // UNROLL, steps, (zero,) * order)
        for r in range(order):
            state_ref[pl.ds(half * SUBLANES * order + r, SUBLANES, stride=order), :] = state[r]


def prefix_kernel(length, members, rate_ref, ends_ref, starts_ref):
    span_decay = jnp.exp(-float(length) * rate_ref[...])
    carry = jnp.zeros(rate_ref.shape, jnp.float32)
    for block in range(len(members)):
        starts_ref[members.index(block)] = carry
        carry = span_decay * carry + ends_ref[members.index(block)]


def tree_sum(terms):
    terms = list(terms)
    while len(terms) > 1:
        terms = [terms[i] + terms[i + 1] if i + 1 < len(terms) else terms[i] for i in range(0, len(terms), 2)]
    return terms[0]


def one_minus_exp(y):
    series = jnp.ones_like(y)
    for k in range(11, 1, -1):
        series = 1.0 - (y * (1.0 / k)) * series
    return jnp.where(y < 0.5, y * series, 1.0 - jnp.exp(-y))


def leaving(chunk, places, gated_ref, out_ref, sems):
    rows = pl.ds(places[chunk] * LANES, LANES)
    return pltpu.make_async_copy(gated_ref.at[rows, :], out_ref.at[rows, :], sems.at[chunk])


def finish(chunk, places, conv_ref, q_ref, gated_ref, out_ref, sems):
    chunks = len(places)
    length = conv_ref.shape[0] // chunks
    rows = pl.ds(places[chunk] * LANES, LANES)
    conv = conv_ref[pl.ds(chunk, length, stride=chunks), :].T
    gated_ref[rows, :] = (q_ref[rows, :].astype(jnp.float32) * conv).astype(jnp.bfloat16)
    leaving(chunk, places, gated_ref, out_ref, sems).start()


def local_kernel(
    places, order, gathered_ref, series_ref, gain_ref, q_ref, conv_ref, weight_ref, out_ref, gated_ref, sems
):
    chunks = len(places)
    length = series_ref.shape[0] // chunks
    for half in range(chunks // SUBLANES):
        rate = mode_rows(gathered_ref, 0, order, 2 * order, chunks, half)
        residue = mode_rows(gathered_ref, order, order, 2 * order, chunks, half)
        decay = [jnp.exp(-rate[r]) for r in range(order)]
        weight = [residue[r] * jnp.sqrt(one_minus_exp(2.0 * rate[r])) for r in range(order)]
        for r in range(order):
            weight_ref[pl.ds(half * SUBLANES * order + r, SUBLANES, stride=order), :] = weight[r]
        own = places[half * SUBLANES : (half + 1) * SUBLANES]
        gain = jnp.concatenate([gain_ref[pl.ds(place, 1), :] for place in own], axis=0)

        def steps(i, state):
            state = list(state)
            for u in range(UNROLL):
                row = pl.multiple_of((i * UNROLL + u) * chunks + half * SUBLANES, SUBLANES)
                x = series_ref[pl.ds(row, SUBLANES), :]
                for r in range(order):
                    state[r] = decay[r] * state[r] + x
                terms = [weight[r] * state[r] for r in range(order)]
                conv_ref[pl.ds(row, SUBLANES), :] = tree_sum(terms + [gain * x])
            return tuple(state)

        zero = jnp.zeros((SUBLANES, LANES), jnp.float32)
        lax.fori_loop(0, length // UNROLL, steps, (zero,) * order)

    @pl.when(lax.axis_index("seq") == 0)
    def _():
        for chunk in range(chunks):
            finish(chunk, places, conv_ref, q_ref, gated_ref, out_ref, sems)
        for chunk in range(chunks):
            leaving(chunk, places, gated_ref, out_ref, sems).wait()


def output_kernel(
    places, order, gathered_ref, weight_ref, carry_ref, local_ref, q_ref, _, out_ref, conv_ref, gated_ref, sems
):
    chunks = len(places)
    length = local_ref.shape[0] // chunks
    tokens = length // SUBLANES

    @pl.when(lax.axis_index("seq") > 0)
    def _():
        for half in range(chunks // SUBLANES):
            decay = [jnp.exp(-rate) for rate in mode_rows(gathered_ref, 0, order, 2 * order, chunks, half)]
            weight = mode_rows(weight_ref, 0, order, order, chunks, half)
            carry = mode_rows(carry_ref, 0, order, order, chunks, half)

            def steps(i, fading):
                fading = list(fading)
                for u in range(tokens):
                    row = (i * tokens + u) * chunks + half * SUBLANES
                    if not isinstance(row, int):
                        row = pl.multiple_of(row, SUBLANES)
                    fading = [decay[r] * fading[r] for r in range(order)]
                    conv_ref[pl.ds(row, SUBLANES), :] = tree_sum(fading + [local_ref[pl.ds(row, SUBLANES), :]])
                return tuple(fading)

            fading = tuple(weight[r] * carry[r] for r in range(order))
            if half == 0:
                lax.fori_loop(0, SUBLANES, steps, fading)
            else:
                for i in range(SUBLANES):
                    fading = steps(i, fading)
                    finish((half - 1) * SUBLANES + i, places, conv_ref, q_ref, gated_ref, out_ref, sems)
        for chunk in range(chunks - SUBLANES, chunks):
            finish(chunk, places, conv_ref, q_ref, gated_ref, out_ref, sems)
        for chunk in range(chunks):
            leaving(chunk, places, gated_ref, out_ref, sems).wait()


def copies_kernel(rate_hbm, residue_hbm, copies_ref, rate_ref, residue_ref, sems):
    pairs = ((rate_hbm, rate_ref), (residue_hbm, residue_ref))
    loads = [pltpu.make_async_copy(source, target, sems.at[i]) for i, (source, target) in enumerate(pairs)]
    for load in loads:
        load.start()
    for load in loads:
        load.wait()
    order = rate_ref.shape[0]
    for piece in range(copies_ref.shape[0]):
        copies_ref[piece, :order] = rate_ref[...]
        copies_ref[piece, order:] = residue_ref[...]


def call(kernel, out_shape, *args, in_spaces=None, out_spaces=None, aliases=None, scratch=(), flops=0):
    in_bytes = sum(a.size * a.dtype.itemsize for a in args)
    in_spaces = in_spaces or [pl.ANY if i in (aliases or {}) else pltpu.VMEM for i in range(len(args))]
    out_spaces = out_spaces or jax.tree.map(lambda _: pltpu.VMEM, out_shape)
    return pl.pallas_call(
        kernel,
        out_shape=out_shape,
        in_specs=[pl.BlockSpec(memory_space=space) for space in in_spaces],
        out_specs=jax.tree.map(lambda space: pl.BlockSpec(memory_space=space), out_spaces),
        scratch_shapes=list(scratch),
        input_output_aliases=aliases or {},
        compiler_params=pltpu.CompilerParams(vmem_limit_bytes=VMEM_LIMIT),
        cost_estimate=pl.CostEstimate(flops=flops, bytes_accessed=in_bytes, transcendentals=0),
    )(*args)


def to_chunks(pieces):
    owners, rows, own = pieces.shape
    if own == LANES:
        return pieces
    if own < LANES:
        group = LANES // own
        return pieces.reshape(owners // group, group, rows, own).swapaxes(1, 2).reshape(-1, rows, LANES)
    return pieces.reshape(owners, rows, own // LANES, LANES).swapaxes(1, 2).reshape(-1, rows, LANES)


def from_chunks(pieces, owners):
    chunks, rows, _ = pieces.shape
    own = chunks * LANES // owners
    if own == LANES:
        return pieces
    if own < LANES:
        group = LANES // own
        return pieces.reshape(chunks, rows, group, own).swapaxes(1, 2).reshape(owners, rows, own)
    return pieces.reshape(owners, own // LANES, rows, LANES).swapaxes(1, 2).reshape(owners, rows, own)


def all_to_all(pieces, members):
    return lax.all_to_all(pieces, "seq", split_axis=0, concat_axis=0, axis_index_groups=[members], tiled=True)


def shards(blocks, q_proj, k_proj, value_projection, residues, rates, direct_gain):
    channels, length = q_proj.shape
    order = residues.shape[1]
    chunks = channels // LANES
    f32 = jnp.float32

    members, places = list(range(blocks)), list(range(chunks))
    if blocks == chunks:
        members, places = members[::-1], places[::-1]

    own_rates = rates.T
    in_hbm = [pltpu.with_memory_space_constraint(array, pltpu.HBM) for array in (own_rates, residues.T)]
    copies = call(
        copies_kernel,
        jax.ShapeDtypeStruct((blocks, 2 * order, rates.shape[0]), f32),
        *in_hbm,
        in_spaces=[pl.ANY] * 2,
        scratch=[pltpu.VMEM(own_rates.shape, f32)] * 2 + [pltpu.SemaphoreType.DMA((2,))],
    )
    gathered = all_to_all(copies, members)
    params = to_chunks(gathered).reshape(chunks * 2 * order, LANES)

    series = call(
        functools.partial(prepare_kernel, places),
        jax.ShapeDtypeStruct((length * chunks, LANES), f32),
        k_proj,
        value_projection,
        flops=channels * length,
    )
    ends = call(
        functools.partial(state_kernel, chunks, order),
        jax.ShapeDtypeStruct((chunks * order, LANES), f32),
        params,
        series,
        flops=2 * order * channels * length,
    )
    local_series, ends = lax.optimization_barrier((series, ends))
    ends = from_chunks(ends.reshape(chunks, order, LANES), blocks)
    out_shape = jax.ShapeDtypeStruct((channels, length), jnp.bfloat16)
    out_scratch = [pltpu.VMEM(out_shape.shape, out_shape.dtype), pltpu.SemaphoreType.DMA((chunks,))]
    local, weights, out = call(
        functools.partial(local_kernel, places, order),
        (
            jax.ShapeDtypeStruct((length * chunks, LANES), f32),
            jax.ShapeDtypeStruct((chunks * order, LANES), f32),
            out_shape,
        ),
        params,
        local_series,
        direct_gain.reshape(chunks, LANES),
        q_proj,
        out_spaces=(pltpu.VMEM, pltpu.VMEM, pl.ANY),
        scratch=out_scratch,
        flops=4 * order * channels * length,
    )
    ends = all_to_all(ends, members)
    starts = call(
        functools.partial(prefix_kernel, length, members),
        jax.ShapeDtypeStruct(ends.shape, f32),
        own_rates,
        ends,
    )
    starts = all_to_all(starts, members)
    carry = to_chunks(starts).reshape(chunks * order, LANES)
    return call(
        functools.partial(output_kernel, places, order),
        out_shape,
        params,
        weights,
        carry,
        local,
        q_proj,
        out,
        out_spaces=pl.ANY,
        aliases={5: 0},
        scratch=[pltpu.VMEM((length * chunks, LANES), f32)] + out_scratch,
        flops=2 * order * channels * length,
    )


def solution(mesh):
    return jax.shard_map(
        functools.partial(shards, mesh.shape["seq"]),
        mesh=mesh,
        in_specs=(
            P("chan", ("groups", "seq")),
            P("chan", ("groups", "seq")),
            P("chan", ("groups", "seq")),
            P(("chan", "seq"), None),
            P(("chan", "seq"), None),
            P("chan"),
        ),
        out_specs=P("chan", ("groups", "seq")),
        check_vma=False,
    )
```

```python
import functools
import jax
import jax.numpy as jnp
from jax import lax
from jax.experimental import pallas as pl
from jax.experimental.pallas import tpu as pltpu
from jax.sharding import PartitionSpec as P

LANES = 128
SUBLANES = 8
UNROLL = 8
VMEM_LIMIT = 32 * 1024 * 1024


def prepare_kernel(places, k_ref, v_ref, series_ref):
    chunks, length = len(places), k_ref.shape[1]
    for chunk, place in enumerate(places):
        rows = pl.ds(place * LANES, LANES)
        gated = k_ref[rows, :].astype(jnp.float32) * v_ref[rows, :].astype(jnp.float32)
        series_ref[pl.ds(chunk, length, stride=chunks), :] = gated.T


def mode_rows(ref, base, order, per_chunk, chunks, half):
    first = half * SUBLANES * per_chunk + base
    return [ref[pl.ds(first + r, SUBLANES, stride=per_chunk), :] for r in range(order)]


def state_kernel(chunks, order, rates_ref, residue_ref, series_ref, state_ref):
    length = series_ref.shape[0] // chunks
    for chunk in range(chunks):
        state_ref[pl.ds((2 * chunk + 1) * order, order), :] = residue_ref[...]
    for half in range(chunks // SUBLANES):
        decay = [jnp.exp(-rate) for rate in mode_rows(rates_ref, 0, order, order, chunks, half)]

        def steps(i, state):
            state = list(state)
            for u in range(UNROLL):
                row = pl.multiple_of((i * UNROLL + u) * chunks + half * SUBLANES, SUBLANES)
                x = series_ref[pl.ds(row, SUBLANES), :]
                for r in range(order):
                    state[r] = decay[r] * state[r] + x
            return tuple(state)

        zero = jnp.zeros((SUBLANES, LANES), jnp.float32)
        state = lax.fori_loop(0, length // UNROLL, steps, (zero,) * order)
        for r in range(order):
            state_ref[pl.ds(half * SUBLANES * 2 * order + r, SUBLANES, stride=2 * order), :] = state[r]


def prefix_kernel(length, members, rate_ref, ends_ref, starts_ref):
    span_decay = jnp.exp(-float(length) * rate_ref[...])
    carry = jnp.zeros(rate_ref.shape, jnp.float32)
    for block in range(len(members)):
        starts_ref[members.index(block)] = carry
        carry = span_decay * carry + ends_ref[members.index(block), : rate_ref.shape[0]]


def tree_sum(terms):
    terms = list(terms)
    while len(terms) > 1:
        terms = [terms[i] + terms[i + 1] if i + 1 < len(terms) else terms[i] for i in range(0, len(terms), 2)]
    return terms[0]


def one_minus_exp(y):
    series = jnp.ones_like(y)
    for k in range(11, 1, -1):
        series = 1.0 - (y * (1.0 / k)) * series
    return jnp.where(y < 0.5, y * series, 1.0 - jnp.exp(-y))


def leaving(chunk, places, gated_ref, out_ref, sems):
    rows = pl.ds(places[chunk] * LANES, LANES)
    return pltpu.make_async_copy(gated_ref.at[rows, :], out_ref.at[rows, :], sems.at[chunk])


def finish(chunk, places, conv_ref, q_ref, gated_ref, out_ref, sems):
    chunks = len(places)
    length = conv_ref.shape[0] // chunks
    rows = pl.ds(places[chunk] * LANES, LANES)
    conv = conv_ref[pl.ds(chunk, length, stride=chunks), :].T
    gated_ref[rows, :] = (q_ref[rows, :].astype(jnp.float32) * conv).astype(jnp.bfloat16)
    leaving(chunk, places, gated_ref, out_ref, sems).start()


def local_kernel(
    places, order, rates_ref, residues_ref, series_ref, gain_ref, q_ref, conv_ref, weight_ref, out_ref, gated_ref, sems
):
    chunks = len(places)
    length = series_ref.shape[0] // chunks
    for half in range(chunks // SUBLANES):
        rate = mode_rows(rates_ref, 0, order, order, chunks, half)
        residue = mode_rows(residues_ref, order, order, 2 * order, chunks, half)
        decay = [jnp.exp(-rate[r]) for r in range(order)]
        weight = [residue[r] * jnp.sqrt(one_minus_exp(2.0 * rate[r])) for r in range(order)]
        for r in range(order):
            weight_ref[pl.ds(half * SUBLANES * order + r, SUBLANES, stride=order), :] = weight[r]
        own = places[half * SUBLANES : (half + 1) * SUBLANES]
        gain = jnp.concatenate([gain_ref[pl.ds(place, 1), :] for place in own], axis=0)

        def steps(i, state):
            state = list(state)
            for u in range(UNROLL):
                row = pl.multiple_of((i * UNROLL + u) * chunks + half * SUBLANES, SUBLANES)
                x = series_ref[pl.ds(row, SUBLANES), :]
                for r in range(order):
                    state[r] = decay[r] * state[r] + x
                terms = [weight[r] * state[r] for r in range(order)]
                conv_ref[pl.ds(row, SUBLANES), :] = tree_sum(terms + [gain * x])
            return tuple(state)

        zero = jnp.zeros((SUBLANES, LANES), jnp.float32)
        lax.fori_loop(0, length // UNROLL, steps, (zero,) * order)

    @pl.when(lax.axis_index("seq") == 0)
    def _():
        for chunk in range(chunks):
            finish(chunk, places, conv_ref, q_ref, gated_ref, out_ref, sems)
        for chunk in range(chunks):
            leaving(chunk, places, gated_ref, out_ref, sems).wait()


def output_kernel(
    places, order, rates_ref, weight_ref, carry_ref, local_ref, q_ref, _, out_ref, conv_ref, gated_ref, sems
):
    chunks = len(places)
    length = local_ref.shape[0] // chunks
    tokens = length // SUBLANES

    @pl.when(lax.axis_index("seq") > 0)
    def _():
        for half in range(chunks // SUBLANES):
            decay = [jnp.exp(-rate) for rate in mode_rows(rates_ref, 0, order, order, chunks, half)]
            weight = mode_rows(weight_ref, 0, order, order, chunks, half)
            carry = mode_rows(carry_ref, 0, order, order, chunks, half)

            def steps(i, fading):
                fading = list(fading)
                for u in range(tokens):
                    row = (i * tokens + u) * chunks + half * SUBLANES
                    if not isinstance(row, int):
                        row = pl.multiple_of(row, SUBLANES)
                    fading = [decay[r] * fading[r] for r in range(order)]
                    conv_ref[pl.ds(row, SUBLANES), :] = tree_sum(fading + [local_ref[pl.ds(row, SUBLANES), :]])
                return tuple(fading)

            fading = tuple(weight[r] * carry[r] for r in range(order))
            if half == 0:
                lax.fori_loop(0, SUBLANES, steps, fading)
            else:
                for i in range(SUBLANES):
                    fading = steps(i, fading)
                    finish((half - 1) * SUBLANES + i, places, conv_ref, q_ref, gated_ref, out_ref, sems)
        for chunk in range(chunks - SUBLANES, chunks):
            finish(chunk, places, conv_ref, q_ref, gated_ref, out_ref, sems)
        for chunk in range(chunks):
            leaving(chunk, places, gated_ref, out_ref, sems).wait()


def call(kernel, out_shape, *args, in_spaces=None, out_spaces=None, aliases=None, scratch=(), flops=0):
    in_bytes = sum(a.size * a.dtype.itemsize for a in args)
    in_spaces = in_spaces or [pl.ANY if i in (aliases or {}) else pltpu.VMEM for i in range(len(args))]
    out_spaces = out_spaces or jax.tree.map(lambda _: pltpu.VMEM, out_shape)
    return pl.pallas_call(
        kernel,
        out_shape=out_shape,
        in_specs=[pl.BlockSpec(memory_space=space) for space in in_spaces],
        out_specs=jax.tree.map(lambda space: pl.BlockSpec(memory_space=space), out_spaces),
        scratch_shapes=list(scratch),
        input_output_aliases=aliases or {},
        compiler_params=pltpu.CompilerParams(vmem_limit_bytes=VMEM_LIMIT),
        cost_estimate=pl.CostEstimate(flops=flops, bytes_accessed=in_bytes, transcendentals=0),
    )(*args)


def to_chunks(pieces):
    owners, rows, own = pieces.shape
    if own == LANES:
        return pieces
    if own < LANES:
        group = LANES // own
        return pieces.reshape(owners // group, group, rows, own).swapaxes(1, 2).reshape(-1, rows, LANES)
    return pieces.reshape(owners, rows, own // LANES, LANES).swapaxes(1, 2).reshape(-1, rows, LANES)


def from_chunks(pieces, owners):
    chunks, rows, _ = pieces.shape
    own = chunks * LANES // owners
    if own == LANES:
        return pieces
    if own < LANES:
        group = LANES // own
        return pieces.reshape(chunks, rows, group, own).swapaxes(1, 2).reshape(owners, rows, own)
    return pieces.reshape(owners, own // LANES, rows, LANES).swapaxes(1, 2).reshape(owners, rows, own)


def all_to_all(pieces, members):
    return lax.all_to_all(pieces, "seq", split_axis=0, concat_axis=0, axis_index_groups=[members], tiled=True)


def shards(blocks, q_proj, k_proj, value_projection, residues, rates, direct_gain):
    channels, length = q_proj.shape
    order = residues.shape[1]
    chunks = channels // LANES
    f32 = jnp.float32

    members, places = list(range(blocks)), list(range(chunks))
    if blocks == chunks:
        members, places = members[::-1], places[::-1]

    own_rates, own_residues = rates.T, residues.T
    copies = jnp.broadcast_to(own_rates[None], (blocks,) + own_rates.shape)
    all_rates = to_chunks(all_to_all(copies, members)).reshape(chunks * order, LANES)

    series = call(
        functools.partial(prepare_kernel, places),
        jax.ShapeDtypeStruct((length * chunks, LANES), f32),
        k_proj,
        value_projection,
        flops=channels * length,
    )
    whole_chunk = own_residues.shape[1] == LANES
    ends = call(
        functools.partial(state_kernel, chunks, order),
        jax.ShapeDtypeStruct((chunks * 2 * order, LANES), f32),
        all_rates,
        own_residues if whole_chunk else jnp.zeros((order, LANES), f32),
        series,
        flops=2 * order * channels * length,
    )
    local_series, ends = lax.optimization_barrier((series, ends))
    ends = from_chunks(ends.reshape(chunks, 2 * order, LANES), blocks)
    if not whole_chunk:
        ends = ends.at[:, order:].set(own_residues)
    ends = all_to_all(ends, members)
    all_residues = to_chunks(ends).reshape(chunks * 2 * order, LANES)
    out_shape = jax.ShapeDtypeStruct((channels, length), jnp.bfloat16)
    out_scratch = [pltpu.VMEM(out_shape.shape, out_shape.dtype), pltpu.SemaphoreType.DMA((chunks,))]
    local, weights, out = call(
        functools.partial(local_kernel, places, order),
        (
            jax.ShapeDtypeStruct((length * chunks, LANES), f32),
            jax.ShapeDtypeStruct((chunks * order, LANES), f32),
            out_shape,
        ),
        all_rates,
        all_residues,
        local_series,
        direct_gain.reshape(chunks, LANES),
        q_proj,
        out_spaces=(pltpu.VMEM, pltpu.VMEM, pl.ANY),
        scratch=out_scratch,
        flops=4 * order * channels * length,
    )
    starts = call(
        functools.partial(prefix_kernel, length, members),
        jax.ShapeDtypeStruct((blocks,) + own_rates.shape, f32),
        own_rates,
        ends,
    )
    starts = all_to_all(starts, members)
    carry = to_chunks(starts).reshape(chunks * order, LANES)
    return call(
        functools.partial(output_kernel, places, order),
        out_shape,
        all_rates,
        weights,
        carry,
        local,
        q_proj,
        out,
        out_spaces=pl.ANY,
        aliases={5: 0},
        scratch=[pltpu.VMEM((length * chunks, LANES), f32)] + out_scratch,
        flops=2 * order * channels * length,
    )


def solution(mesh):
    return jax.shard_map(
        functools.partial(shards, mesh.shape["seq"]),
        mesh=mesh,
        in_specs=(
            P("chan", ("groups", "seq")),
            P("chan", ("groups", "seq")),
            P("chan", ("groups", "seq")),
            P(("chan", "seq"), None),
            P(("chan", "seq"), None),
            P("chan"),
        ),
        out_specs=P("chan", ("groups", "seq")),
        check_vma=False,
    )
```

```python
import functools
import jax
import jax.numpy as jnp
from jax import lax
from jax.experimental import pallas as pl
from jax.experimental.pallas import tpu as pltpu
from jax.sharding import PartitionSpec as P

LANES = 128
SUBLANES = 8
UNROLL = 8
VMEM_LIMIT = 32 * 1024 * 1024


def prepare_kernel(places, k_ref, v_ref, series_ref):
    chunks, length = len(places), k_ref.shape[1]
    for chunk, place in enumerate(places):
        rows = pl.ds(place * LANES, LANES)
        gated = k_ref[rows, :].astype(jnp.float32) * v_ref[rows, :].astype(jnp.float32)
        series_ref[pl.ds(chunk, length, stride=chunks), :] = gated.T


def mode_rows(ref, base, order, per_chunk, chunks, half):
    first = half * SUBLANES * per_chunk + base
    return [ref[pl.ds(first + r, SUBLANES, stride=per_chunk), :] for r in range(order)]


def state_kernel(chunks, order, rates_ref, series_ref, state_ref):
    length = series_ref.shape[0] // chunks
    for half in range(chunks // SUBLANES):
        decay = [jnp.exp(-rate) for rate in mode_rows(rates_ref, 0, order, order, chunks, half)]

        def steps(i, state):
            state = list(state)
            for u in range(UNROLL):
                row = pl.multiple_of((i * UNROLL + u) * chunks + half * SUBLANES, SUBLANES)
                x = series_ref[pl.ds(row, SUBLANES), :]
                for r in range(order):
                    state[r] = decay[r] * state[r] + x
            return tuple(state)

        zero = jnp.zeros((SUBLANES, LANES), jnp.float32)
        state = lax.fori_loop(0, length // UNROLL, steps, (zero,) * order)
        for r in range(order):
            state_ref[pl.ds(half * SUBLANES * order + r, SUBLANES, stride=order), :] = state[r]


def prefix_kernel(length, members, rate_ref, ends_ref, starts_ref):
    span_decay = jnp.exp(-float(length) * rate_ref[...])
    carry = jnp.zeros(rate_ref.shape, jnp.float32)
    for block in range(len(members)):
        starts_ref[members.index(block)] = carry
        carry = span_decay * carry + ends_ref[members.index(block)]


def tree_sum(terms):
    terms = list(terms)
    while len(terms) > 1:
        terms = [terms[i] + terms[i + 1] if i + 1 < len(terms) else terms[i] for i in range(0, len(terms), 2)]
    return terms[0]


def one_minus_exp(y):
    series = jnp.ones_like(y)
    for k in range(11, 1, -1):
        series = 1.0 - (y * (1.0 / k)) * series
    return jnp.where(y < 0.5, y * series, 1.0 - jnp.exp(-y))


def leaving(chunk, places, gated_ref, out_ref, sems):
    rows = pl.ds(places[chunk] * LANES, LANES)
    return pltpu.make_async_copy(gated_ref.at[rows, :], out_ref.at[rows, :], sems.at[chunk])


def finish(chunk, places, conv_ref, q_ref, gated_ref, out_ref, sems):
    chunks = len(places)
    length = conv_ref.shape[0] // chunks
    rows = pl.ds(places[chunk] * LANES, LANES)
    conv = conv_ref[pl.ds(chunk, length, stride=chunks), :].T
    gated_ref[rows, :] = (q_ref[rows, :].astype(jnp.float32) * conv).astype(jnp.bfloat16)
    leaving(chunk, places, gated_ref, out_ref, sems).start()


def local_kernel(
    places, order, rates_ref, residues_ref, series_ref, gain_ref, q_ref, conv_ref, weight_ref, out_ref, gated_ref, sems
):
    chunks = len(places)
    length = series_ref.shape[0] // chunks
    for half in range(chunks // SUBLANES):
        rate = mode_rows(rates_ref, 0, order, order, chunks, half)
        residue = mode_rows(residues_ref, 0, order, order, chunks, half)
        decay = [jnp.exp(-rate[r]) for r in range(order)]
        weight = [residue[r] * jnp.sqrt(one_minus_exp(2.0 * rate[r])) for r in range(order)]
        for r in range(order):
            weight_ref[pl.ds(half * SUBLANES * order + r, SUBLANES, stride=order), :] = weight[r]
        own = places[half * SUBLANES : (half + 1) * SUBLANES]
        gain = jnp.concatenate([gain_ref[pl.ds(place, 1), :] for place in own], axis=0)

        def steps(i, state):
            state = list(state)
            for u in range(UNROLL):
                row = pl.multiple_of((i * UNROLL + u) * chunks + half * SUBLANES, SUBLANES)
                x = series_ref[pl.ds(row, SUBLANES), :]
                for r in range(order):
                    state[r] = decay[r] * state[r] + x
                terms = [weight[r] * state[r] for r in range(order)]
                conv_ref[pl.ds(row, SUBLANES), :] = tree_sum(terms + [gain * x])
            return tuple(state)

        zero = jnp.zeros((SUBLANES, LANES), jnp.float32)
        lax.fori_loop(0, length // UNROLL, steps, (zero,) * order)

    @pl.when(lax.axis_index("seq") == 0)
    def _():
        for chunk in range(chunks):
            finish(chunk, places, conv_ref, q_ref, gated_ref, out_ref, sems)
        for chunk in range(chunks):
            leaving(chunk, places, gated_ref, out_ref, sems).wait()


def output_kernel(
    places, order, rates_ref, weight_ref, carry_ref, local_ref, q_ref, _, out_ref, conv_ref, gated_ref, sems
):
    chunks = len(places)
    length = local_ref.shape[0] // chunks
    tokens = length // SUBLANES

    @pl.when(lax.axis_index("seq") > 0)
    def _():
        for half in range(chunks // SUBLANES):
            decay = [jnp.exp(-rate) for rate in mode_rows(rates_ref, 0, order, order, chunks, half)]
            weight = mode_rows(weight_ref, 0, order, order, chunks, half)
            carry = mode_rows(carry_ref, 0, order, order, chunks, half)

            def steps(i, fading):
                fading = list(fading)
                for u in range(tokens):
                    row = (i * tokens + u) * chunks + half * SUBLANES
                    if not isinstance(row, int):
                        row = pl.multiple_of(row, SUBLANES)
                    fading = [decay[r] * fading[r] for r in range(order)]
                    conv_ref[pl.ds(row, SUBLANES), :] = tree_sum(fading + [local_ref[pl.ds(row, SUBLANES), :]])
                return tuple(fading)

            fading = tuple(weight[r] * carry[r] for r in range(order))
            if half == 0:
                lax.fori_loop(0, SUBLANES, steps, fading)
            else:
                for i in range(SUBLANES):
                    fading = steps(i, fading)
                    finish((half - 1) * SUBLANES + i, places, conv_ref, q_ref, gated_ref, out_ref, sems)
        for chunk in range(chunks - SUBLANES, chunks):
            finish(chunk, places, conv_ref, q_ref, gated_ref, out_ref, sems)
        for chunk in range(chunks):
            leaving(chunk, places, gated_ref, out_ref, sems).wait()


def call(kernel, out_shape, *args, in_spaces=None, out_spaces=None, aliases=None, scratch=(), flops=0):
    in_bytes = sum(a.size * a.dtype.itemsize for a in args)
    in_spaces = in_spaces or [pl.ANY if i in (aliases or {}) else pltpu.VMEM for i in range(len(args))]
    out_spaces = out_spaces or jax.tree.map(lambda _: pltpu.VMEM, out_shape)
    return pl.pallas_call(
        kernel,
        out_shape=out_shape,
        in_specs=[pl.BlockSpec(memory_space=space) for space in in_spaces],
        out_specs=jax.tree.map(lambda space: pl.BlockSpec(memory_space=space), out_spaces),
        scratch_shapes=list(scratch),
        input_output_aliases=aliases or {},
        compiler_params=pltpu.CompilerParams(vmem_limit_bytes=VMEM_LIMIT),
        cost_estimate=pl.CostEstimate(flops=flops, bytes_accessed=in_bytes, transcendentals=0),
    )(*args)


def to_chunks(pieces):
    owners, rows, own = pieces.shape
    if own == LANES:
        return pieces
    if own < LANES:
        group = LANES // own
        return pieces.reshape(owners // group, group, rows, own).swapaxes(1, 2).reshape(-1, rows, LANES)
    return pieces.reshape(owners, rows, own // LANES, LANES).swapaxes(1, 2).reshape(-1, rows, LANES)


def from_chunks(pieces, owners):
    chunks, rows, _ = pieces.shape
    own = chunks * LANES // owners
    if own == LANES:
        return pieces
    if own < LANES:
        group = LANES // own
        return pieces.reshape(chunks, rows, group, own).swapaxes(1, 2).reshape(owners, rows, own)
    return pieces.reshape(owners, own // LANES, rows, LANES).swapaxes(1, 2).reshape(owners, rows, own)


def all_to_all(pieces, members):
    return lax.all_to_all(pieces, "seq", split_axis=0, concat_axis=0, axis_index_groups=[members], tiled=True)


def shards(blocks, q_proj, k_proj, value_projection, residues, rates, direct_gain):
    channels, length = q_proj.shape
    order = residues.shape[1]
    chunks = channels // LANES
    f32 = jnp.float32

    members, places = list(range(blocks)), list(range(chunks))
    if blocks == chunks:
        members, places = members[::-1], places[::-1]

    own_rates = rates.T
    all_residues = lax.all_gather(residues.T, "seq", axis=0, axis_index_groups=[members])
    all_residues = to_chunks(all_residues).reshape(chunks * order, LANES)
    copies = jnp.broadcast_to(own_rates[None], (blocks,) + own_rates.shape)
    all_rates = to_chunks(all_to_all(copies, members)).reshape(chunks * order, LANES)

    series = call(
        functools.partial(prepare_kernel, places),
        jax.ShapeDtypeStruct((length * chunks, LANES), f32),
        k_proj,
        value_projection,
        flops=channels * length,
    )
    ends = call(
        functools.partial(state_kernel, chunks, order),
        jax.ShapeDtypeStruct((chunks * order, LANES), f32),
        all_rates,
        series,
        flops=2 * order * channels * length,
    )
    local_series, ends = lax.optimization_barrier((series, ends))
    ends = all_to_all(from_chunks(ends.reshape(chunks, order, LANES), blocks), members)
    out_shape = jax.ShapeDtypeStruct((channels, length), jnp.bfloat16)
    out_scratch = [pltpu.VMEM(out_shape.shape, out_shape.dtype), pltpu.SemaphoreType.DMA((chunks,))]
    local, weights, out = call(
        functools.partial(local_kernel, places, order),
        (
            jax.ShapeDtypeStruct((length * chunks, LANES), f32),
            jax.ShapeDtypeStruct((chunks * order, LANES), f32),
            out_shape,
        ),
        all_rates,
        all_residues,
        local_series,
        direct_gain.reshape(chunks, LANES),
        q_proj,
        out_spaces=(pltpu.VMEM, pltpu.VMEM, pl.ANY),
        scratch=out_scratch,
        flops=4 * order * channels * length,
    )
    starts = call(
        functools.partial(prefix_kernel, length, members),
        jax.ShapeDtypeStruct((blocks,) + own_rates.shape, f32),
        own_rates,
        ends,
    )
    starts = all_to_all(starts, members)
    carry = to_chunks(starts).reshape(chunks * order, LANES)
    return call(
        functools.partial(output_kernel, places, order),
        out_shape,
        all_rates,
        weights,
        carry,
        local,
        q_proj,
        out,
        out_spaces=pl.ANY,
        aliases={5: 0},
        scratch=[pltpu.VMEM((length * chunks, LANES), f32)] + out_scratch,
        flops=2 * order * channels * length,
    )


def solution(mesh):
    return jax.shard_map(
        functools.partial(shards, mesh.shape["seq"]),
        mesh=mesh,
        in_specs=(
            P("chan", ("groups", "seq")),
            P("chan", ("groups", "seq")),
            P("chan", ("groups", "seq")),
            P(("chan", "seq"), None),
            P(("chan", "seq"), None),
            P("chan"),
        ),
        out_specs=P("chan", ("groups", "seq")),
        check_vma=False,
    )
```

```python
import functools
import jax
import jax.numpy as jnp
from jax import lax
from jax.experimental import pallas as pl
from jax.experimental.pallas import tpu as pltpu
from jax.sharding import PartitionSpec as P

LANES = 128
SUBLANES = 8
UNROLL = 8
COPIES_COST = 10**10
VMEM_LIMIT = 32 * 1024 * 1024


def copies_kernel(rate_hbm, copies_ref, rate_ref, sem):
    load = pltpu.make_async_copy(rate_hbm, rate_ref, sem)
    load.start()
    load.wait()
    decay = jnp.exp(-rate_ref[...])
    for piece in range(copies_ref.shape[0]):
        copies_ref[piece] = decay


def mode_rows(ref, base, order, per_chunk, chunks, half):
    first = half * SUBLANES * per_chunk + base
    return [ref[pl.ds(first + r, SUBLANES, stride=per_chunk), :] for r in range(order)]


def one_minus_exp(y):
    series = jnp.ones_like(y)
    for k in range(11, 1, -1):
        series = 1.0 - (y * (1.0 / k)) * series
    return jnp.where(y < 0.5, y * series, 1.0 - jnp.exp(-y))


def weights_of(residue, rate):
    return residue * jnp.sqrt(one_minus_exp(2.0 * rate))


def state_kernel(places, order, decays_ref, rate_ref, residue_ref, k_ref, v_ref, series_ref, state_ref):
    chunks, length = len(places), k_ref.shape[1]
    tokens = length // SUBLANES
    halves = chunks // SUBLANES

    def build(chunk):
        rows = pl.ds(places[chunk] * LANES, LANES)
        gated = k_ref[rows, :].astype(jnp.float32) * v_ref[rows, :].astype(jnp.float32)
        series_ref[pl.ds(chunk, length, stride=chunks), :] = gated.T

    weight = weights_of(residue_ref[...], rate_ref[...])
    for chunk in range(chunks):
        state_ref[pl.ds((2 * chunk + 1) * order, order), :] = weight
    for chunk in range(SUBLANES):
        build(chunk)
    for half in range(halves):
        decay = mode_rows(decays_ref, 0, order, order, chunks, half)

        def steps(i, state):
            state = list(state)
            for u in range(tokens):
                row = (i * tokens + u) * chunks + half * SUBLANES
                if not isinstance(row, int):
                    row = pl.multiple_of(row, SUBLANES)
                x = series_ref[pl.ds(row, SUBLANES), :]
                for r in range(order):
                    state[r] = decay[r] * state[r] + x
            return tuple(state)

        state = (jnp.zeros((SUBLANES, LANES), jnp.float32),) * order
        if half + 1 < halves:
            for i in range(SUBLANES):
                state = steps(i, state)
                build((half + 1) * SUBLANES + i)
        else:
            state = lax.fori_loop(0, SUBLANES, steps, state)
        for r in range(order):
            state_ref[pl.ds(half * SUBLANES * 2 * order + r, SUBLANES, stride=2 * order), :] = state[r]


def prefix_kernel(length, members, rate_ref, ends_ref, starts_ref):
    span_decay = jnp.exp(-float(length) * rate_ref[...])
    carry = jnp.zeros(rate_ref.shape, jnp.float32)
    for block in range(len(members)):
        starts_ref[members.index(block)] = carry
        carry = span_decay * carry + ends_ref[members.index(block), : rate_ref.shape[0]]


def tree_sum(terms):
    terms = list(terms)
    while len(terms) > 1:
        terms = [terms[i] + terms[i + 1] if i + 1 < len(terms) else terms[i] for i in range(0, len(terms), 2)]
    return terms[0]


def leaving(chunk, places, gated_ref, out_ref, sems):
    rows = pl.ds(places[chunk] * LANES, LANES)
    return pltpu.make_async_copy(gated_ref.at[rows, :], out_ref.at[rows, :], sems.at[chunk])


def finish(chunk, places, conv_ref, q_ref, gated_ref, out_ref, sems):
    chunks = len(places)
    length = conv_ref.shape[0] // chunks
    rows = pl.ds(places[chunk] * LANES, LANES)
    conv = conv_ref[pl.ds(chunk, length, stride=chunks), :].T
    gated_ref[rows, :] = (q_ref[rows, :].astype(jnp.float32) * conv).astype(jnp.bfloat16)
    leaving(chunk, places, gated_ref, out_ref, sems).start()


def local_kernel(
    places, order, decays_ref, weights_ref, series_ref, gain_ref, q_ref, conv_ref, out_ref, gated_ref, sems
):
    chunks = len(places)
    length = series_ref.shape[0] // chunks
    for half in range(chunks // SUBLANES):
        decay = mode_rows(decays_ref, 0, order, order, chunks, half)
        weight = mode_rows(weights_ref, order, order, 2 * order, chunks, half)
        own = places[half * SUBLANES : (half + 1) * SUBLANES]
        gain = jnp.concatenate([gain_ref[pl.ds(place, 1), :] for place in own], axis=0)

        def steps(i, state):
            state = list(state)
            for u in range(UNROLL):
                row = pl.multiple_of((i * UNROLL + u) * chunks + half * SUBLANES, SUBLANES)
                x = series_ref[pl.ds(row, SUBLANES), :]
                for r in range(order):
                    state[r] = decay[r] * state[r] + x
                terms = [weight[r] * state[r] for r in range(order)]
                conv_ref[pl.ds(row, SUBLANES), :] = tree_sum(terms + [gain * x])
            return tuple(state)

        zero = jnp.zeros((SUBLANES, LANES), jnp.float32)
        lax.fori_loop(0, length // UNROLL, steps, (zero,) * order)

    @pl.when(lax.axis_index("seq") == 0)
    def _():
        for chunk in range(chunks):
            finish(chunk, places, conv_ref, q_ref, gated_ref, out_ref, sems)
        for chunk in range(chunks):
            leaving(chunk, places, gated_ref, out_ref, sems).wait()


def output_kernel(
    places, order, decays_ref, weights_ref, carry_ref, local_ref, q_ref, _, out_ref, conv_ref, gated_ref, sems
):
    chunks = len(places)
    length = local_ref.shape[0] // chunks
    tokens = length // SUBLANES

    @pl.when(lax.axis_index("seq") > 0)
    def _():
        for half in range(chunks // SUBLANES):
            decay = mode_rows(decays_ref, 0, order, order, chunks, half)
            weight = mode_rows(weights_ref, order, order, 2 * order, chunks, half)
            carry = mode_rows(carry_ref, 0, order, order, chunks, half)

            def steps(i, fading):
                fading = list(fading)
                for u in range(tokens):
                    row = (i * tokens + u) * chunks + half * SUBLANES
                    if not isinstance(row, int):
                        row = pl.multiple_of(row, SUBLANES)
                    fading = [decay[r] * fading[r] for r in range(order)]
                    conv_ref[pl.ds(row, SUBLANES), :] = tree_sum(fading + [local_ref[pl.ds(row, SUBLANES), :]])
                return tuple(fading)

            fading = tuple(weight[r] * carry[r] for r in range(order))
            if half == 0:
                lax.fori_loop(0, SUBLANES, steps, fading)
            else:
                for i in range(SUBLANES):
                    fading = steps(i, fading)
                    finish((half - 1) * SUBLANES + i, places, conv_ref, q_ref, gated_ref, out_ref, sems)
        for chunk in range(chunks - SUBLANES, chunks):
            finish(chunk, places, conv_ref, q_ref, gated_ref, out_ref, sems)
        for chunk in range(chunks):
            leaving(chunk, places, gated_ref, out_ref, sems).wait()


def call(kernel, out_shape, *args, in_spaces=None, out_spaces=None, aliases=None, scratch=(), flops=0):
    in_bytes = sum(a.size * a.dtype.itemsize for a in args)
    in_spaces = in_spaces or [pl.ANY if i in (aliases or {}) else pltpu.VMEM for i in range(len(args))]
    out_spaces = out_spaces or jax.tree.map(lambda _: pltpu.VMEM, out_shape)
    return pl.pallas_call(
        kernel,
        out_shape=out_shape,
        in_specs=[pl.BlockSpec(memory_space=space) for space in in_spaces],
        out_specs=jax.tree.map(lambda space: pl.BlockSpec(memory_space=space), out_spaces),
        scratch_shapes=list(scratch),
        input_output_aliases=aliases or {},
        compiler_params=pltpu.CompilerParams(vmem_limit_bytes=VMEM_LIMIT),
        cost_estimate=pl.CostEstimate(flops=flops, bytes_accessed=in_bytes, transcendentals=0),
    )(*args)


def to_chunks(pieces):
    owners, rows, own = pieces.shape
    if own == LANES:
        return pieces
    if own < LANES:
        group = LANES // own
        return pieces.reshape(owners // group, group, rows, own).swapaxes(1, 2).reshape(-1, rows, LANES)
    return pieces.reshape(owners, rows, own // LANES, LANES).swapaxes(1, 2).reshape(-1, rows, LANES)


def from_chunks(pieces, owners):
    chunks, rows, _ = pieces.shape
    own = chunks * LANES // owners
    if own == LANES:
        return pieces
    if own < LANES:
        group = LANES // own
        return pieces.reshape(chunks, rows, group, own).swapaxes(1, 2).reshape(owners, rows, own)
    return pieces.reshape(owners, own // LANES, rows, LANES).swapaxes(1, 2).reshape(owners, rows, own)


def all_to_all(pieces, members):
    return lax.all_to_all(pieces, "seq", split_axis=0, concat_axis=0, axis_index_groups=[members], tiled=True)


def shards(blocks, q_proj, k_proj, value_projection, residues, rates, direct_gain):
    channels, length = q_proj.shape
    order = residues.shape[1]
    chunks = channels // LANES
    f32 = jnp.float32

    members, places = list(range(blocks)), list(range(chunks))
    if blocks == chunks:
        members, places = members[::-1], places[::-1]

    own_rates, own_residues = rates.T, residues.T
    copies = call(
        copies_kernel,
        jax.ShapeDtypeStruct((blocks,) + own_rates.shape, f32),
        pltpu.with_memory_space_constraint(own_rates, pltpu.HBM),
        in_spaces=[pl.ANY],
        scratch=[pltpu.VMEM(own_rates.shape, f32), pltpu.SemaphoreType.DMA],
        flops=COPIES_COST,
    )
    decays = to_chunks(all_to_all(copies, members)).reshape(chunks * order, LANES)

    whole_chunk = own_rates.shape[1] == LANES
    unused = jnp.zeros((order, LANES), f32)
    series, ends = call(
        functools.partial(state_kernel, places, order),
        (
            jax.ShapeDtypeStruct((length * chunks, LANES), f32),
            jax.ShapeDtypeStruct((chunks * 2 * order, LANES), f32),
        ),
        decays,
        own_rates if whole_chunk else unused,
        own_residues if whole_chunk else unused,
        k_proj,
        value_projection,
        flops=2 * order * channels * length,
    )
    local_series, ends = lax.optimization_barrier((series, ends))
    ends = from_chunks(ends.reshape(chunks, 2 * order, LANES), blocks)
    if not whole_chunk:
        ends = ends.at[:, order:].set(weights_of(own_residues, own_rates))
    ends = all_to_all(ends, members)
    weights = to_chunks(ends).reshape(chunks * 2 * order, LANES)
    out_shape = jax.ShapeDtypeStruct((channels, length), jnp.bfloat16)
    out_scratch = [pltpu.VMEM(out_shape.shape, out_shape.dtype), pltpu.SemaphoreType.DMA((chunks,))]
    local, out = call(
        functools.partial(local_kernel, places, order),
        (
            jax.ShapeDtypeStruct((length * chunks, LANES), f32),
            out_shape,
        ),
        decays,
        weights,
        local_series,
        direct_gain.reshape(chunks, LANES),
        q_proj,
        out_spaces=(pltpu.VMEM, pl.ANY),
        scratch=out_scratch,
        flops=4 * order * channels * length,
    )
    starts = call(
        functools.partial(prefix_kernel, length, members),
        jax.ShapeDtypeStruct((blocks,) + own_rates.shape, f32),
        own_rates,
        ends,
    )
    starts = all_to_all(starts, members)
    carry = to_chunks(starts).reshape(chunks * order, LANES)
    return call(
        functools.partial(output_kernel, places, order),
        out_shape,
        decays,
        weights,
        carry,
        local,
        q_proj,
        out,
        out_spaces=pl.ANY,
        aliases={5: 0},
        scratch=[pltpu.VMEM((length * chunks, LANES), f32)] + out_scratch,
        flops=2 * order * channels * length,
    )


def solution(mesh):
    return jax.shard_map(
        functools.partial(shards, mesh.shape["seq"]),
        mesh=mesh,
        in_specs=(
            P("chan", ("groups", "seq")),
            P("chan", ("groups", "seq")),
            P("chan", ("groups", "seq")),
            P(("chan", "seq"), None),
            P(("chan", "seq"), None),
            P("chan"),
        ),
        out_specs=P("chan", ("groups", "seq")),
        check_vma=False,
    )
```

```python
import functools
import jax
import jax.numpy as jnp
from jax import lax
from jax.experimental import pallas as pl
from jax.experimental.pallas import tpu as pltpu
from jax.sharding import PartitionSpec as P

LANES = 128
SUBLANES = 8
UNROLL = 8
COPIES_COST = 10**10
VMEM_LIMIT = 32 * 1024 * 1024


def copies_kernel(rate_hbm, copies_ref, rate_ref, sem):
    load = pltpu.make_async_copy(rate_hbm, rate_ref, sem)
    load.start()
    load.wait()
    decay = jnp.exp(-rate_ref[...])
    for piece in range(copies_ref.shape[0]):
        copies_ref[piece] = decay


def token_rows(half, length, token):
    row = (half * length + token) * SUBLANES
    return pl.ds(row if isinstance(row, int) else pl.multiple_of(row, SUBLANES), SUBLANES)


def chunk_rows(chunk, length):
    return pl.ds(chunk // SUBLANES * length * SUBLANES + chunk % SUBLANES, length, stride=SUBLANES)


def mode_rows(ref, base, order, per_chunk, chunks, half):
    first = half * SUBLANES * per_chunk + base
    return [ref[pl.ds(first + r, SUBLANES, stride=per_chunk), :] for r in range(order)]


def one_minus_exp(y):
    series = jnp.ones_like(y)
    for k in range(11, 1, -1):
        series = 1.0 - (y * (1.0 / k)) * series
    return jnp.where(y < 0.5, y * series, 1.0 - jnp.exp(-y))


def weights_of(residue, rate):
    return residue * jnp.sqrt(one_minus_exp(2.0 * rate))


def state_kernel(places, order, decays_ref, rate_ref, residue_ref, k_ref, v_ref, series_ref, state_ref):
    chunks, length = len(places), k_ref.shape[1]
    tokens = length // SUBLANES
    halves = chunks // SUBLANES

    def build(chunk):
        rows = pl.ds(places[chunk] * LANES, LANES)
        gated = k_ref[rows, :].astype(jnp.float32) * v_ref[rows, :].astype(jnp.float32)
        series_ref[chunk_rows(chunk, length), :] = gated.T

    weight = weights_of(residue_ref[...], rate_ref[...])
    for chunk in range(chunks):
        state_ref[pl.ds((2 * chunk + 1) * order, order), :] = weight
    for chunk in range(SUBLANES):
        build(chunk)
    for half in range(halves):
        decay = mode_rows(decays_ref, 0, order, order, chunks, half)

        def steps(i, state):
            state = list(state)
            for u in range(tokens):
                x = series_ref[token_rows(half, length, i * tokens + u), :]
                for r in range(order):
                    state[r] = decay[r] * state[r] + x
            return tuple(state)

        state = (jnp.zeros((SUBLANES, LANES), jnp.float32),) * order
        if half + 1 < halves:
            for i in range(SUBLANES):
                state = steps(i, state)
                build((half + 1) * SUBLANES + i)
        else:
            state = lax.fori_loop(0, SUBLANES, steps, state)
        for r in range(order):
            state_ref[pl.ds(half * SUBLANES * 2 * order + r, SUBLANES, stride=2 * order), :] = state[r]


def prefix_kernel(length, members, rate_ref, ends_ref, starts_ref):
    span_decay = jnp.exp(-float(length) * rate_ref[...])
    carry = jnp.zeros(rate_ref.shape, jnp.float32)
    for block in range(len(members)):
        starts_ref[members.index(block)] = carry
        carry = span_decay * carry + ends_ref[members.index(block), : rate_ref.shape[0]]


def tree_sum(terms):
    terms = list(terms)
    while len(terms) > 1:
        terms = [terms[i] + terms[i + 1] if i + 1 < len(terms) else terms[i] for i in range(0, len(terms), 2)]
    return terms[0]


def leaving(chunk, places, gated_ref, out_ref, sems):
    rows = pl.ds(places[chunk] * LANES, LANES)
    return pltpu.make_async_copy(gated_ref.at[rows, :], out_ref.at[rows, :], sems.at[chunk])


def finish(chunk, places, conv_ref, q_ref, gated_ref, out_ref, sems):
    length = conv_ref.shape[0] // len(places)
    rows = pl.ds(places[chunk] * LANES, LANES)
    conv = conv_ref[chunk_rows(chunk, length), :].T
    gated_ref[rows, :] = (q_ref[rows, :].astype(jnp.float32) * conv).astype(jnp.bfloat16)
    leaving(chunk, places, gated_ref, out_ref, sems).start()


def local_kernel(
    places, order, decays_ref, weights_ref, series_ref, gain_ref, q_ref, conv_ref, out_ref, gated_ref, sems
):
    chunks = len(places)
    length = series_ref.shape[0] // chunks
    for half in range(chunks // SUBLANES):
        decay = mode_rows(decays_ref, 0, order, order, chunks, half)
        weight = mode_rows(weights_ref, order, order, 2 * order, chunks, half)
        own = places[half * SUBLANES : (half + 1) * SUBLANES]
        gain = jnp.concatenate([gain_ref[pl.ds(place, 1), :] for place in own], axis=0)

        def steps(i, state):
            state = list(state)
            for u in range(UNROLL):
                rows = token_rows(half, length, i * UNROLL + u)
                x = series_ref[rows, :]
                for r in range(order):
                    state[r] = decay[r] * state[r] + x
                terms = [weight[r] * state[r] for r in range(order)]
                conv_ref[rows, :] = tree_sum(terms + [gain * x])
            return tuple(state)

        zero = jnp.zeros((SUBLANES, LANES), jnp.float32)
        lax.fori_loop(0, length // UNROLL, steps, (zero,) * order)

    @pl.when(lax.axis_index("seq") == 0)
    def _():
        for chunk in range(chunks):
            finish(chunk, places, conv_ref, q_ref, gated_ref, out_ref, sems)
        for chunk in range(chunks):
            leaving(chunk, places, gated_ref, out_ref, sems).wait()


def output_kernel(
    places, order, decays_ref, weights_ref, carry_ref, local_ref, q_ref, _, out_ref, conv_ref, gated_ref, sems
):
    chunks = len(places)
    length = local_ref.shape[0] // chunks
    tokens = length // SUBLANES

    @pl.when(lax.axis_index("seq") > 0)
    def _():
        for half in range(chunks // SUBLANES):
            decay = mode_rows(decays_ref, 0, order, order, chunks, half)
            weight = mode_rows(weights_ref, order, order, 2 * order, chunks, half)
            carry = mode_rows(carry_ref, 0, order, order, chunks, half)

            def steps(i, fading):
                fading = list(fading)
                for u in range(tokens):
                    rows = token_rows(half, length, i * tokens + u)
                    fading = [decay[r] * fading[r] for r in range(order)]
                    conv_ref[rows, :] = tree_sum(fading + [local_ref[rows, :]])
                return tuple(fading)

            fading = tuple(weight[r] * carry[r] for r in range(order))
            if half == 0:
                lax.fori_loop(0, SUBLANES, steps, fading)
            else:
                for i in range(SUBLANES):
                    fading = steps(i, fading)
                    finish((half - 1) * SUBLANES + i, places, conv_ref, q_ref, gated_ref, out_ref, sems)
        for chunk in range(chunks - SUBLANES, chunks):
            finish(chunk, places, conv_ref, q_ref, gated_ref, out_ref, sems)
        for chunk in range(chunks):
            leaving(chunk, places, gated_ref, out_ref, sems).wait()


def call(kernel, out_shape, *args, in_spaces=None, out_spaces=None, aliases=None, scratch=(), flops=0):
    in_bytes = sum(a.size * a.dtype.itemsize for a in args)
    in_spaces = in_spaces or [pl.ANY if i in (aliases or {}) else pltpu.VMEM for i in range(len(args))]
    out_spaces = out_spaces or jax.tree.map(lambda _: pltpu.VMEM, out_shape)
    return pl.pallas_call(
        kernel,
        out_shape=out_shape,
        in_specs=[pl.BlockSpec(memory_space=space) for space in in_spaces],
        out_specs=jax.tree.map(lambda space: pl.BlockSpec(memory_space=space), out_spaces),
        scratch_shapes=list(scratch),
        input_output_aliases=aliases or {},
        compiler_params=pltpu.CompilerParams(vmem_limit_bytes=VMEM_LIMIT),
        cost_estimate=pl.CostEstimate(flops=flops, bytes_accessed=in_bytes, transcendentals=0),
    )(*args)


def to_chunks(pieces):
    owners, rows, own = pieces.shape
    if own == LANES:
        return pieces
    if own < LANES:
        group = LANES // own
        return pieces.reshape(owners // group, group, rows, own).swapaxes(1, 2).reshape(-1, rows, LANES)
    return pieces.reshape(owners, rows, own // LANES, LANES).swapaxes(1, 2).reshape(-1, rows, LANES)


def from_chunks(pieces, owners):
    chunks, rows, _ = pieces.shape
    own = chunks * LANES // owners
    if own == LANES:
        return pieces
    if own < LANES:
        group = LANES // own
        return pieces.reshape(chunks, rows, group, own).swapaxes(1, 2).reshape(owners, rows, own)
    return pieces.reshape(owners, own // LANES, rows, LANES).swapaxes(1, 2).reshape(owners, rows, own)


def all_to_all(pieces, members):
    return lax.all_to_all(pieces, "seq", split_axis=0, concat_axis=0, axis_index_groups=[members], tiled=True)


def shards(blocks, q_proj, k_proj, value_projection, residues, rates, direct_gain):
    channels, length = q_proj.shape
    order = residues.shape[1]
    chunks = channels // LANES
    f32 = jnp.float32

    members, places = list(range(blocks)), list(range(chunks))
    if blocks == chunks:
        members, places = members[::-1], places[::-1]

    own_rates, own_residues = rates.T, residues.T
    copies = call(
        copies_kernel,
        jax.ShapeDtypeStruct((blocks,) + own_rates.shape, f32),
        pltpu.with_memory_space_constraint(own_rates, pltpu.HBM),
        in_spaces=[pl.ANY],
        scratch=[pltpu.VMEM(own_rates.shape, f32), pltpu.SemaphoreType.DMA],
        flops=COPIES_COST,
    )
    decays = to_chunks(all_to_all(copies, members)).reshape(chunks * order, LANES)

    whole_chunk = own_rates.shape[1] == LANES
    unused = jnp.zeros((order, LANES), f32)
    series, ends = call(
        functools.partial(state_kernel, places, order),
        (
            jax.ShapeDtypeStruct((length * chunks, LANES), f32),
            jax.ShapeDtypeStruct((chunks * 2 * order, LANES), f32),
        ),
        decays,
        own_rates if whole_chunk else unused,
        own_residues if whole_chunk else unused,
        k_proj,
        value_projection,
        flops=2 * order * channels * length,
    )
    local_series, ends = lax.optimization_barrier((series, ends))
    ends = from_chunks(ends.reshape(chunks, 2 * order, LANES), blocks)
    if not whole_chunk:
        ends = ends.at[:, order:].set(weights_of(own_residues, own_rates))
    ends = all_to_all(ends, members)
    weights = to_chunks(ends).reshape(chunks * 2 * order, LANES)
    out_shape = jax.ShapeDtypeStruct((channels, length), jnp.bfloat16)
    out_scratch = [pltpu.VMEM(out_shape.shape, out_shape.dtype), pltpu.SemaphoreType.DMA((chunks,))]
    local, out = call(
        functools.partial(local_kernel, places, order),
        (
            jax.ShapeDtypeStruct((length * chunks, LANES), f32),
            out_shape,
        ),
        decays,
        weights,
        local_series,
        direct_gain.reshape(chunks, LANES),
        q_proj,
        out_spaces=(pltpu.VMEM, pl.ANY),
        scratch=out_scratch,
        flops=4 * order * channels * length,
    )
    starts = call(
        functools.partial(prefix_kernel, length, members),
        jax.ShapeDtypeStruct((blocks,) + own_rates.shape, f32),
        own_rates,
        ends,
    )
    starts = all_to_all(starts, members)
    carry = to_chunks(starts).reshape(chunks * order, LANES)
    return call(
        functools.partial(output_kernel, places, order),
        out_shape,
        decays,
        weights,
        carry,
        local,
        q_proj,
        out,
        out_spaces=pl.ANY,
        aliases={5: 0},
        scratch=[pltpu.VMEM((length * chunks, LANES), f32)] + out_scratch,
        flops=2 * order * channels * length,
    )


def solution(mesh):
    return jax.shard_map(
        functools.partial(shards, mesh.shape["seq"]),
        mesh=mesh,
        in_specs=(
            P("chan", ("groups", "seq")),
            P("chan", ("groups", "seq")),
            P("chan", ("groups", "seq")),
            P(("chan", "seq"), None),
            P(("chan", "seq"), None),
            P("chan"),
        ),
        out_specs=P("chan", ("groups", "seq")),
        check_vma=False,
    )
```

```python
import functools
import jax
import jax.numpy as jnp
from jax import lax
from jax.experimental import pallas as pl
from jax.experimental.pallas import tpu as pltpu
from jax.sharding import PartitionSpec as P

LANES = 128
SUBLANES = 8
COPIES_COST = 10**10
VMEM_LIMIT = 32 * 1024 * 1024


def copies_kernel(rate_hbm, copies_ref, rate_ref, sem):
    load = pltpu.make_async_copy(rate_hbm, rate_ref, sem)
    load.start()
    load.wait()
    decay = jnp.exp(-rate_ref[...])
    for piece in range(copies_ref.shape[0]):
        copies_ref[piece] = decay


def token_rows(half, length, token):
    row = (half * length + token) * SUBLANES
    return pl.ds(row if isinstance(row, int) else pl.multiple_of(row, SUBLANES), SUBLANES)


def chunk_rows(chunk, length):
    return pl.ds(chunk // SUBLANES * length * SUBLANES + chunk % SUBLANES, length, stride=SUBLANES)


def mode_rows(ref, base, order, per_chunk, chunks, half):
    first = half * SUBLANES * per_chunk + base
    return [ref[pl.ds(first + r, SUBLANES, stride=per_chunk), :] for r in range(order)]


def one_minus_exp(y):
    series = jnp.ones_like(y)
    for k in range(11, 1, -1):
        series = 1.0 - (y * (1.0 / k)) * series
    return jnp.where(y < 0.5, y * series, 1.0 - jnp.exp(-y))


def weights_of(residue, rate):
    return residue * jnp.sqrt(one_minus_exp(2.0 * rate))


def state_kernel(places, order, decays_ref, rate_ref, residue_ref, k_ref, v_ref, series_ref, state_ref):
    chunks, length = len(places), k_ref.shape[1]
    tokens = length // SUBLANES
    halves = chunks // SUBLANES

    def build(chunk):
        rows = pl.ds(places[chunk] * LANES, LANES)
        gated = k_ref[rows, :].astype(jnp.float32) * v_ref[rows, :].astype(jnp.float32)
        series_ref[chunk_rows(chunk, length), :] = gated.T

    weight = weights_of(residue_ref[...], rate_ref[...])
    for chunk in range(chunks):
        state_ref[pl.ds((2 * chunk + 1) * order, order), :] = weight
    for chunk in range(SUBLANES):
        build(chunk)
    for half in range(halves):
        decay = mode_rows(decays_ref, 0, order, order, chunks, half)

        def steps(i, state):
            state = list(state)
            for u in range(tokens):
                x = series_ref[token_rows(half, length, i * tokens + u), :]
                for r in range(order):
                    state[r] = decay[r] * state[r] + x
            return tuple(state)

        state = (jnp.zeros((SUBLANES, LANES), jnp.float32),) * order
        if half + 1 < halves:
            for i in range(SUBLANES):
                state = steps(i, state)
                build((half + 1) * SUBLANES + i)
        else:
            state = lax.fori_loop(0, SUBLANES, steps, state)
        for r in range(order):
            state_ref[pl.ds(half * SUBLANES * 2 * order + r, SUBLANES, stride=2 * order), :] = state[r]


def tree_sum(terms):
    terms = list(terms)
    while len(terms) > 1:
        terms = [terms[i] + terms[i + 1] if i + 1 < len(terms) else terms[i] for i in range(0, len(terms), 2)]
    return terms[0]


def leaving(chunk, places, gated_ref, out_ref, sems):
    rows = pl.ds(places[chunk] * LANES, LANES)
    return pltpu.make_async_copy(gated_ref.at[rows, :], out_ref.at[rows, :], sems.at[chunk])


def finish(chunk, places, conv_ref, q_ref, gated_ref, out_ref, sems):
    length = conv_ref.shape[0] // len(places)
    rows = pl.ds(places[chunk] * LANES, LANES)
    conv = conv_ref[chunk_rows(chunk, length), :].T
    gated_ref[rows, :] = (q_ref[rows, :].astype(jnp.float32) * conv).astype(jnp.bfloat16)
    leaving(chunk, places, gated_ref, out_ref, sems).start()


def convolve(halves, places, order, carry_ref, decays_ref, weights_ref, series_ref, gain_ref, q_ref, out):
    out_ref, conv_ref, gated_ref, sems = out
    chunks = len(places)
    length = series_ref.shape[0] // chunks
    tokens = length // SUBLANES
    todo = []
    for half in halves:
        decay = mode_rows(decays_ref, 0, order, order, chunks, half)
        weight = mode_rows(weights_ref, order, order, 2 * order, chunks, half)
        own = places[half * SUBLANES : (half + 1) * SUBLANES]
        gain = jnp.concatenate([gain_ref[pl.ds(place, 1), :] for place in own], axis=0)

        def steps(i, state):
            state = list(state)
            for u in range(tokens):
                rows = token_rows(half, length, i * tokens + u)
                x = series_ref[rows, :]
                for r in range(order):
                    state[r] = decay[r] * state[r] + x
                conv_ref[rows, :] = tree_sum([weight[r] * state[r] for r in range(order)] + [gain * x])
            return tuple(state)

        if carry_ref is None:
            state = (jnp.zeros((SUBLANES, LANES), jnp.float32),) * order
        else:
            state = tuple(mode_rows(carry_ref, 0, order, order, chunks, half))
        if todo:
            for i, chunk in enumerate(todo):
                state = steps(i, state)
                finish(chunk, places, conv_ref, q_ref, gated_ref, out_ref, sems)
        else:
            lax.fori_loop(0, SUBLANES, steps, state)
        todo = range(half * SUBLANES, (half + 1) * SUBLANES)
    for chunk in todo:
        finish(chunk, places, conv_ref, q_ref, gated_ref, out_ref, sems)
    for half in halves:
        for chunk in range(half * SUBLANES, (half + 1) * SUBLANES):
            leaving(chunk, places, gated_ref, out_ref, sems).wait()


def prefix_kernel(
    members, places, order, rate_ref, ends_ref, decays_ref, weights_ref, series_ref, gain_ref, q_ref,
    starts_ref, out_ref, *scratch
):
    length = series_ref.shape[0] // len(places)
    span_decay = jnp.exp(-float(length) * rate_ref[...])
    carry = jnp.zeros(rate_ref.shape, jnp.float32)
    for block in range(len(members)):
        starts_ref[members.index(block)] = carry
        carry = span_decay * carry + ends_ref[members.index(block), : rate_ref.shape[0]]

    @pl.when(lax.axis_index("seq") == 0)
    def _():
        halves = range(len(places) // SUBLANES // 2)
        refs = (decays_ref, weights_ref, series_ref, gain_ref, q_ref, (out_ref,) + scratch)
        convolve(halves, places, order, None, *refs)


def output_kernel(
    places, order, carry_ref, decays_ref, weights_ref, series_ref, gain_ref, q_ref, _, out_ref, *scratch
):
    halves = len(places) // SUBLANES
    refs = (carry_ref, decays_ref, weights_ref, series_ref, gain_ref, q_ref, (out_ref,) + scratch)

    @pl.when(lax.axis_index("seq") == 0)
    def _():
        convolve(range(halves // 2, halves), places, order, *refs)

    @pl.when(lax.axis_index("seq") > 0)
    def _():
        convolve(range(halves), places, order, *refs)


def call(kernel, out_shape, *args, in_spaces=None, out_spaces=None, aliases=None, scratch=(), flops=0):
    in_bytes = sum(a.size * a.dtype.itemsize for a in args)
    in_spaces = in_spaces or [pl.ANY if i in (aliases or {}) else pltpu.VMEM for i in range(len(args))]
    out_spaces = out_spaces or jax.tree.map(lambda _: pltpu.VMEM, out_shape)
    return pl.pallas_call(
        kernel,
        out_shape=out_shape,
        in_specs=[pl.BlockSpec(memory_space=space) for space in in_spaces],
        out_specs=jax.tree.map(lambda space: pl.BlockSpec(memory_space=space), out_spaces),
        scratch_shapes=list(scratch),
        input_output_aliases=aliases or {},
        compiler_params=pltpu.CompilerParams(vmem_limit_bytes=VMEM_LIMIT),
        cost_estimate=pl.CostEstimate(flops=flops, bytes_accessed=in_bytes, transcendentals=0),
    )(*args)


def to_chunks(pieces):
    owners, rows, own = pieces.shape
    if own == LANES:
        return pieces
    if own < LANES:
        group = LANES // own
        return pieces.reshape(owners // group, group, rows, own).swapaxes(1, 2).reshape(-1, rows, LANES)
    return pieces.reshape(owners, rows, own // LANES, LANES).swapaxes(1, 2).reshape(-1, rows, LANES)


def from_chunks(pieces, owners):
    chunks, rows, _ = pieces.shape
    own = chunks * LANES // owners
    if own == LANES:
        return pieces
    if own < LANES:
        group = LANES // own
        return pieces.reshape(chunks, rows, group, own).swapaxes(1, 2).reshape(owners, rows, own)
    return pieces.reshape(owners, own // LANES, rows, LANES).swapaxes(1, 2).reshape(owners, rows, own)


def all_to_all(pieces, members):
    return lax.all_to_all(pieces, "seq", split_axis=0, concat_axis=0, axis_index_groups=[members], tiled=True)


def shards(blocks, q_proj, k_proj, value_projection, residues, rates, direct_gain):
    channels, length = q_proj.shape
    order = residues.shape[1]
    chunks = channels // LANES
    f32 = jnp.float32

    members, places = list(range(blocks)), list(range(chunks))
    if blocks == chunks:
        members, places = members[::-1], places[::-1]

    own_rates, own_residues = rates.T, residues.T
    copies = call(
        copies_kernel,
        jax.ShapeDtypeStruct((blocks,) + own_rates.shape, f32),
        pltpu.with_memory_space_constraint(own_rates, pltpu.HBM),
        in_spaces=[pl.ANY],
        scratch=[pltpu.VMEM(own_rates.shape, f32), pltpu.SemaphoreType.DMA],
        flops=COPIES_COST,
    )
    decays = to_chunks(all_to_all(copies, members)).reshape(chunks * order, LANES)

    whole_chunk = own_rates.shape[1] == LANES
    unused = jnp.zeros((order, LANES), f32)
    series, ends = call(
        functools.partial(state_kernel, places, order),
        (
            jax.ShapeDtypeStruct((length * chunks, LANES), f32),
            jax.ShapeDtypeStruct((chunks * 2 * order, LANES), f32),
        ),
        decays,
        own_rates if whole_chunk else unused,
        own_residues if whole_chunk else unused,
        k_proj,
        value_projection,
        flops=2 * order * channels * length,
    )
    ends = from_chunks(ends.reshape(chunks, 2 * order, LANES), blocks)
    if not whole_chunk:
        ends = ends.at[:, order:].set(weights_of(own_residues, own_rates))
    ends = all_to_all(ends, members)
    weights = to_chunks(ends).reshape(chunks * 2 * order, LANES)

    operands = (decays, weights, series, direct_gain.reshape(chunks, LANES), q_proj)
    out_shape = jax.ShapeDtypeStruct((channels, length), jnp.bfloat16)
    scratch = [
        pltpu.VMEM((length * chunks, LANES), f32),
        pltpu.VMEM(out_shape.shape, out_shape.dtype),
        pltpu.SemaphoreType.DMA((chunks,)),
    ]
    starts, out = call(
        functools.partial(prefix_kernel, members, places, order),
        (jax.ShapeDtypeStruct((blocks,) + own_rates.shape, f32), out_shape),
        own_rates,
        ends,
        *operands,
        out_spaces=(pltpu.VMEM, pl.ANY),
        scratch=scratch,
    )
    carry = to_chunks(all_to_all(starts, members)).reshape(chunks * order, LANES)
    return call(
        functools.partial(output_kernel, places, order),
        out_shape,
        carry,
        *operands,
        out,
        out_spaces=pl.ANY,
        aliases={1 + len(operands): 0},
        scratch=scratch,
        flops=4 * order * channels * length,
    )


def solution(mesh):
    return jax.shard_map(
        functools.partial(shards, mesh.shape["seq"]),
        mesh=mesh,
        in_specs=(
            P("chan", ("groups", "seq")),
            P("chan", ("groups", "seq")),
            P("chan", ("groups", "seq")),
            P(("chan", "seq"), None),
            P(("chan", "seq"), None),
            P("chan"),
        ),
        out_specs=P("chan", ("groups", "seq")),
        check_vma=False,
    )
```

```python
import functools
import jax
import jax.numpy as jnp
from jax import lax
from jax.experimental import pallas as pl
from jax.experimental.pallas import tpu as pltpu
from jax.sharding import PartitionSpec as P

LANES = 128
SUBLANES = 8
UNROLL = 8
COPIES_COST = 10**10
VMEM_LIMIT = 32 * 1024 * 1024


def copies_kernel(rate_hbm, copies_ref, rate_ref, sem):
    load = pltpu.make_async_copy(rate_hbm, rate_ref, sem)
    load.start()
    load.wait()
    decay = jnp.exp(-rate_ref[...])
    for piece in range(copies_ref.shape[0]):
        copies_ref[piece] = decay


def token_rows(half, length, token):
    row = (half * length + token) * SUBLANES
    return pl.ds(row if isinstance(row, int) else pl.multiple_of(row, SUBLANES), SUBLANES)


def chunk_rows(chunk, length):
    return pl.ds(chunk // SUBLANES * length * SUBLANES + chunk % SUBLANES, length, stride=SUBLANES)


def mode_rows(ref, base, order, per_chunk, chunks, half):
    first = half * SUBLANES * per_chunk + base
    return [ref[pl.ds(first + r, SUBLANES, stride=per_chunk), :] for r in range(order)]


def one_minus_exp(y):
    series = jnp.ones_like(y)
    for k in range(11, 1, -1):
        series = 1.0 - (y * (1.0 / k)) * series
    return jnp.where(y < 0.5, y * series, 1.0 - jnp.exp(-y))


def weights_of(residue, rate):
    return residue * jnp.sqrt(one_minus_exp(2.0 * rate))


def state_kernel(places, order, decays_ref, rate_ref, residue_ref, k_ref, v_ref, series_ref, state_ref):
    chunks, length = len(places), k_ref.shape[1]
    tokens = length // SUBLANES
    halves = chunks // SUBLANES

    def build(chunk):
        rows = pl.ds(places[chunk] * LANES, LANES)
        gated = k_ref[rows, :].astype(jnp.float32) * v_ref[rows, :].astype(jnp.float32)
        series_ref[chunk_rows(chunk, length), :] = gated.T

    weight = weights_of(residue_ref[...], rate_ref[...])
    for chunk in range(chunks):
        state_ref[pl.ds((2 * chunk + 1) * order, order), :] = weight
    for chunk in range(SUBLANES):
        build(chunk)
    for half in range(halves):
        decay = mode_rows(decays_ref, 0, order, order, chunks, half)

        def steps(i, state):
            state = list(state)
            for u in range(tokens):
                x = series_ref[token_rows(half, length, i * tokens + u), :]
                for r in range(order):
                    state[r] = decay[r] * state[r] + x
            return tuple(state)

        state = (jnp.zeros((SUBLANES, LANES), jnp.float32),) * order
        if half + 1 < halves:
            for i in range(SUBLANES):
                state = steps(i, state)
                build((half + 1) * SUBLANES + i)
        else:
            state = lax.fori_loop(0, SUBLANES, steps, state)
        for r in range(order):
            state_ref[pl.ds(half * SUBLANES * 2 * order + r, SUBLANES, stride=2 * order), :] = state[r]


def prefix_kernel(length, members, rate_ref, ends_ref, starts_ref):
    span_decay = jnp.exp(-float(length) * rate_ref[...])
    carry = jnp.zeros(rate_ref.shape, jnp.float32)
    for block in range(len(members)):
        starts_ref[members.index(block)] = carry
        carry = span_decay * carry + ends_ref[members.index(block), : rate_ref.shape[0]]


def tree_sum(terms):
    terms = list(terms)
    while len(terms) > 1:
        terms = [terms[i] + terms[i + 1] if i + 1 < len(terms) else terms[i] for i in range(0, len(terms), 2)]
    return terms[0]


def leaving(chunk, places, gated_ref, out_ref, sems):
    rows = pl.ds(places[chunk] * LANES, LANES)
    return pltpu.make_async_copy(gated_ref.at[rows, :], out_ref.at[rows, :], sems.at[chunk])


def finish(chunk, places, conv_ref, q_ref, gated_ref, out_ref, sems):
    length = conv_ref.shape[0] // len(places)
    rows = pl.ds(places[chunk] * LANES, LANES)
    conv = conv_ref[chunk_rows(chunk, length), :].T
    gated_ref[rows, :] = (q_ref[rows, :].astype(jnp.float32) * conv).astype(jnp.bfloat16)
    leaving(chunk, places, gated_ref, out_ref, sems).start()


def local_kernel(
    places, order, decays_ref, weights_ref, series_ref, gain_ref, q_ref, conv_ref, out_ref, gated_ref, sems
):
    chunks = len(places)
    length = series_ref.shape[0] // chunks
    for half in range(chunks // SUBLANES):
        decay = mode_rows(decays_ref, 0, order, order, chunks, half)
        weight = mode_rows(weights_ref, order, order, 2 * order, chunks, half)
        own = places[half * SUBLANES : (half + 1) * SUBLANES]
        gain = jnp.concatenate([gain_ref[pl.ds(place, 1), :] for place in own], axis=0)

        def steps(i, state):
            state = list(state)
            for u in range(UNROLL):
                rows = token_rows(half, length, i * UNROLL + u)
                x = series_ref[rows, :]
                for r in range(order):
                    state[r] = decay[r] * state[r] + x
                terms = [weight[r] * state[r] for r in range(order)]
                conv_ref[rows, :] = tree_sum(terms + [gain * x])
            return tuple(state)

        zero = jnp.zeros((SUBLANES, LANES), jnp.float32)
        lax.fori_loop(0, length // UNROLL, steps, (zero,) * order)

    @pl.when(lax.axis_index("seq") == 0)
    def _():
        for chunk in range(chunks):
            finish(chunk, places, conv_ref, q_ref, gated_ref, out_ref, sems)
        for chunk in range(chunks):
            leaving(chunk, places, gated_ref, out_ref, sems).wait()


def output_kernel(
    places, order, decays_ref, weights_ref, carry_ref, local_ref, q_ref, _, out_ref, conv_ref, gated_ref, sems
):
    chunks = len(places)
    length = local_ref.shape[0] // chunks
    tokens = length // SUBLANES

    @pl.when(lax.axis_index("seq") > 0)
    def _():
        for half in range(chunks // SUBLANES):
            decay = mode_rows(decays_ref, 0, order, order, chunks, half)
            weight = mode_rows(weights_ref, order, order, 2 * order, chunks, half)
            carry = mode_rows(carry_ref, 0, order, order, chunks, half)

            def steps(i, fading):
                fading = list(fading)
                for u in range(tokens):
                    rows = token_rows(half, length, i * tokens + u)
                    fading = [decay[r] * fading[r] for r in range(order)]
                    conv_ref[rows, :] = tree_sum(fading + [local_ref[rows, :]])
                return tuple(fading)

            fading = tuple(weight[r] * carry[r] for r in range(order))
            if half == 0:
                lax.fori_loop(0, SUBLANES, steps, fading)
            else:
                for i in range(SUBLANES):
                    fading = steps(i, fading)
                    finish((half - 1) * SUBLANES + i, places, conv_ref, q_ref, gated_ref, out_ref, sems)
        for chunk in range(chunks - SUBLANES, chunks):
            finish(chunk, places, conv_ref, q_ref, gated_ref, out_ref, sems)
        for chunk in range(chunks):
            leaving(chunk, places, gated_ref, out_ref, sems).wait()


def call(kernel, out_shape, *args, in_spaces=None, out_spaces=None, aliases=None, scratch=(), flops=0):
    in_bytes = sum(a.size * a.dtype.itemsize for a in args)
    in_spaces = in_spaces or [pl.ANY if i in (aliases or {}) else pltpu.VMEM for i in range(len(args))]
    out_spaces = out_spaces or jax.tree.map(lambda _: pltpu.VMEM, out_shape)
    return pl.pallas_call(
        kernel,
        out_shape=out_shape,
        in_specs=[pl.BlockSpec(memory_space=space) for space in in_spaces],
        out_specs=jax.tree.map(lambda space: pl.BlockSpec(memory_space=space), out_spaces),
        scratch_shapes=list(scratch),
        input_output_aliases=aliases or {},
        compiler_params=pltpu.CompilerParams(vmem_limit_bytes=VMEM_LIMIT),
        cost_estimate=pl.CostEstimate(flops=flops, bytes_accessed=in_bytes, transcendentals=0),
    )(*args)


def to_chunks(pieces):
    owners, rows, own = pieces.shape
    if own == LANES:
        return pieces
    if own < LANES:
        group = LANES // own
        return pieces.reshape(owners // group, group, rows, own).swapaxes(1, 2).reshape(-1, rows, LANES)
    return pieces.reshape(owners, rows, own // LANES, LANES).swapaxes(1, 2).reshape(-1, rows, LANES)


def from_chunks(pieces, owners):
    chunks, rows, _ = pieces.shape
    own = chunks * LANES // owners
    if own == LANES:
        return pieces
    if own < LANES:
        group = LANES // own
        return pieces.reshape(chunks, rows, group, own).swapaxes(1, 2).reshape(owners, rows, own)
    return pieces.reshape(owners, own // LANES, rows, LANES).swapaxes(1, 2).reshape(owners, rows, own)


def all_to_all(pieces, members):
    return lax.all_to_all(pieces, "seq", split_axis=0, concat_axis=0, axis_index_groups=[members], tiled=True)


def shards(blocks, q_proj, k_proj, value_projection, residues, rates, direct_gain):
    channels, length = q_proj.shape
    order = residues.shape[1]
    chunks = channels // LANES
    f32 = jnp.float32

    members, places = list(range(blocks)), list(range(chunks))
    if blocks == chunks:
        middle = blocks * 11 // 16
        members = [middle] + [block for block in members[::-1] if block != middle]
        places = list(members)

    own_rates, own_residues = rates.T, residues.T
    copies = call(
        copies_kernel,
        jax.ShapeDtypeStruct((blocks,) + own_rates.shape, f32),
        pltpu.with_memory_space_constraint(own_rates, pltpu.HBM),
        in_spaces=[pl.ANY],
        scratch=[pltpu.VMEM(own_rates.shape, f32), pltpu.SemaphoreType.DMA],
        flops=COPIES_COST,
    )
    decays = to_chunks(all_to_all(copies, members)).reshape(chunks * order, LANES)

    whole_chunk = own_rates.shape[1] == LANES
    unused = jnp.zeros((order, LANES), f32)
    series, ends = call(
        functools.partial(state_kernel, places, order),
        (
            jax.ShapeDtypeStruct((length * chunks, LANES), f32),
            jax.ShapeDtypeStruct((chunks * 2 * order, LANES), f32),
        ),
        decays,
        own_rates if whole_chunk else unused,
        own_residues if whole_chunk else unused,
        k_proj,
        value_projection,
        flops=2 * order * channels * length,
    )
    local_series, ends = lax.optimization_barrier((series, ends))
    ends = from_chunks(ends.reshape(chunks, 2 * order, LANES), blocks)
    if not whole_chunk:
        ends = ends.at[:, order:].set(weights_of(own_residues, own_rates))
    ends = all_to_all(ends, members)
    weights = to_chunks(ends).reshape(chunks * 2 * order, LANES)
    out_shape = jax.ShapeDtypeStruct((channels, length), jnp.bfloat16)
    out_scratch = [pltpu.VMEM(out_shape.shape, out_shape.dtype), pltpu.SemaphoreType.DMA((chunks,))]
    local, out = call(
        functools.partial(local_kernel, places, order),
        (
            jax.ShapeDtypeStruct((length * chunks, LANES), f32),
            out_shape,
        ),
        decays,
        weights,
        local_series,
        direct_gain.reshape(chunks, LANES),
        q_proj,
        out_spaces=(pltpu.VMEM, pl.ANY),
        scratch=out_scratch,
        flops=4 * order * channels * length,
    )
    starts = call(
        functools.partial(prefix_kernel, length, members),
        jax.ShapeDtypeStruct((blocks,) + own_rates.shape, f32),
        own_rates,
        ends,
    )
    starts = all_to_all(starts, members)
    carry = to_chunks(starts).reshape(chunks * order, LANES)
    return call(
        functools.partial(output_kernel, places, order),
        out_shape,
        decays,
        weights,
        carry,
        local,
        q_proj,
        out,
        out_spaces=pl.ANY,
        aliases={5: 0},
        scratch=[pltpu.VMEM((length * chunks, LANES), f32)] + out_scratch,
        flops=2 * order * channels * length,
    )


def solution(mesh):
    return jax.shard_map(
        functools.partial(shards, mesh.shape["seq"]),
        mesh=mesh,
        in_specs=(
            P("chan", ("groups", "seq")),
            P("chan", ("groups", "seq")),
            P("chan", ("groups", "seq")),
            P(("chan", "seq"), None),
            P(("chan", "seq"), None),
            P("chan"),
        ),
        out_specs=P("chan", ("groups", "seq")),
        check_vma=False,
    )
```

```python
import functools
import jax
import jax.numpy as jnp
from jax import lax
from jax.experimental import pallas as pl
from jax.experimental.pallas import tpu as pltpu
from jax.sharding import PartitionSpec as P

LANES = 128
SUBLANES = 8
UNROLL = 8
COPIES_COST = 10**10
VMEM_LIMIT = 32 * 1024 * 1024


def copies_kernel(rate_hbm, copies_ref, rate_ref, sem):
    load = pltpu.make_async_copy(rate_hbm, rate_ref, sem)
    load.start()
    load.wait()
    decay = jnp.exp(-rate_ref[...])
    for piece in range(copies_ref.shape[0]):
        copies_ref[piece] = decay


def token_rows(half, length, token):
    row = (half * length + token) * SUBLANES
    return pl.ds(row if isinstance(row, int) else pl.multiple_of(row, SUBLANES), SUBLANES)


def chunk_rows(chunk, length):
    return pl.ds(chunk // SUBLANES * length * SUBLANES + chunk % SUBLANES, length, stride=SUBLANES)


def mode_rows(ref, base, order, per_chunk, chunks, half):
    first = half * SUBLANES * per_chunk + base
    return [ref[pl.ds(first + r, SUBLANES, stride=per_chunk), :] for r in range(order)]


def one_minus_exp(y):
    series = jnp.ones_like(y)
    for k in range(11, 1, -1):
        series = 1.0 - (y * (1.0 / k)) * series
    return jnp.where(y < 0.5, y * series, 1.0 - jnp.exp(-y))


def weights_of(residue, rate):
    return residue * jnp.sqrt(one_minus_exp(2.0 * rate))


def state_kernel(places, order, decays_ref, rate_ref, residue_ref, k_ref, v_ref, series_ref, state_ref):
    chunks, length = len(places), k_ref.shape[1]
    tokens = length // SUBLANES
    halves = chunks // SUBLANES

    def build(chunk):
        rows = pl.ds(places[chunk] * LANES, LANES)
        gated = k_ref[rows, :].astype(jnp.float32) * v_ref[rows, :].astype(jnp.float32)
        series_ref[chunk_rows(chunk, length), :] = gated.T

    weight = weights_of(residue_ref[...], rate_ref[...])
    for chunk in range(chunks):
        state_ref[pl.ds((2 * chunk + 1) * order, order), :] = weight
    for chunk in range(SUBLANES):
        build(chunk)
    for half in range(halves):
        decay = mode_rows(decays_ref, 0, order, order, chunks, half)

        def steps(i, state):
            state = list(state)
            for u in range(tokens):
                x = series_ref[token_rows(half, length, i * tokens + u), :]
                for r in range(order):
                    state[r] = decay[r] * state[r] + x
            return tuple(state)

        state = (jnp.zeros((SUBLANES, LANES), jnp.float32),) * order
        if half + 1 < halves:
            for i in range(SUBLANES):
                state = steps(i, state)
                build((half + 1) * SUBLANES + i)
        else:
            state = lax.fori_loop(0, SUBLANES, steps, state)
        for r in range(order):
            state_ref[pl.ds(half * SUBLANES * 2 * order + r, SUBLANES, stride=2 * order), :] = state[r]


def prefix_kernel(length, members, rate_ref, ends_ref, starts_ref):
    span_decay = jnp.exp(-float(length) * rate_ref[...])
    carry = jnp.zeros(rate_ref.shape, jnp.float32)
    for block in range(len(members)):
        starts_ref[members.index(block)] = carry
        carry = span_decay * carry + ends_ref[members.index(block), : rate_ref.shape[0]]


def tree_sum(terms):
    terms = list(terms)
    while len(terms) > 1:
        terms = [terms[i] + terms[i + 1] if i + 1 < len(terms) else terms[i] for i in range(0, len(terms), 2)]
    return terms[0]


def leaving(chunk, places, gated_ref, out_ref, sems):
    rows = pl.ds(places[chunk] * LANES, LANES)
    return pltpu.make_async_copy(gated_ref.at[rows, :], out_ref.at[rows, :], sems.at[chunk])


def finish(chunk, places, conv_ref, q_ref, gated_ref, out_ref, sems):
    length = conv_ref.shape[0] // len(places)
    rows = pl.ds(places[chunk] * LANES, LANES)
    conv = conv_ref[chunk_rows(chunk, length), :].T
    gated_ref[rows, :] = (q_ref[rows, :].astype(jnp.float32) * conv).astype(jnp.bfloat16)
    leaving(chunk, places, gated_ref, out_ref, sems).start()


def local_kernel(
    places, order, decays_ref, weights_ref, series_ref, gain_ref, q_ref, conv_ref, out_ref, gated_ref, sems
):
    chunks = len(places)
    length = series_ref.shape[0] // chunks
    for half in range(chunks // SUBLANES):
        decay = mode_rows(decays_ref, 0, order, order, chunks, half)
        weight = mode_rows(weights_ref, order, order, 2 * order, chunks, half)
        own = places[half * SUBLANES : (half + 1) * SUBLANES]
        gain = jnp.concatenate([gain_ref[pl.ds(place, 1), :] for place in own], axis=0)

        def steps(i, state):
            state = list(state)
            for u in range(UNROLL):
                rows = token_rows(half, length, i * UNROLL + u)
                x = series_ref[rows, :]
                for r in range(order):
                    state[r] = decay[r] * state[r] + x
                terms = [weight[r] * state[r] for r in range(order)]
                conv_ref[rows, :] = tree_sum(terms + [gain * x])
            return tuple(state)

        zero = jnp.zeros((SUBLANES, LANES), jnp.float32)
        lax.fori_loop(0, length // UNROLL, steps, (zero,) * order)

    @pl.when(lax.axis_index("seq") == 0)
    def _():
        for chunk in range(chunks):
            finish(chunk, places, conv_ref, q_ref, gated_ref, out_ref, sems)
        for chunk in range(chunks):
            leaving(chunk, places, gated_ref, out_ref, sems).wait()


def output_kernel(
    places, order, decays_ref, weights_ref, carry_ref, local_ref, q_ref, _, out_ref, conv_ref, gated_ref, sems
):
    chunks = len(places)
    length = local_ref.shape[0] // chunks
    tokens = length // SUBLANES

    @pl.when(lax.axis_index("seq") > 0)
    def _():
        for half in range(chunks // SUBLANES):
            decay = mode_rows(decays_ref, 0, order, order, chunks, half)
            weight = mode_rows(weights_ref, order, order, 2 * order, chunks, half)
            carry = mode_rows(carry_ref, 0, order, order, chunks, half)

            def steps(i, fading):
                fading = list(fading)
                for u in range(tokens):
                    rows = token_rows(half, length, i * tokens + u)
                    fading = [decay[r] * fading[r] for r in range(order)]
                    conv_ref[rows, :] = tree_sum(fading + [local_ref[rows, :]])
                return tuple(fading)

            fading = tuple(weight[r] * carry[r] for r in range(order))
            if half == 0:
                lax.fori_loop(0, SUBLANES, steps, fading)
            else:
                for i in range(SUBLANES):
                    fading = steps(i, fading)
                    finish((half - 1) * SUBLANES + i, places, conv_ref, q_ref, gated_ref, out_ref, sems)
        for chunk in range(chunks - SUBLANES, chunks):
            finish(chunk, places, conv_ref, q_ref, gated_ref, out_ref, sems)
        for chunk in range(chunks):
            leaving(chunk, places, gated_ref, out_ref, sems).wait()


def call(kernel, out_shape, *args, in_spaces=None, out_spaces=None, aliases=None, scratch=(), flops=0):
    in_bytes = sum(a.size * a.dtype.itemsize for a in args)
    in_spaces = in_spaces or [pl.ANY if i in (aliases or {}) else pltpu.VMEM for i in range(len(args))]
    out_spaces = out_spaces or jax.tree.map(lambda _: pltpu.VMEM, out_shape)
    return pl.pallas_call(
        kernel,
        out_shape=out_shape,
        in_specs=[pl.BlockSpec(memory_space=space) for space in in_spaces],
        out_specs=jax.tree.map(lambda space: pl.BlockSpec(memory_space=space), out_spaces),
        scratch_shapes=list(scratch),
        input_output_aliases=aliases or {},
        compiler_params=pltpu.CompilerParams(vmem_limit_bytes=VMEM_LIMIT),
        cost_estimate=pl.CostEstimate(flops=flops, bytes_accessed=in_bytes, transcendentals=0),
    )(*args)


def to_chunks(pieces):
    owners, rows, own = pieces.shape
    if own == LANES:
        return pieces
    if own < LANES:
        group = LANES // own
        return pieces.reshape(owners // group, group, rows, own).swapaxes(1, 2).reshape(-1, rows, LANES)
    return pieces.reshape(owners, rows, own // LANES, LANES).swapaxes(1, 2).reshape(-1, rows, LANES)


def from_chunks(pieces, owners):
    chunks, rows, _ = pieces.shape
    own = chunks * LANES // owners
    if own == LANES:
        return pieces
    if own < LANES:
        group = LANES // own
        return pieces.reshape(chunks, rows, group, own).swapaxes(1, 2).reshape(owners, rows, own)
    return pieces.reshape(owners, own // LANES, rows, LANES).swapaxes(1, 2).reshape(owners, rows, own)


def all_to_all(pieces, members):
    return lax.all_to_all(pieces, "seq", split_axis=0, concat_axis=0, axis_index_groups=[members], tiled=True)


def shards(blocks, q_proj, k_proj, value_projection, residues, rates, direct_gain):
    channels, length = q_proj.shape
    order = residues.shape[1]
    chunks = channels // LANES
    f32 = jnp.float32

    members, places = list(range(blocks)), list(range(chunks))
    if blocks == chunks:
        far, middle = blocks // 2, blocks * 11 // 16
        upper = [middle] + [block for block in members[:far - 1:-1] if block != middle]
        members = [block for one in upper for block in (one, one - far)]
        places = list(members)

    own_rates, own_residues = rates.T, residues.T
    copies = call(
        copies_kernel,
        jax.ShapeDtypeStruct((blocks,) + own_rates.shape, f32),
        pltpu.with_memory_space_constraint(own_rates, pltpu.HBM),
        in_spaces=[pl.ANY],
        scratch=[pltpu.VMEM(own_rates.shape, f32), pltpu.SemaphoreType.DMA],
        flops=COPIES_COST,
    )
    decays = to_chunks(all_to_all(copies, members)).reshape(chunks * order, LANES)

    whole_chunk = own_rates.shape[1] == LANES
    unused = jnp.zeros((order, LANES), f32)
    series, ends = call(
        functools.partial(state_kernel, places, order),
        (
            jax.ShapeDtypeStruct((length * chunks, LANES), f32),
            jax.ShapeDtypeStruct((chunks * 2 * order, LANES), f32),
        ),
        decays,
        own_rates if whole_chunk else unused,
        own_residues if whole_chunk else unused,
        k_proj,
        value_projection,
        flops=2 * order * channels * length,
    )
    local_series, ends = lax.optimization_barrier((series, ends))
    ends = from_chunks(ends.reshape(chunks, 2 * order, LANES), blocks)
    if not whole_chunk:
        ends = ends.at[:, order:].set(weights_of(own_residues, own_rates))
    ends = all_to_all(ends, members)
    weights = to_chunks(ends).reshape(chunks * 2 * order, LANES)
    out_shape = jax.ShapeDtypeStruct((channels, length), jnp.bfloat16)
    out_scratch = [pltpu.VMEM(out_shape.shape, out_shape.dtype), pltpu.SemaphoreType.DMA((chunks,))]
    local, out = call(
        functools.partial(local_kernel, places, order),
        (
            jax.ShapeDtypeStruct((length * chunks, LANES), f32),
            out_shape,
        ),
        decays,
        weights,
        local_series,
        direct_gain.reshape(chunks, LANES),
        q_proj,
        out_spaces=(pltpu.VMEM, pl.ANY),
        scratch=out_scratch,
        flops=4 * order * channels * length,
    )
    starts = call(
        functools.partial(prefix_kernel, length, members),
        jax.ShapeDtypeStruct((blocks,) + own_rates.shape, f32),
        own_rates,
        ends,
    )
    starts = all_to_all(starts, members)
    carry = to_chunks(starts).reshape(chunks * order, LANES)
    return call(
        functools.partial(output_kernel, places, order),
        out_shape,
        decays,
        weights,
        carry,
        local,
        q_proj,
        out,
        out_spaces=pl.ANY,
        aliases={5: 0},
        scratch=[pltpu.VMEM((length * chunks, LANES), f32)] + out_scratch,
        flops=2 * order * channels * length,
    )


def solution(mesh):
    return jax.shard_map(
        functools.partial(shards, mesh.shape["seq"]),
        mesh=mesh,
        in_specs=(
            P("chan", ("groups", "seq")),
            P("chan", ("groups", "seq")),
            P("chan", ("groups", "seq")),
            P(("chan", "seq"), None),
            P(("chan", "seq"), None),
            P("chan"),
        ),
        out_specs=P("chan", ("groups", "seq")),
        check_vma=False,
    )
```

```python
import functools
import jax
import jax.numpy as jnp
from jax import lax
from jax.experimental import pallas as pl
from jax.experimental.pallas import tpu as pltpu
from jax.sharding import PartitionSpec as P

LANES = 128
SUBLANES = 8
UNROLL = 8
COPIES_COST = 10**10
VMEM_LIMIT = 32 * 1024 * 1024


def copies_kernel(rate_hbm, copies_ref, rate_ref, sem):
    load = pltpu.make_async_copy(rate_hbm, rate_ref, sem)
    load.start()
    load.wait()
    decay = jnp.exp(-rate_ref[...])
    for piece in range(copies_ref.shape[0]):
        copies_ref[piece] = decay


def token_rows(half, length, token):
    row = (half * length + token) * SUBLANES
    return pl.ds(row if isinstance(row, int) else pl.multiple_of(row, SUBLANES), SUBLANES)


def chunk_rows(chunk, length):
    return pl.ds(chunk // SUBLANES * length * SUBLANES + chunk % SUBLANES, length, stride=SUBLANES)


def mode_rows(ref, base, order, per_chunk, chunks, half):
    first = half * SUBLANES * per_chunk + base
    return [ref[pl.ds(first + r, SUBLANES, stride=per_chunk), :] for r in range(order)]


def one_minus_exp(y):
    series = jnp.ones_like(y)
    for k in range(11, 1, -1):
        series = 1.0 - (y * (1.0 / k)) * series
    return jnp.where(y < 0.5, y * series, 1.0 - jnp.exp(-y))


def weights_of(residue, rate):
    return residue * jnp.sqrt(one_minus_exp(2.0 * rate))


def state_kernel(places, order, decays_ref, rate_ref, residue_ref, k_ref, v_ref, series_ref, state_ref):
    chunks, length = len(places), k_ref.shape[1]
    tokens = length // SUBLANES
    halves = chunks // SUBLANES

    def build(chunk):
        rows = pl.ds(places[chunk] * LANES, LANES)
        gated = k_ref[rows, :].astype(jnp.float32) * v_ref[rows, :].astype(jnp.float32)
        series_ref[chunk_rows(chunk, length), :] = gated.T

    weight = weights_of(residue_ref[...], rate_ref[...])
    for chunk in range(chunks):
        state_ref[pl.ds((2 * chunk + 1) * order, order), :] = weight
    for chunk in range(SUBLANES):
        build(chunk)
    for half in range(halves):
        decay = mode_rows(decays_ref, 0, order, order, chunks, half)

        def steps(i, state):
            state = list(state)
            for u in range(tokens):
                x = series_ref[token_rows(half, length, i * tokens + u), :]
                for r in range(order):
                    state[r] = decay[r] * state[r] + x
            return tuple(state)

        state = (jnp.zeros((SUBLANES, LANES), jnp.float32),) * order
        if half + 1 < halves:
            for i in range(SUBLANES):
                state = steps(i, state)
                build((half + 1) * SUBLANES + i)
        else:
            state = lax.fori_loop(0, SUBLANES, steps, state)
        for r in range(order):
            state_ref[pl.ds(half * SUBLANES * 2 * order + r, SUBLANES, stride=2 * order), :] = state[r]


def prefix_kernel(length, members, rate_ref, ends_ref, starts_ref):
    span_decay = jnp.exp(-float(length) * rate_ref[...])
    carry = jnp.zeros(rate_ref.shape, jnp.float32)
    for block in range(len(members)):
        starts_ref[members.index(block)] = carry
        carry = span_decay * carry + ends_ref[members.index(block), : rate_ref.shape[0]]


def tree_sum(terms):
    terms = list(terms)
    while len(terms) > 1:
        terms = [terms[i] + terms[i + 1] if i + 1 < len(terms) else terms[i] for i in range(0, len(terms), 2)]
    return terms[0]


def leaving(chunk, places, gated_ref, out_ref, sems):
    rows = pl.ds(places[chunk] * LANES, LANES)
    return pltpu.make_async_copy(gated_ref.at[rows, :], out_ref.at[rows, :], sems.at[chunk])


def finish(chunk, places, conv_ref, q_ref, gated_ref, out_ref, sems):
    length = conv_ref.shape[0] // len(places)
    rows = pl.ds(places[chunk] * LANES, LANES)
    conv = conv_ref[chunk_rows(chunk, length), :].T
    gated_ref[rows, :] = (q_ref[rows, :].astype(jnp.float32) * conv).astype(jnp.bfloat16)
    leaving(chunk, places, gated_ref, out_ref, sems).start()


def local_kernel(
    places, order, decays_ref, weights_ref, series_ref, gain_ref, q_ref, conv_ref, out_ref, gated_ref, sems
):
    chunks = len(places)
    length = series_ref.shape[0] // chunks
    for half in range(chunks // SUBLANES):
        decay = mode_rows(decays_ref, 0, order, order, chunks, half)
        weight = mode_rows(weights_ref, order, order, 2 * order, chunks, half)
        own = places[half * SUBLANES : (half + 1) * SUBLANES]
        gain = jnp.concatenate([gain_ref[pl.ds(place, 1), :] for place in own], axis=0)

        def steps(i, state):
            state = list(state)
            for u in range(UNROLL):
                rows = token_rows(half, length, i * UNROLL + u)
                x = series_ref[rows, :]
                for r in range(order):
                    state[r] = decay[r] * state[r] + x
                terms = [weight[r] * state[r] for r in range(order)]
                conv_ref[rows, :] = tree_sum(terms + [gain * x])
            return tuple(state)

        zero = jnp.zeros((SUBLANES, LANES), jnp.float32)
        lax.fori_loop(0, length // UNROLL, steps, (zero,) * order)

    @pl.when(lax.axis_index("seq") == 0)
    def _():
        for chunk in range(chunks):
            finish(chunk, places, conv_ref, q_ref, gated_ref, out_ref, sems)
        for chunk in range(chunks):
            leaving(chunk, places, gated_ref, out_ref, sems).wait()


def output_kernel(
    places, order, decays_ref, weights_ref, carry_ref, local_ref, q_ref, _, out_ref, conv_ref, gated_ref, sems
):
    chunks = len(places)
    length = local_ref.shape[0] // chunks
    tokens = length // SUBLANES

    @pl.when(lax.axis_index("seq") > 0)
    def _():
        for half in range(chunks // SUBLANES):
            decay = mode_rows(decays_ref, 0, order, order, chunks, half)
            weight = mode_rows(weights_ref, order, order, 2 * order, chunks, half)
            carry = mode_rows(carry_ref, 0, order, order, chunks, half)

            def steps(i, fading):
                fading = list(fading)
                for u in range(tokens):
                    rows = token_rows(half, length, i * tokens + u)
                    fading = [decay[r] * fading[r] for r in range(order)]
                    conv_ref[rows, :] = tree_sum(fading + [local_ref[rows, :]])
                return tuple(fading)

            fading = tuple(weight[r] * carry[r] for r in range(order))
            if half == 0:
                lax.fori_loop(0, SUBLANES, steps, fading)
            else:
                for i in range(SUBLANES):
                    fading = steps(i, fading)
                    finish((half - 1) * SUBLANES + i, places, conv_ref, q_ref, gated_ref, out_ref, sems)
        for chunk in range(chunks - SUBLANES, chunks):
            finish(chunk, places, conv_ref, q_ref, gated_ref, out_ref, sems)
        for chunk in range(chunks):
            leaving(chunk, places, gated_ref, out_ref, sems).wait()


def call(kernel, out_shape, *args, in_spaces=None, out_spaces=None, aliases=None, scratch=(), flops=0):
    in_bytes = sum(a.size * a.dtype.itemsize for a in args)
    in_spaces = in_spaces or [pl.ANY if i in (aliases or {}) else pltpu.VMEM for i in range(len(args))]
    out_spaces = out_spaces or jax.tree.map(lambda _: pltpu.VMEM, out_shape)
    return pl.pallas_call(
        kernel,
        out_shape=out_shape,
        in_specs=[pl.BlockSpec(memory_space=space) for space in in_spaces],
        out_specs=jax.tree.map(lambda space: pl.BlockSpec(memory_space=space), out_spaces),
        scratch_shapes=list(scratch),
        input_output_aliases=aliases or {},
        compiler_params=pltpu.CompilerParams(vmem_limit_bytes=VMEM_LIMIT),
        cost_estimate=pl.CostEstimate(flops=flops, bytes_accessed=in_bytes, transcendentals=0),
    )(*args)


def to_chunks(pieces):
    owners, rows, own = pieces.shape
    if own == LANES:
        return pieces
    if own < LANES:
        group = LANES // own
        return pieces.reshape(owners // group, group, rows, own).swapaxes(1, 2).reshape(-1, rows, LANES)
    return pieces.reshape(owners, rows, own // LANES, LANES).swapaxes(1, 2).reshape(-1, rows, LANES)


def from_chunks(pieces, owners):
    chunks, rows, _ = pieces.shape
    own = chunks * LANES // owners
    if own == LANES:
        return pieces
    if own < LANES:
        group = LANES // own
        return pieces.reshape(chunks, rows, group, own).swapaxes(1, 2).reshape(owners, rows, own)
    return pieces.reshape(owners, own // LANES, rows, LANES).swapaxes(1, 2).reshape(owners, rows, own)


def all_to_all(pieces, members):
    return lax.all_to_all(pieces, "seq", split_axis=0, concat_axis=0, axis_index_groups=[members], tiled=True)


def shards(blocks, q_proj, k_proj, value_projection, residues, rates, direct_gain):
    channels, length = q_proj.shape
    order = residues.shape[1]
    chunks = channels // LANES
    f32 = jnp.float32

    members, places = list(range(blocks)), list(range(chunks))
    if blocks == chunks and blocks % 4 == 0:
        quarter = blocks // 4
        members = [part * quarter + i for i in reversed(range(quarter)) for part in (2, 0, 3, 1)]
        places = list(members)

    own_rates, own_residues = rates.T, residues.T
    copies = call(
        copies_kernel,
        jax.ShapeDtypeStruct((blocks,) + own_rates.shape, f32),
        pltpu.with_memory_space_constraint(own_rates, pltpu.HBM),
        in_spaces=[pl.ANY],
        scratch=[pltpu.VMEM(own_rates.shape, f32), pltpu.SemaphoreType.DMA],
        flops=COPIES_COST,
    )
    decays = to_chunks(all_to_all(copies, members)).reshape(chunks * order, LANES)

    whole_chunk = own_rates.shape[1] == LANES
    unused = jnp.zeros((order, LANES), f32)
    series, ends = call(
        functools.partial(state_kernel, places, order),
        (
            jax.ShapeDtypeStruct((length * chunks, LANES), f32),
            jax.ShapeDtypeStruct((chunks * 2 * order, LANES), f32),
        ),
        decays,
        own_rates if whole_chunk else unused,
        own_residues if whole_chunk else unused,
        k_proj,
        value_projection,
        flops=2 * order * channels * length,
    )
    local_series, ends = lax.optimization_barrier((series, ends))
    ends = from_chunks(ends.reshape(chunks, 2 * order, LANES), blocks)
    if not whole_chunk:
        ends = ends.at[:, order:].set(weights_of(own_residues, own_rates))
    ends = all_to_all(ends, members)
    weights = to_chunks(ends).reshape(chunks * 2 * order, LANES)
    out_shape = jax.ShapeDtypeStruct((channels, length), jnp.bfloat16)
    out_scratch = [pltpu.VMEM(out_shape.shape, out_shape.dtype), pltpu.SemaphoreType.DMA((chunks,))]
    local, out = call(
        functools.partial(local_kernel, places, order),
        (
            jax.ShapeDtypeStruct((length * chunks, LANES), f32),
            out_shape,
        ),
        decays,
        weights,
        local_series,
        direct_gain.reshape(chunks, LANES),
        q_proj,
        out_spaces=(pltpu.VMEM, pl.ANY),
        scratch=out_scratch,
        flops=4 * order * channels * length,
    )
    starts = call(
        functools.partial(prefix_kernel, length, members),
        jax.ShapeDtypeStruct((blocks,) + own_rates.shape, f32),
        own_rates,
        ends,
    )
    starts = all_to_all(starts, members)
    carry = to_chunks(starts).reshape(chunks * order, LANES)
    return call(
        functools.partial(output_kernel, places, order),
        out_shape,
        decays,
        weights,
        carry,
        local,
        q_proj,
        out,
        out_spaces=pl.ANY,
        aliases={5: 0},
        scratch=[pltpu.VMEM((length * chunks, LANES), f32)] + out_scratch,
        flops=2 * order * channels * length,
    )


def solution(mesh):
    return jax.shard_map(
        functools.partial(shards, mesh.shape["seq"]),
        mesh=mesh,
        in_specs=(
            P("chan", ("groups", "seq")),
            P("chan", ("groups", "seq")),
            P("chan", ("groups", "seq")),
            P(("chan", "seq"), None),
            P(("chan", "seq"), None),
            P("chan"),
        ),
        out_specs=P("chan", ("groups", "seq")),
        check_vma=False,
    )
```

```python
import functools
import jax
import jax.numpy as jnp
from jax import lax
from jax.experimental import pallas as pl
from jax.experimental.pallas import tpu as pltpu
from jax.sharding import PartitionSpec as P

LANES = 128
SUBLANES = 8
UNROLL = 8
COPIES_COST = 10**10
VMEM_LIMIT = 32 * 1024 * 1024


def copies_kernel(rate_hbm, copies_ref, rate_ref, sem):
    load = pltpu.make_async_copy(rate_hbm, rate_ref, sem)
    load.start()
    load.wait()
    decay = jnp.exp(-rate_ref[...])
    for piece in range(copies_ref.shape[0]):
        copies_ref[piece] = decay


def token_rows(half, length, token):
    row = (half * length + token) * SUBLANES
    return pl.ds(row if isinstance(row, int) else pl.multiple_of(row, SUBLANES), SUBLANES)


def chunk_rows(chunk, length):
    return pl.ds(chunk // SUBLANES * length * SUBLANES + chunk % SUBLANES, length, stride=SUBLANES)


def mode_rows(ref, base, order, per_chunk, chunks, half):
    first = half * SUBLANES * per_chunk + base
    return [ref[pl.ds(first + r, SUBLANES, stride=per_chunk), :] for r in range(order)]


def one_minus_exp(y):
    series = jnp.ones_like(y)
    for k in range(11, 1, -1):
        series = 1.0 - (y * (1.0 / k)) * series
    return jnp.where(y < 0.5, y * series, 1.0 - jnp.exp(-y))


def weights_of(residue, rate):
    return residue * jnp.sqrt(one_minus_exp(2.0 * rate))


def state_kernel(places, order, decays_ref, rate_ref, residue_ref, k_ref, v_ref, series_ref, state_ref):
    chunks, length = len(places), k_ref.shape[1]
    tokens = length // SUBLANES
    halves = chunks // SUBLANES

    def build(chunk):
        rows = pl.ds(places[chunk] * LANES, LANES)
        gated = k_ref[rows, :].astype(jnp.float32) * v_ref[rows, :].astype(jnp.float32)
        series_ref[chunk_rows(chunk, length), :] = gated.T

    weight = weights_of(residue_ref[...], rate_ref[...])
    for chunk in range(chunks):
        state_ref[pl.ds((2 * chunk + 1) * order, order), :] = weight
    for chunk in range(SUBLANES):
        build(chunk)
    for half in range(halves):
        decay = mode_rows(decays_ref, 0, order, order, chunks, half)

        def steps(i, state):
            state = list(state)
            for u in range(tokens):
                x = series_ref[token_rows(half, length, i * tokens + u), :]
                for r in range(order):
                    state[r] = decay[r] * state[r] + x
            return tuple(state)

        state = (jnp.zeros((SUBLANES, LANES), jnp.float32),) * order
        if half + 1 < halves:
            for i in range(SUBLANES):
                state = steps(i, state)
                build((half + 1) * SUBLANES + i)
        else:
            state = lax.fori_loop(0, SUBLANES, steps, state)
        for r in range(order):
            state_ref[pl.ds(half * SUBLANES * 2 * order + r, SUBLANES, stride=2 * order), :] = state[r]


def prefix_kernel(length, members, rate_ref, ends_ref, starts_ref):
    span_decay = jnp.exp(-float(length) * rate_ref[...])
    carry = jnp.zeros(rate_ref.shape, jnp.float32)
    for block in range(len(members)):
        starts_ref[members.index(block)] = carry
        carry = span_decay * carry + ends_ref[members.index(block), : rate_ref.shape[0]]


def tree_sum(terms):
    terms = list(terms)
    while len(terms) > 1:
        terms = [terms[i] + terms[i + 1] if i + 1 < len(terms) else terms[i] for i in range(0, len(terms), 2)]
    return terms[0]


def leaving(chunk, places, gated_ref, out_ref, sems):
    rows = pl.ds(places[chunk] * LANES, LANES)
    return pltpu.make_async_copy(gated_ref.at[rows, :], out_ref.at[rows, :], sems.at[chunk])


def finish(chunk, places, conv, q_ref, gated_ref, out_ref, sems):
    rows = pl.ds(places[chunk] * LANES, LANES)
    gated_ref[rows, :] = (q_ref[rows, :].astype(jnp.float32) * conv.T).astype(jnp.bfloat16)
    leaving(chunk, places, gated_ref, out_ref, sems).start()


def power(base, exponent):
    result = None
    while exponent > 0:
        if exponent % 2 == 1:
            result = base if result is None else result * base
        base = base * base
        exponent //= 2
    return result


def local_kernel(
    places, order, decays_ref, weights_ref, series_ref, gain_ref, q_ref, conv_ref, factors_ref, out_ref, gated_ref, sems
):
    chunks = len(places)
    length = series_ref.shape[0] // chunks
    for half in range(chunks // SUBLANES):
        decay = mode_rows(decays_ref, 0, order, order, chunks, half)
        weight = mode_rows(weights_ref, order, order, 2 * order, chunks, half)
        own = places[half * SUBLANES : (half + 1) * SUBLANES]
        gain = jnp.concatenate([gain_ref[pl.ds(place, 1), :] for place in own], axis=0)

        def steps(i, state):
            state = list(state)
            for u in range(UNROLL):
                rows = token_rows(half, length, i * UNROLL + u)
                x = series_ref[rows, :]
                for r in range(order):
                    state[r] = decay[r] * state[r] + x
                terms = [weight[r] * state[r] for r in range(order)]
                conv_ref[rows, :] = tree_sum(terms + [gain * x])
            return tuple(state)

        zero = jnp.zeros((SUBLANES, LANES), jnp.float32)
        lax.fori_loop(0, length // UNROLL, steps, (zero,) * order)

    first = lax.axis_index("seq") == 0

    @pl.when(first)
    def _():
        for chunk in range(chunks):
            finish(chunk, places, conv_ref[chunk_rows(chunk, length), :], q_ref, gated_ref, out_ref, sems)
        for chunk in range(chunks):
            leaving(chunk, places, gated_ref, out_ref, sems).wait()

    @pl.when(jnp.logical_not(first))
    def _():
        stretch = length // SUBLANES
        index = lax.broadcasted_iota(jnp.int32, (SUBLANES, LANES), 0)

        def one_row(row, _):
            decay = jnp.broadcast_to(decays_ref[pl.ds(row, 1), :], (SUBLANES, LANES))
            chunk = row // order
            weight = weights_ref[pl.ds(chunk * 2 * order + order + row - chunk * order, 1), :]
            factor = decay * weight
            step = power(decay, stretch)
            for bit in range(3):
                factor = jnp.where(index & (1 << bit) != 0, factor * step, factor)
                step = step * step
            factors_ref[pl.ds(pl.multiple_of(row * SUBLANES, SUBLANES), SUBLANES), :] = factor
            return 0

        lax.fori_loop(0, chunks * order, one_row, 0, unroll=8)


def output_kernel(
    places, order, decays_ref, factors_ref, carry_ref, local_ref, q_ref, _, out_ref, conv_ref, gated_ref, sems
):
    chunks = len(places)
    length = local_ref.shape[0] // chunks
    stretch = length // SUBLANES

    def scan(chunk):
        rows = [chunk * order + r for r in range(order)]
        decay = [jnp.broadcast_to(decays_ref[pl.ds(row, 1), :], (SUBLANES, LANES)) for row in rows]
        fading = [factors_ref[pl.ds(row * SUBLANES, SUBLANES), :] * carry_ref[pl.ds(row, 1), :] for row in rows]
        first = chunk // SUBLANES * length * SUBLANES + chunk % SUBLANES
        for i in range(stretch):
            local = local_ref[pl.ds(first + i * SUBLANES, SUBLANES, stride=stretch * SUBLANES), :]
            conv_ref[pl.ds(chunk * length + i * SUBLANES, SUBLANES), :] = tree_sum(fading + [local])
            if i + 1 < stretch:
                fading = [decay[r] * fading[r] for r in range(order)]

    def send(chunk):
        parts = [conv_ref[pl.ds(chunk * length + i, stretch, stride=SUBLANES), :] for i in range(SUBLANES)]
        finish(chunk, places, jnp.concatenate(parts, axis=0), q_ref, gated_ref, out_ref, sems)

    @pl.when(lax.axis_index("seq") > 0)
    def _():
        for chunk in range(chunks):
            scan(chunk)
            if chunk > 0:
                send(chunk - 1)
        send(chunks - 1)
        for chunk in range(chunks):
            leaving(chunk, places, gated_ref, out_ref, sems).wait()


def call(kernel, out_shape, *args, in_spaces=None, out_spaces=None, aliases=None, scratch=(), flops=0):
    in_bytes = sum(a.size * a.dtype.itemsize for a in args)
    in_spaces = in_spaces or [pl.ANY if i in (aliases or {}) else pltpu.VMEM for i in range(len(args))]
    out_spaces = out_spaces or jax.tree.map(lambda _: pltpu.VMEM, out_shape)
    return pl.pallas_call(
        kernel,
        out_shape=out_shape,
        in_specs=[pl.BlockSpec(memory_space=space) for space in in_spaces],
        out_specs=jax.tree.map(lambda space: pl.BlockSpec(memory_space=space), out_spaces),
        scratch_shapes=list(scratch),
        input_output_aliases=aliases or {},
        compiler_params=pltpu.CompilerParams(vmem_limit_bytes=VMEM_LIMIT),
        cost_estimate=pl.CostEstimate(flops=flops, bytes_accessed=in_bytes, transcendentals=0),
    )(*args)


def to_chunks(pieces):
    owners, rows, own = pieces.shape
    if own == LANES:
        return pieces
    if own < LANES:
        group = LANES // own
        return pieces.reshape(owners // group, group, rows, own).swapaxes(1, 2).reshape(-1, rows, LANES)
    return pieces.reshape(owners, rows, own // LANES, LANES).swapaxes(1, 2).reshape(-1, rows, LANES)


def from_chunks(pieces, owners):
    chunks, rows, _ = pieces.shape
    own = chunks * LANES // owners
    if own == LANES:
        return pieces
    if own < LANES:
        group = LANES // own
        return pieces.reshape(chunks, rows, group, own).swapaxes(1, 2).reshape(owners, rows, own)
    return pieces.reshape(owners, own // LANES, rows, LANES).swapaxes(1, 2).reshape(owners, rows, own)


def all_to_all(pieces, members):
    return lax.all_to_all(pieces, "seq", split_axis=0, concat_axis=0, axis_index_groups=[members], tiled=True)


def shards(blocks, q_proj, k_proj, value_projection, residues, rates, direct_gain):
    channels, length = q_proj.shape
    order = residues.shape[1]
    chunks = channels // LANES
    f32 = jnp.float32

    members, places = list(range(blocks)), list(range(chunks))
    if blocks == chunks:
        far, middle = blocks // 2, blocks * 11 // 16
        upper = [middle] + [block for block in members[:far - 1:-1] if block != middle]
        members = [block for one in upper for block in (one, one - far)]
        places = list(members)

    own_rates, own_residues = rates.T, residues.T
    copies = call(
        copies_kernel,
        jax.ShapeDtypeStruct((blocks,) + own_rates.shape, f32),
        pltpu.with_memory_space_constraint(own_rates, pltpu.HBM),
        in_spaces=[pl.ANY],
        scratch=[pltpu.VMEM(own_rates.shape, f32), pltpu.SemaphoreType.DMA],
        flops=COPIES_COST,
    )
    decays = to_chunks(all_to_all(copies, members)).reshape(chunks * order, LANES)

    whole_chunk = own_rates.shape[1] == LANES
    unused = jnp.zeros((order, LANES), f32)
    series, ends = call(
        functools.partial(state_kernel, places, order),
        (
            jax.ShapeDtypeStruct((length * chunks, LANES), f32),
            jax.ShapeDtypeStruct((chunks * 2 * order, LANES), f32),
        ),
        decays,
        own_rates if whole_chunk else unused,
        own_residues if whole_chunk else unused,
        k_proj,
        value_projection,
        flops=2 * order * channels * length,
    )
    local_series, ends = lax.optimization_barrier((series, ends))
    ends = from_chunks(ends.reshape(chunks, 2 * order, LANES), blocks)
    if not whole_chunk:
        ends = ends.at[:, order:].set(weights_of(own_residues, own_rates))
    ends = all_to_all(ends, members)
    weights = to_chunks(ends).reshape(chunks * 2 * order, LANES)
    out_shape = jax.ShapeDtypeStruct((channels, length), jnp.bfloat16)
    out_scratch = [pltpu.VMEM(out_shape.shape, out_shape.dtype), pltpu.SemaphoreType.DMA((chunks,))]
    local, factors, out = call(
        functools.partial(local_kernel, places, order),
        (
            jax.ShapeDtypeStruct((length * chunks, LANES), f32),
            jax.ShapeDtypeStruct((chunks * order * SUBLANES, LANES), f32),
            out_shape,
        ),
        decays,
        weights,
        local_series,
        direct_gain.reshape(chunks, LANES),
        q_proj,
        out_spaces=(pltpu.VMEM, pltpu.VMEM, pl.ANY),
        scratch=out_scratch,
        flops=4 * order * channels * length,
    )
    starts = call(
        functools.partial(prefix_kernel, length, members),
        jax.ShapeDtypeStruct((blocks,) + own_rates.shape, f32),
        own_rates,
        ends,
    )
    starts = all_to_all(starts, members)
    carry = to_chunks(starts).reshape(chunks * order, LANES)
    return call(
        functools.partial(output_kernel, places, order),
        out_shape,
        decays,
        factors,
        carry,
        local,
        q_proj,
        out,
        out_spaces=pl.ANY,
        aliases={5: 0},
        scratch=[pltpu.VMEM((length * chunks, LANES), f32)] + out_scratch,
        flops=2 * order * channels * length,
    )


def solution(mesh):
    return jax.shard_map(
        functools.partial(shards, mesh.shape["seq"]),
        mesh=mesh,
        in_specs=(
            P("chan", ("groups", "seq")),
            P("chan", ("groups", "seq")),
            P("chan", ("groups", "seq")),
            P(("chan", "seq"), None),
            P(("chan", "seq"), None),
            P("chan"),
        ),
        out_specs=P("chan", ("groups", "seq")),
        check_vma=False,
    )
```

```python
import functools
import jax
import jax.numpy as jnp
from jax import lax
from jax.experimental import pallas as pl
from jax.experimental.pallas import tpu as pltpu
from jax.sharding import PartitionSpec as P

LANES = 128
SUBLANES = 8
UNROLL = 8
COPIES_COST = 10**10
VMEM_LIMIT = 32 * 1024 * 1024


def one_minus_exp(y):
    series = jnp.ones_like(y)
    for k in range(11, 1, -1):
        series = 1.0 - (y * (1.0 / k)) * series
    return jnp.where(y < 0.5, y * series, 1.0 - jnp.exp(-y))


def weights_of(residue, rate):
    return residue * jnp.sqrt(one_minus_exp(2.0 * rate))


def copies_kernel(rate_hbm, residue_hbm, copies_ref, rate_ref, residue_ref, sems):
    pairs = ((rate_hbm, rate_ref), (residue_hbm, residue_ref))
    loads = [pltpu.make_async_copy(source, target, sems.at[i]) for i, (source, target) in enumerate(pairs)]
    for load in loads:
        load.start()
    for load in loads:
        load.wait()
    rate = rate_ref[...]
    order = rate.shape[0]
    decay, weight = jnp.exp(-rate), weights_of(residue_ref[...], rate)
    for piece in range(copies_ref.shape[0]):
        copies_ref[piece, :order] = decay
        copies_ref[piece, order:] = weight


def token_rows(half, length, token):
    row = (half * length + token) * SUBLANES
    return pl.ds(row if isinstance(row, int) else pl.multiple_of(row, SUBLANES), SUBLANES)


def chunk_rows(chunk, length):
    return pl.ds(chunk // SUBLANES * length * SUBLANES + chunk % SUBLANES, length, stride=SUBLANES)


def mode_rows(ref, base, order, per_chunk, half):
    first = half * SUBLANES * per_chunk + base
    return [ref[pl.ds(first + r, SUBLANES, stride=per_chunk), :] for r in range(order)]


def gain_rows(gain_ref, places, half):
    own = places[half * SUBLANES : (half + 1) * SUBLANES]
    return jnp.concatenate([gain_ref[pl.ds(place, 1), :] for place in own], axis=0)


def scan_half(half, places, order, state, params_ref, series_ref, gain_ref, conv_ref, beside=()):
    length = series_ref.shape[0] // len(places)
    tokens = length // SUBLANES
    decay = mode_rows(params_ref, 0, order, 2 * order, half)
    if conv_ref is not None:
        weight = mode_rows(params_ref, order, order, 2 * order, half)
        gain = gain_rows(gain_ref, places, half)

    def steps(i, state):
        state = list(state)
        for u in range(tokens):
            rows = token_rows(half, length, i * tokens + u)
            x = series_ref[rows, :]
            for r in range(order):
                state[r] = decay[r] * state[r] + x
            if conv_ref is not None:
                conv_ref[rows, :] = tree_sum([weight[r] * state[r] for r in range(order)] + [gain * x])
        return tuple(state)

    if not beside:
        return lax.fori_loop(0, SUBLANES, steps, tuple(state))
    for i, call_beside in enumerate(beside):
        state = steps(i, state)
        call_beside()
    return state


def state_kernel(places, order, params_ref, k_ref, v_ref, gain_ref, series_ref, state_ref, early_ref):
    chunks, length = len(places), k_ref.shape[1]
    halves = chunks // SUBLANES

    def build(chunk):
        rows = pl.ds(places[chunk] * LANES, LANES)
        gated = k_ref[rows, :].astype(jnp.float32) * v_ref[rows, :].astype(jnp.float32)
        series_ref[chunk_rows(chunk, length), :] = gated.T

    def scan(conv_ref):
        for half in range(halves):
            after = range((half + 1) * SUBLANES, min((half + 2) * SUBLANES, chunks))
            beside = [functools.partial(build, chunk) for chunk in after]
            state = (jnp.zeros((SUBLANES, LANES), jnp.float32),) * order
            state = scan_half(half, places, order, state, params_ref, series_ref, gain_ref, conv_ref, beside)
            for r in range(order):
                state_ref[pl.ds(half * SUBLANES * order + r, SUBLANES, stride=order), :] = state[r]

    for chunk in range(SUBLANES):
        build(chunk)
    first = lax.axis_index("seq") == 0

    @pl.when(first)
    def _():
        scan(early_ref)

    @pl.when(jnp.logical_not(first))
    def _():
        scan(None)


def prefix_kernel(length, members, rate_ref, ends_ref, starts_ref):
    span_decay = jnp.exp(-float(length) * rate_ref[...])
    carry = jnp.zeros(rate_ref.shape, jnp.float32)
    for block in range(len(members)):
        starts_ref[members.index(block)] = carry
        carry = span_decay * carry + ends_ref[members.index(block)]


def tree_sum(terms):
    terms = list(terms)
    while len(terms) > 1:
        terms = [terms[i] + terms[i + 1] if i + 1 < len(terms) else terms[i] for i in range(0, len(terms), 2)]
    return terms[0]


def leaving(chunk, places, gated_ref, out_ref, sems):
    rows = pl.ds(places[chunk] * LANES, LANES)
    return pltpu.make_async_copy(gated_ref.at[rows, :], out_ref.at[rows, :], sems.at[chunk])


def finish(chunk, places, conv_ref, q_ref, gated_ref, out_ref, sems):
    length = conv_ref.shape[0] // len(places)
    rows = pl.ds(places[chunk] * LANES, LANES)
    conv = conv_ref[chunk_rows(chunk, length), :].T
    gated_ref[rows, :] = (q_ref[rows, :].astype(jnp.float32) * conv).astype(jnp.bfloat16)
    leaving(chunk, places, gated_ref, out_ref, sems).start()


def output_kernel(
    places, order, carry_ref, params_ref, series_ref, early_ref, gain_ref, q_ref, out_ref, conv_ref, gated_ref, sems
):
    chunks = len(places)
    halves = chunks // SUBLANES
    first = lax.axis_index("seq") == 0

    def send(chunk, source_ref):
        finish(chunk, places, source_ref, q_ref, gated_ref, out_ref, sems)

    @pl.when(first)
    def _():
        for chunk in range(chunks):
            send(chunk, early_ref)

    @pl.when(jnp.logical_not(first))
    def _():
        for half in range(halves):
            before = range(max(half - 1, 0) * SUBLANES, half * SUBLANES)
            beside = [functools.partial(send, chunk, conv_ref) for chunk in before]
            state = mode_rows(carry_ref, 0, order, order, half)
            scan_half(half, places, order, state, params_ref, series_ref, gain_ref, conv_ref, beside)
        for chunk in range(chunks - SUBLANES, chunks):
            send(chunk, conv_ref)

    for chunk in range(chunks):
        leaving(chunk, places, gated_ref, out_ref, sems).wait()


def call(kernel, out_shape, *args, in_spaces=None, out_spaces=None, scratch=(), flops=0):
    in_bytes = sum(a.size * a.dtype.itemsize for a in args)
    in_spaces = in_spaces or [pltpu.VMEM] * len(args)
    out_spaces = out_spaces or jax.tree.map(lambda _: pltpu.VMEM, out_shape)
    return pl.pallas_call(
        kernel,
        out_shape=out_shape,
        in_specs=[pl.BlockSpec(memory_space=space) for space in in_spaces],
        out_specs=jax.tree.map(lambda space: pl.BlockSpec(memory_space=space), out_spaces),
        scratch_shapes=list(scratch),
        compiler_params=pltpu.CompilerParams(vmem_limit_bytes=VMEM_LIMIT),
        cost_estimate=pl.CostEstimate(flops=flops, bytes_accessed=in_bytes, transcendentals=0),
    )(*args)


def to_chunks(pieces):
    owners, rows, own = pieces.shape
    if own == LANES:
        return pieces
    if own < LANES:
        group = LANES // own
        return pieces.reshape(owners // group, group, rows, own).swapaxes(1, 2).reshape(-1, rows, LANES)
    return pieces.reshape(owners, rows, own // LANES, LANES).swapaxes(1, 2).reshape(-1, rows, LANES)


def from_chunks(pieces, owners):
    chunks, rows, _ = pieces.shape
    own = chunks * LANES // owners
    if own == LANES:
        return pieces
    if own < LANES:
        group = LANES // own
        return pieces.reshape(chunks, rows, group, own).swapaxes(1, 2).reshape(owners, rows, own)
    return pieces.reshape(owners, own // LANES, rows, LANES).swapaxes(1, 2).reshape(owners, rows, own)


def all_to_all(pieces, members):
    return lax.all_to_all(pieces, "seq", split_axis=0, concat_axis=0, axis_index_groups=[members], tiled=True)


def shards(blocks, q_proj, k_proj, value_projection, residues, rates, direct_gain):
    channels, length = q_proj.shape
    order = residues.shape[1]
    chunks = channels // LANES
    f32 = jnp.float32

    members, places = list(range(blocks)), list(range(chunks))
    if blocks == chunks:
        far, middle = blocks // 2, blocks * 11 // 16
        upper = [middle] + [block for block in members[:far - 1:-1] if block != middle]
        members = [block for one in upper for block in (one, one - far)]
        places = list(members)

    own_rates = rates.T
    copies = call(
        copies_kernel,
        jax.ShapeDtypeStruct((blocks, 2 * order, rates.shape[0]), f32),
        pltpu.with_memory_space_constraint(own_rates, pltpu.HBM),
        pltpu.with_memory_space_constraint(residues.T, pltpu.HBM),
        in_spaces=[pl.ANY] * 2,
        scratch=[pltpu.VMEM(own_rates.shape, f32)] * 2 + [pltpu.SemaphoreType.DMA((2,))],
        flops=COPIES_COST,
    )
    params = to_chunks(all_to_all(copies, members)).reshape(chunks * 2 * order, LANES)

    gain = direct_gain.reshape(chunks, LANES)
    rows = jax.ShapeDtypeStruct((length * chunks, LANES), f32)
    series, ends, early = call(
        functools.partial(state_kernel, places, order),
        (rows, jax.ShapeDtypeStruct((chunks * order, LANES), f32), rows),
        params,
        k_proj,
        value_projection,
        gain,
        flops=2 * order * channels * length,
    )
    ends = all_to_all(from_chunks(ends.reshape(chunks, order, LANES), blocks), members)
    starts = call(
        functools.partial(prefix_kernel, length, members),
        jax.ShapeDtypeStruct(ends.shape, f32),
        own_rates,
        ends,
    )
    carry = to_chunks(all_to_all(starts, members)).reshape(chunks * order, LANES)
    out_shape = jax.ShapeDtypeStruct((channels, length), jnp.bfloat16)
    return call(
        functools.partial(output_kernel, places, order),
        out_shape,
        carry,
        params,
        series,
        early,
        gain,
        q_proj,
        out_spaces=pl.ANY,
        scratch=[
            pltpu.VMEM(rows.shape, f32),
            pltpu.VMEM(out_shape.shape, out_shape.dtype),
            pltpu.SemaphoreType.DMA((chunks,)),
        ],
        flops=4 * order * channels * length,
    )


def solution(mesh):
    return jax.shard_map(
        functools.partial(shards, mesh.shape["seq"]),
        mesh=mesh,
        in_specs=(
            P("chan", ("groups", "seq")),
            P("chan", ("groups", "seq")),
            P("chan", ("groups", "seq")),
            P(("chan", "seq"), None),
            P(("chan", "seq"), None),
            P("chan"),
        ),
        out_specs=P("chan", ("groups", "seq")),
        check_vma=False,
    )
```

```python
import functools
import jax
import jax.numpy as jnp
from jax import lax
from jax.experimental import pallas as pl
from jax.experimental.pallas import tpu as pltpu
from jax.sharding import PartitionSpec as P

LANES = 128
SUBLANES = 8
UNROLL = 8
COPIES_COST = 10**10
VMEM_LIMIT = 32 * 1024 * 1024


def copies_kernel(rate_hbm, copies_ref, rate_ref, sem):
    load = pltpu.make_async_copy(rate_hbm, rate_ref, sem)
    load.start()
    load.wait()
    decay = jnp.exp(-rate_ref[...])
    for piece in range(copies_ref.shape[0]):
        copies_ref[piece] = decay


def token_rows(half, length, token):
    row = (half * length + token) * SUBLANES
    return pl.ds(row if isinstance(row, int) else pl.multiple_of(row, SUBLANES), SUBLANES)


def chunk_rows(chunk, length):
    return pl.ds(chunk // SUBLANES * length * SUBLANES + chunk % SUBLANES, length, stride=SUBLANES)


def mode_rows(ref, base, order, per_chunk, chunks, half):
    first = half * SUBLANES * per_chunk + base
    return [ref[pl.ds(first + r, SUBLANES, stride=per_chunk), :] for r in range(order)]


def one_minus_exp(y):
    series = jnp.ones_like(y)
    for k in range(11, 1, -1):
        series = 1.0 - (y * (1.0 / k)) * series
    return jnp.where(y < 0.5, y * series, 1.0 - jnp.exp(-y))


def weights_of(residue, rate):
    return residue * jnp.sqrt(one_minus_exp(2.0 * rate))


def state_kernel(places, order, decays_ref, rate_ref, residue_ref, k_ref, v_ref, series_ref, state_ref):
    chunks, length = len(places), k_ref.shape[1]
    tokens = length // SUBLANES
    halves = chunks // SUBLANES

    def build(chunk):
        rows = pl.ds(places[chunk] * LANES, LANES)
        gated = k_ref[rows, :].astype(jnp.float32) * v_ref[rows, :].astype(jnp.float32)
        series_ref[chunk_rows(chunk, length), :] = gated.T

    weight = weights_of(residue_ref[...], rate_ref[...])
    for chunk in range(chunks):
        state_ref[pl.ds((2 * chunk + 1) * order, order), :] = weight
    for chunk in range(SUBLANES):
        build(chunk)
    for half in range(halves):
        decay = mode_rows(decays_ref, 0, order, order, chunks, half)
        square = [one * one for one in decay]

        def steps(i, state):
            state = list(state)
            for u in range(0, tokens, 2):
                x = series_ref[token_rows(half, length, i * tokens + u), :]
                y = series_ref[token_rows(half, length, i * tokens + u + 1), :]
                for r in range(order):
                    state[r] = square[r] * state[r] + (decay[r] * x + y)
            return tuple(state)

        state = (jnp.zeros((SUBLANES, LANES), jnp.float32),) * order
        if half + 1 < halves:
            for i in range(SUBLANES):
                state = steps(i, state)
                build((half + 1) * SUBLANES + i)
        else:
            state = lax.fori_loop(0, SUBLANES, steps, state)
        for r in range(order):
            state_ref[pl.ds(half * SUBLANES * 2 * order + r, SUBLANES, stride=2 * order), :] = state[r]


def prefix_kernel(length, members, rate_ref, ends_ref, starts_ref):
    span_decay = jnp.exp(-float(length) * rate_ref[...])
    carry = jnp.zeros(rate_ref.shape, jnp.float32)
    for block in range(len(members)):
        starts_ref[members.index(block)] = carry
        carry = span_decay * carry + ends_ref[members.index(block), : rate_ref.shape[0]]


def tree_sum(terms):
    terms = list(terms)
    while len(terms) > 1:
        terms = [terms[i] + terms[i + 1] if i + 1 < len(terms) else terms[i] for i in range(0, len(terms), 2)]
    return terms[0]


def leaving(chunk, places, gated_ref, out_ref, sems):
    rows = pl.ds(places[chunk] * LANES, LANES)
    return pltpu.make_async_copy(gated_ref.at[rows, :], out_ref.at[rows, :], sems.at[chunk])


def finish(chunk, places, conv_ref, q_ref, gated_ref, out_ref, sems):
    length = conv_ref.shape[0] // len(places)
    rows = pl.ds(places[chunk] * LANES, LANES)
    conv = conv_ref[chunk_rows(chunk, length), :].T
    gated_ref[rows, :] = (q_ref[rows, :].astype(jnp.float32) * conv).astype(jnp.bfloat16)
    leaving(chunk, places, gated_ref, out_ref, sems).start()


def local_kernel(
    places, order, decays_ref, weights_ref, series_ref, gain_ref, q_ref, conv_ref, out_ref, gated_ref, sems
):
    chunks = len(places)
    length = series_ref.shape[0] // chunks
    for half in range(chunks // SUBLANES):
        decay = mode_rows(decays_ref, 0, order, order, chunks, half)
        weight = mode_rows(weights_ref, order, order, 2 * order, chunks, half)
        own = places[half * SUBLANES : (half + 1) * SUBLANES]
        gain = jnp.concatenate([gain_ref[pl.ds(place, 1), :] for place in own], axis=0)

        def steps(i, state):
            state = list(state)
            for u in range(UNROLL):
                rows = token_rows(half, length, i * UNROLL + u)
                x = series_ref[rows, :]
                for r in range(order):
                    state[r] = decay[r] * state[r] + x
                terms = [weight[r] * state[r] for r in range(order)]
                conv_ref[rows, :] = tree_sum(terms + [gain * x])
            return tuple(state)

        zero = jnp.zeros((SUBLANES, LANES), jnp.float32)
        lax.fori_loop(0, length // UNROLL, steps, (zero,) * order)

    @pl.when(lax.axis_index("seq") == 0)
    def _():
        for chunk in range(chunks):
            finish(chunk, places, conv_ref, q_ref, gated_ref, out_ref, sems)
        for chunk in range(chunks):
            leaving(chunk, places, gated_ref, out_ref, sems).wait()


def output_kernel(
    places, order, decays_ref, weights_ref, carry_ref, local_ref, q_ref, _, out_ref, conv_ref, gated_ref, sems
):
    chunks = len(places)
    length = local_ref.shape[0] // chunks
    tokens = length // SUBLANES

    @pl.when(lax.axis_index("seq") > 0)
    def _():
        for half in range(chunks // SUBLANES):
            decay = mode_rows(decays_ref, 0, order, order, chunks, half)
            weight = mode_rows(weights_ref, order, order, 2 * order, chunks, half)
            carry = mode_rows(carry_ref, 0, order, order, chunks, half)

            def steps(i, fading):
                fading = list(fading)
                for u in range(tokens):
                    rows = token_rows(half, length, i * tokens + u)
                    fading = [decay[r] * fading[r] for r in range(order)]
                    conv_ref[rows, :] = tree_sum(fading + [local_ref[rows, :]])
                return tuple(fading)

            fading = tuple(weight[r] * carry[r] for r in range(order))
            if half == 0:
                lax.fori_loop(0, SUBLANES, steps, fading)
            else:
                for i in range(SUBLANES):
                    fading = steps(i, fading)
                    finish((half - 1) * SUBLANES + i, places, conv_ref, q_ref, gated_ref, out_ref, sems)
        for chunk in range(chunks - SUBLANES, chunks):
            finish(chunk, places, conv_ref, q_ref, gated_ref, out_ref, sems)
        for chunk in range(chunks):
            leaving(chunk, places, gated_ref, out_ref, sems).wait()


def call(kernel, out_shape, *args, in_spaces=None, out_spaces=None, aliases=None, scratch=(), flops=0):
    in_bytes = sum(a.size * a.dtype.itemsize for a in args)
    in_spaces = in_spaces or [pl.ANY if i in (aliases or {}) else pltpu.VMEM for i in range(len(args))]
    out_spaces = out_spaces or jax.tree.map(lambda _: pltpu.VMEM, out_shape)
    return pl.pallas_call(
        kernel,
        out_shape=out_shape,
        in_specs=[pl.BlockSpec(memory_space=space) for space in in_spaces],
        out_specs=jax.tree.map(lambda space: pl.BlockSpec(memory_space=space), out_spaces),
        scratch_shapes=list(scratch),
        input_output_aliases=aliases or {},
        compiler_params=pltpu.CompilerParams(vmem_limit_bytes=VMEM_LIMIT),
        cost_estimate=pl.CostEstimate(flops=flops, bytes_accessed=in_bytes, transcendentals=0),
    )(*args)


def to_chunks(pieces):
    owners, rows, own = pieces.shape
    if own == LANES:
        return pieces
    if own < LANES:
        group = LANES // own
        return pieces.reshape(owners // group, group, rows, own).swapaxes(1, 2).reshape(-1, rows, LANES)
    return pieces.reshape(owners, rows, own // LANES, LANES).swapaxes(1, 2).reshape(-1, rows, LANES)


def from_chunks(pieces, owners):
    chunks, rows, _ = pieces.shape
    own = chunks * LANES // owners
    if own == LANES:
        return pieces
    if own < LANES:
        group = LANES // own
        return pieces.reshape(chunks, rows, group, own).swapaxes(1, 2).reshape(owners, rows, own)
    return pieces.reshape(owners, own // LANES, rows, LANES).swapaxes(1, 2).reshape(owners, rows, own)


def all_to_all(pieces, members):
    return lax.all_to_all(pieces, "seq", split_axis=0, concat_axis=0, axis_index_groups=[members], tiled=True)


def shards(blocks, q_proj, k_proj, value_projection, residues, rates, direct_gain):
    channels, length = q_proj.shape
    order = residues.shape[1]
    chunks = channels // LANES
    f32 = jnp.float32

    members, places = list(range(blocks)), list(range(chunks))
    if blocks == chunks:
        far, middle = blocks // 2, blocks * 11 // 16
        upper = [middle] + [block for block in members[:far - 1:-1] if block != middle]
        members = [block for one in upper for block in (one, one - far)]
        places = list(members)

    own_rates, own_residues = rates.T, residues.T
    copies = call(
        copies_kernel,
        jax.ShapeDtypeStruct((blocks,) + own_rates.shape, f32),
        pltpu.with_memory_space_constraint(own_rates, pltpu.HBM),
        in_spaces=[pl.ANY],
        scratch=[pltpu.VMEM(own_rates.shape, f32), pltpu.SemaphoreType.DMA],
        flops=COPIES_COST,
    )
    decays = to_chunks(all_to_all(copies, members)).reshape(chunks * order, LANES)

    whole_chunk = own_rates.shape[1] == LANES
    unused = jnp.zeros((order, LANES), f32)
    series, ends = call(
        functools.partial(state_kernel, places, order),
        (
            jax.ShapeDtypeStruct((length * chunks, LANES), f32),
            jax.ShapeDtypeStruct((chunks * 2 * order, LANES), f32),
        ),
        decays,
        own_rates if whole_chunk else unused,
        own_residues if whole_chunk else unused,
        k_proj,
        value_projection,
        flops=2 * order * channels * length,
    )
    local_series, ends = lax.optimization_barrier((series, ends))
    ends = from_chunks(ends.reshape(chunks, 2 * order, LANES), blocks)
    if not whole_chunk:
        ends = ends.at[:, order:].set(weights_of(own_residues, own_rates))
    ends = all_to_all(ends, members)
    weights = to_chunks(ends).reshape(chunks * 2 * order, LANES)
    out_shape = jax.ShapeDtypeStruct((channels, length), jnp.bfloat16)
    out_scratch = [pltpu.VMEM(out_shape.shape, out_shape.dtype), pltpu.SemaphoreType.DMA((chunks,))]
    local, out = call(
        functools.partial(local_kernel, places, order),
        (
            jax.ShapeDtypeStruct((length * chunks, LANES), f32),
            out_shape,
        ),
        decays,
        weights,
        local_series,
        direct_gain.reshape(chunks, LANES),
        q_proj,
        out_spaces=(pltpu.VMEM, pl.ANY),
        scratch=out_scratch,
        flops=4 * order * channels * length,
    )
    starts = call(
        functools.partial(prefix_kernel, length, members),
        jax.ShapeDtypeStruct((blocks,) + own_rates.shape, f32),
        own_rates,
        ends,
    )
    starts = all_to_all(starts, members)
    carry = to_chunks(starts).reshape(chunks * order, LANES)
    return call(
        functools.partial(output_kernel, places, order),
        out_shape,
        decays,
        weights,
        carry,
        local,
        q_proj,
        out,
        out_spaces=pl.ANY,
        aliases={5: 0},
        scratch=[pltpu.VMEM((length * chunks, LANES), f32)] + out_scratch,
        flops=2 * order * channels * length,
    )


def solution(mesh):
    return jax.shard_map(
        functools.partial(shards, mesh.shape["seq"]),
        mesh=mesh,
        in_specs=(
            P("chan", ("groups", "seq")),
            P("chan", ("groups", "seq")),
            P("chan", ("groups", "seq")),
            P(("chan", "seq"), None),
            P(("chan", "seq"), None),
            P("chan"),
        ),
        out_specs=P("chan", ("groups", "seq")),
        check_vma=False,
    )
```

```python
import functools
import jax
import jax.numpy as jnp
from jax import lax
from jax.experimental import pallas as pl
from jax.experimental.pallas import tpu as pltpu
from jax.sharding import PartitionSpec as P

LANES = 128
SUBLANES = 8
UNROLL = 8
COPIES_COST = 10**10
VMEM_LIMIT = 32 * 1024 * 1024


def copies_kernel(rate_hbm, copies_ref, rate_ref, sem):
    load = pltpu.make_async_copy(rate_hbm, rate_ref, sem)
    load.start()
    load.wait()
    decay = jnp.exp(-rate_ref[...])
    for piece in range(copies_ref.shape[0]):
        copies_ref[piece] = decay


def token_rows(half, length, token):
    row = (half * length + token) * SUBLANES
    return pl.ds(row if isinstance(row, int) else pl.multiple_of(row, SUBLANES), SUBLANES)


def chunk_rows(chunk, length):
    return pl.ds(chunk // SUBLANES * length * SUBLANES + chunk % SUBLANES, length, stride=SUBLANES)


def mode_rows(ref, base, order, per_chunk, chunks, half):
    first = half * SUBLANES * per_chunk + base
    return [ref[pl.ds(first + r, SUBLANES, stride=per_chunk), :] for r in range(order)]


def one_minus_exp(y):
    series = jnp.ones_like(y)
    for k in range(11, 1, -1):
        series = 1.0 - (y * (1.0 / k)) * series
    return jnp.where(y < 0.5, y * series, 1.0 - jnp.exp(-y))


def weights_of(residue, rate):
    return residue * jnp.sqrt(one_minus_exp(2.0 * rate))


def state_kernel(places, order, decays_ref, rate_ref, residue_ref, k_ref, v_ref, series_ref, state_ref):
    chunks, length = len(places), k_ref.shape[1]
    tokens = length // SUBLANES
    halves = chunks // SUBLANES

    def build(chunk):
        rows = pl.ds(places[chunk] * LANES, LANES)
        gated = k_ref[rows, :].astype(jnp.float32) * v_ref[rows, :].astype(jnp.float32)
        series_ref[chunk_rows(chunk, length), :] = gated.T

    weight = weights_of(residue_ref[...], rate_ref[...])
    for chunk in range(chunks):
        state_ref[pl.ds((2 * chunk + 1) * order, order), :] = weight
    for chunk in range(SUBLANES):
        build(chunk)
    for half in range(halves):
        decay = mode_rows(decays_ref, 0, order, order, chunks, half)
        square = [one * one for one in decay]

        def steps(i, state):
            state = list(state)
            for u in range(0, tokens, 2):
                x = series_ref[token_rows(half, length, i * tokens + u), :]
                y = series_ref[token_rows(half, length, i * tokens + u + 1), :]
                for r in range(order):
                    state[r] = square[r] * state[r] + (decay[r] * x + y)
            return tuple(state)

        state = (jnp.zeros((SUBLANES, LANES), jnp.float32),) * order
        if half + 1 < halves:
            for i in range(SUBLANES):
                state = steps(i, state)
                build((half + 1) * SUBLANES + i)
        else:
            state = lax.fori_loop(0, SUBLANES, steps, state)
        for r in range(order):
            state_ref[pl.ds(half * SUBLANES * 2 * order + r, SUBLANES, stride=2 * order), :] = state[r]


def prefix_kernel(length, members, rate_ref, ends_ref, starts_ref):
    span_decay = jnp.exp(-float(length) * rate_ref[...])
    carry = jnp.zeros(rate_ref.shape, jnp.float32)
    for block in range(len(members)):
        starts_ref[members.index(block)] = carry
        carry = span_decay * carry + ends_ref[members.index(block), : rate_ref.shape[0]]


def tree_sum(terms):
    terms = list(terms)
    while len(terms) > 1:
        terms = [terms[i] + terms[i + 1] if i + 1 < len(terms) else terms[i] for i in range(0, len(terms), 2)]
    return terms[0]


def leaving(chunk, places, gated_ref, out_ref, sems):
    rows = pl.ds(places[chunk] * LANES, LANES)
    return pltpu.make_async_copy(gated_ref.at[rows, :], out_ref.at[rows, :], sems.at[chunk])


def finish(chunk, places, conv_ref, q_ref, gated_ref, out_ref, sems):
    length = conv_ref.shape[0] // len(places)
    rows = pl.ds(places[chunk] * LANES, LANES)
    conv = conv_ref[chunk_rows(chunk, length), :].T
    gated_ref[rows, :] = (q_ref[rows, :].astype(jnp.float32) * conv).astype(jnp.bfloat16)
    leaving(chunk, places, gated_ref, out_ref, sems).start()


def local_kernel(
    places, order, decays_ref, weights_ref, series_ref, gain_ref, q_ref, conv_ref, out_ref, gated_ref, sems
):
    chunks = len(places)
    length = series_ref.shape[0] // chunks
    for half in range(chunks // SUBLANES):
        decay = mode_rows(decays_ref, 0, order, order, chunks, half)
        weight = mode_rows(weights_ref, order, order, 2 * order, chunks, half)
        own = places[half * SUBLANES : (half + 1) * SUBLANES]
        gain = jnp.concatenate([gain_ref[pl.ds(place, 1), :] for place in own], axis=0)

        def steps(i, state):
            state = list(state)
            for u in range(UNROLL):
                rows = token_rows(half, length, i * UNROLL + u)
                x = series_ref[rows, :]
                for r in range(order):
                    state[r] = decay[r] * state[r] + x
                terms = [weight[r] * state[r] for r in range(order)]
                conv_ref[rows, :] = tree_sum(terms + [gain * x])
            return tuple(state)

        zero = jnp.zeros((SUBLANES, LANES), jnp.float32)
        lax.fori_loop(0, length // UNROLL, steps, (zero,) * order)

    @pl.when(lax.axis_index("seq") == 0)
    def _():
        for chunk in range(chunks):
            finish(chunk, places, conv_ref, q_ref, gated_ref, out_ref, sems)
        for chunk in range(chunks):
            leaving(chunk, places, gated_ref, out_ref, sems).wait()


def output_kernel(
    places, order, decays_ref, weights_ref, carry_ref, local_ref, q_ref, _, out_ref, conv_ref, gated_ref, sems
):
    chunks = len(places)
    length = local_ref.shape[0] // chunks
    tokens = length // SUBLANES

    @pl.when(lax.axis_index("seq") > 0)
    def _():
        for half in range(chunks // SUBLANES):
            decay = mode_rows(decays_ref, 0, order, order, chunks, half)
            weight = mode_rows(weights_ref, order, order, 2 * order, chunks, half)
            carry = mode_rows(carry_ref, 0, order, order, chunks, half)

            def steps(i, fading):
                fading = list(fading)
                for u in range(tokens):
                    rows = token_rows(half, length, i * tokens + u)
                    fading = [decay[r] * fading[r] for r in range(order)]
                    conv_ref[rows, :] = tree_sum(fading + [local_ref[rows, :]])
                return tuple(fading)

            fading = tuple(weight[r] * carry[r] for r in range(order))
            if half == 0:
                lax.fori_loop(0, SUBLANES, steps, fading)
            else:
                for i in range(SUBLANES):
                    fading = steps(i, fading)
                    finish((half - 1) * SUBLANES + i, places, conv_ref, q_ref, gated_ref, out_ref, sems)
        for chunk in range(chunks - SUBLANES, chunks):
            finish(chunk, places, conv_ref, q_ref, gated_ref, out_ref, sems)
        for chunk in range(chunks):
            leaving(chunk, places, gated_ref, out_ref, sems).wait()


def call(kernel, out_shape, *args, in_spaces=None, out_spaces=None, aliases=None, scratch=(), flops=0):
    in_bytes = sum(a.size * a.dtype.itemsize for a in args)
    in_spaces = in_spaces or [pl.ANY if i in (aliases or {}) else pltpu.VMEM for i in range(len(args))]
    out_spaces = out_spaces or jax.tree.map(lambda _: pltpu.VMEM, out_shape)
    return pl.pallas_call(
        kernel,
        out_shape=out_shape,
        in_specs=[pl.BlockSpec(memory_space=space) for space in in_spaces],
        out_specs=jax.tree.map(lambda space: pl.BlockSpec(memory_space=space), out_spaces),
        scratch_shapes=list(scratch),
        input_output_aliases=aliases or {},
        compiler_params=pltpu.CompilerParams(vmem_limit_bytes=VMEM_LIMIT),
        cost_estimate=pl.CostEstimate(flops=flops, bytes_accessed=in_bytes, transcendentals=0),
    )(*args)


def to_chunks(pieces):
    owners, rows, own = pieces.shape
    if own == LANES:
        return pieces
    if own < LANES:
        group = LANES // own
        return pieces.reshape(owners // group, group, rows, own).swapaxes(1, 2).reshape(-1, rows, LANES)
    return pieces.reshape(owners, rows, own // LANES, LANES).swapaxes(1, 2).reshape(-1, rows, LANES)


def from_chunks(pieces, owners):
    chunks, rows, _ = pieces.shape
    own = chunks * LANES // owners
    if own == LANES:
        return pieces
    if own < LANES:
        group = LANES // own
        return pieces.reshape(chunks, rows, group, own).swapaxes(1, 2).reshape(owners, rows, own)
    return pieces.reshape(owners, own // LANES, rows, LANES).swapaxes(1, 2).reshape(owners, rows, own)


def all_to_all(pieces, members):
    return lax.all_to_all(pieces, "seq", split_axis=0, concat_axis=0, axis_index_groups=[members], tiled=True)


def shards(blocks, q_proj, k_proj, value_projection, residues, rates, direct_gain):
    channels, length = q_proj.shape
    order = residues.shape[1]
    chunks = channels // LANES
    f32 = jnp.float32

    members, places = list(range(blocks)), list(range(chunks))
    if blocks == chunks:
        far, middle = blocks // 2, blocks * 7 // 16
        lower = [middle] + [block for block in members[far - 1 :: -1] if block != middle]
        members = [block for one in lower for block in (one, one + far)]
        places = list(members)

    own_rates, own_residues = rates.T, residues.T
    copies = call(
        copies_kernel,
        jax.ShapeDtypeStruct((blocks,) + own_rates.shape, f32),
        pltpu.with_memory_space_constraint(own_rates, pltpu.HBM),
        in_spaces=[pl.ANY],
        scratch=[pltpu.VMEM(own_rates.shape, f32), pltpu.SemaphoreType.DMA],
        flops=COPIES_COST,
    )
    decays = to_chunks(all_to_all(copies, members)).reshape(chunks * order, LANES)

    whole_chunk = own_rates.shape[1] == LANES
    unused = jnp.zeros((order, LANES), f32)
    series, ends = call(
        functools.partial(state_kernel, places, order),
        (
            jax.ShapeDtypeStruct((length * chunks, LANES), f32),
            jax.ShapeDtypeStruct((chunks * 2 * order, LANES), f32),
        ),
        decays,
        own_rates if whole_chunk else unused,
        own_residues if whole_chunk else unused,
        k_proj,
        value_projection,
        flops=2 * order * channels * length,
    )
    local_series, ends = lax.optimization_barrier((series, ends))
    ends = from_chunks(ends.reshape(chunks, 2 * order, LANES), blocks)
    if not whole_chunk:
        ends = ends.at[:, order:].set(weights_of(own_residues, own_rates))
    ends = all_to_all(ends, members)
    weights = to_chunks(ends).reshape(chunks * 2 * order, LANES)
    out_shape = jax.ShapeDtypeStruct((channels, length), jnp.bfloat16)
    out_scratch = [pltpu.VMEM(out_shape.shape, out_shape.dtype), pltpu.SemaphoreType.DMA((chunks,))]
    local, out = call(
        functools.partial(local_kernel, places, order),
        (
            jax.ShapeDtypeStruct((length * chunks, LANES), f32),
            out_shape,
        ),
        decays,
        weights,
        local_series,
        direct_gain.reshape(chunks, LANES),
        q_proj,
        out_spaces=(pltpu.VMEM, pl.ANY),
        scratch=out_scratch,
        flops=4 * order * channels * length,
    )
    starts = call(
        functools.partial(prefix_kernel, length, members),
        jax.ShapeDtypeStruct((blocks,) + own_rates.shape, f32),
        own_rates,
        ends,
    )
    starts = all_to_all(starts, members)
    carry = to_chunks(starts).reshape(chunks * order, LANES)
    return call(
        functools.partial(output_kernel, places, order),
        out_shape,
        decays,
        weights,
        carry,
        local,
        q_proj,
        out,
        out_spaces=pl.ANY,
        aliases={5: 0},
        scratch=[pltpu.VMEM((length * chunks, LANES), f32)] + out_scratch,
        flops=2 * order * channels * length,
    )


def solution(mesh):
    return jax.shard_map(
        functools.partial(shards, mesh.shape["seq"]),
        mesh=mesh,
        in_specs=(
            P("chan", ("groups", "seq")),
            P("chan", ("groups", "seq")),
            P("chan", ("groups", "seq")),
            P(("chan", "seq"), None),
            P(("chan", "seq"), None),
            P("chan"),
        ),
        out_specs=P("chan", ("groups", "seq")),
        check_vma=False,
    )
```

```python
import functools
import jax
import jax.numpy as jnp
from jax import lax
from jax.experimental import pallas as pl
from jax.experimental.pallas import tpu as pltpu
from jax.sharding import PartitionSpec as P

LANES = 128
SUBLANES = 8
UNROLL = 8
COPIES_COST = 10**10
VMEM_LIMIT = 32 * 1024 * 1024


def copies_kernel(rate_hbm, copies_ref, rate_ref, sem):
    load = pltpu.make_async_copy(rate_hbm, rate_ref, sem)
    load.start()
    load.wait()
    decay = jnp.exp(-rate_ref[...])
    for piece in range(copies_ref.shape[0]):
        copies_ref[piece] = decay


def token_rows(half, length, token):
    row = (half * length + token) * SUBLANES
    return pl.ds(row if isinstance(row, int) else pl.multiple_of(row, SUBLANES), SUBLANES)


def chunk_rows(chunk, length):
    return pl.ds(chunk // SUBLANES * length * SUBLANES + chunk % SUBLANES, length, stride=SUBLANES)


def mode_rows(ref, base, order, per_chunk, chunks, half):
    first = half * SUBLANES * per_chunk + base
    return [ref[pl.ds(first + r, SUBLANES, stride=per_chunk), :] for r in range(order)]


def one_minus_exp(y):
    series = jnp.ones_like(y)
    for k in range(11, 1, -1):
        series = 1.0 - (y * (1.0 / k)) * series
    return jnp.where(y < 0.5, y * series, 1.0 - jnp.exp(-y))


def weights_of(residue, rate):
    return residue * jnp.sqrt(one_minus_exp(2.0 * rate))


def state_kernel(places, order, decays_ref, rate_ref, residue_ref, k_ref, v_ref, series_ref, state_ref):
    chunks, length = len(places), k_ref.shape[1]
    tokens = length // SUBLANES
    halves = chunks // SUBLANES

    def build(chunk):
        rows = pl.ds(places[chunk] * LANES, LANES)
        gated = k_ref[rows, :].astype(jnp.float32) * v_ref[rows, :].astype(jnp.float32)
        series_ref[chunk_rows(chunk, length), :] = gated.T

    weight = weights_of(residue_ref[...], rate_ref[...])
    for chunk in range(chunks):
        state_ref[pl.ds((2 * chunk + 1) * order, order), :] = weight
    for chunk in range(SUBLANES):
        build(chunk)
    for half in range(halves):
        decay = mode_rows(decays_ref, 0, order, order, chunks, half)
        square = [one * one for one in decay]

        def steps(i, state):
            state = list(state)
            for u in range(0, tokens, 2):
                x = series_ref[token_rows(half, length, i * tokens + u), :]
                y = series_ref[token_rows(half, length, i * tokens + u + 1), :]
                for r in range(order):
                    state[r] = square[r] * state[r] + (decay[r] * x + y)
            return tuple(state)

        state = (jnp.zeros((SUBLANES, LANES), jnp.float32),) * order
        if half + 1 < halves:
            for i in range(SUBLANES):
                state = steps(i, state)
                build((half + 1) * SUBLANES + i)
        else:
            state = lax.fori_loop(0, SUBLANES, steps, state)
        for r in range(order):
            state_ref[pl.ds(half * SUBLANES * 2 * order + r, SUBLANES, stride=2 * order), :] = state[r]


def prefix_kernel(length, members, rate_ref, ends_ref, starts_ref):
    span_decay = jnp.exp(-float(length) * rate_ref[...])
    carry = jnp.zeros(rate_ref.shape, jnp.float32)
    for block in range(len(members)):
        starts_ref[members.index(block)] = carry
        carry = span_decay * carry + ends_ref[members.index(block), : rate_ref.shape[0]]


def tree_sum(terms):
    terms = list(terms)
    while len(terms) > 1:
        terms = [terms[i] + terms[i + 1] if i + 1 < len(terms) else terms[i] for i in range(0, len(terms), 2)]
    return terms[0]


def leaving(chunk, places, gated_ref, out_ref, sems):
    rows = pl.ds(places[chunk] * LANES, LANES)
    return pltpu.make_async_copy(gated_ref.at[rows, :], out_ref.at[rows, :], sems.at[chunk])


def finish(chunk, places, conv_ref, q_ref, gated_ref, out_ref, sems):
    length = conv_ref.shape[0] // len(places)
    rows = pl.ds(places[chunk] * LANES, LANES)
    conv = conv_ref[chunk_rows(chunk, length), :].T
    gated_ref[rows, :] = (q_ref[rows, :].astype(jnp.float32) * conv).astype(jnp.bfloat16)
    leaving(chunk, places, gated_ref, out_ref, sems).start()


def local_kernel(
    places, order, decays_ref, weights_ref, series_ref, gain_ref, q_ref, conv_ref, out_ref, gated_ref, sems
):
    chunks = len(places)
    length = series_ref.shape[0] // chunks
    for half in range(chunks // SUBLANES):
        decay = mode_rows(decays_ref, 0, order, order, chunks, half)
        weight = mode_rows(weights_ref, order, order, 2 * order, chunks, half)
        own = places[half * SUBLANES : (half + 1) * SUBLANES]
        gain = jnp.concatenate([gain_ref[pl.ds(place, 1), :] for place in own], axis=0)

        def steps(i, state):
            state = list(state)
            for u in range(UNROLL):
                rows = token_rows(half, length, i * UNROLL + u)
                x = series_ref[rows, :]
                for r in range(order):
                    state[r] = decay[r] * state[r] + x
                terms = [weight[r] * state[r] for r in range(order)]
                conv_ref[rows, :] = tree_sum(terms + [gain * x])
            return tuple(state)

        zero = jnp.zeros((SUBLANES, LANES), jnp.float32)
        lax.fori_loop(0, length // UNROLL, steps, (zero,) * order)

    @pl.when(lax.axis_index("seq") == 0)
    def _():
        for chunk in range(chunks):
            finish(chunk, places, conv_ref, q_ref, gated_ref, out_ref, sems)
        for chunk in range(chunks):
            leaving(chunk, places, gated_ref, out_ref, sems).wait()


def output_kernel(
    places, order, decays_ref, weights_ref, carry_ref, local_ref, q_ref, _, out_ref, conv_ref, gated_ref, sems
):
    chunks = len(places)
    length = local_ref.shape[0] // chunks
    tokens = length // SUBLANES

    @pl.when(lax.axis_index("seq") > 0)
    def _():
        for half in range(chunks // SUBLANES):
            decay = mode_rows(decays_ref, 0, order, order, chunks, half)
            weight = mode_rows(weights_ref, order, order, 2 * order, chunks, half)
            carry = mode_rows(carry_ref, 0, order, order, chunks, half)

            def steps(i, fading):
                fading = list(fading)
                for u in range(tokens):
                    rows = token_rows(half, length, i * tokens + u)
                    fading = [decay[r] * fading[r] for r in range(order)]
                    conv_ref[rows, :] = tree_sum(fading + [local_ref[rows, :]])
                return tuple(fading)

            fading = tuple(weight[r] * carry[r] for r in range(order))
            if half == 0:
                lax.fori_loop(0, SUBLANES, steps, fading)
            else:
                for i in range(SUBLANES):
                    fading = steps(i, fading)
                    finish((half - 1) * SUBLANES + i, places, conv_ref, q_ref, gated_ref, out_ref, sems)
        for chunk in range(chunks - SUBLANES, chunks):
            finish(chunk, places, conv_ref, q_ref, gated_ref, out_ref, sems)
        for chunk in range(chunks):
            leaving(chunk, places, gated_ref, out_ref, sems).wait()


def call(kernel, out_shape, *args, in_spaces=None, out_spaces=None, aliases=None, scratch=(), flops=0):
    in_bytes = sum(a.size * a.dtype.itemsize for a in args)
    in_spaces = in_spaces or [pl.ANY if i in (aliases or {}) else pltpu.VMEM for i in range(len(args))]
    out_spaces = out_spaces or jax.tree.map(lambda _: pltpu.VMEM, out_shape)
    return pl.pallas_call(
        kernel,
        out_shape=out_shape,
        in_specs=[pl.BlockSpec(memory_space=space) for space in in_spaces],
        out_specs=jax.tree.map(lambda space: pl.BlockSpec(memory_space=space), out_spaces),
        scratch_shapes=list(scratch),
        input_output_aliases=aliases or {},
        compiler_params=pltpu.CompilerParams(vmem_limit_bytes=VMEM_LIMIT),
        cost_estimate=pl.CostEstimate(flops=flops, bytes_accessed=in_bytes, transcendentals=0),
    )(*args)


def to_chunks(pieces):
    owners, rows, own = pieces.shape
    if own == LANES:
        return pieces
    if own < LANES:
        group = LANES // own
        return pieces.reshape(owners // group, group, rows, own).swapaxes(1, 2).reshape(-1, rows, LANES)
    return pieces.reshape(owners, rows, own // LANES, LANES).swapaxes(1, 2).reshape(-1, rows, LANES)


def from_chunks(pieces, owners):
    chunks, rows, _ = pieces.shape
    own = chunks * LANES // owners
    if own == LANES:
        return pieces
    if own < LANES:
        group = LANES // own
        return pieces.reshape(chunks, rows, group, own).swapaxes(1, 2).reshape(owners, rows, own)
    return pieces.reshape(owners, own // LANES, rows, LANES).swapaxes(1, 2).reshape(owners, rows, own)


def all_to_all(pieces, members):
    return lax.all_to_all(pieces, "seq", split_axis=0, concat_axis=0, axis_index_groups=[members], tiled=True)


def shards(blocks, q_proj, k_proj, value_projection, residues, rates, direct_gain):
    channels, length = q_proj.shape
    order = residues.shape[1]
    chunks = channels // LANES
    f32 = jnp.float32

    members, places = list(range(blocks)), list(range(chunks))
    if blocks == chunks and blocks >= 8:
        far, middle = blocks // 2, blocks * 11 // 16
        upper = [block for block in members[: far - 1 : -1] if block not in (middle, blocks - 1)]
        upper = [middle] + upper + [blocks - 1]
        members = [block for pair in zip(upper, members[far - 1 :: -1]) for block in pair]
        places = list(members)

    own_rates, own_residues = rates.T, residues.T
    copies = call(
        copies_kernel,
        jax.ShapeDtypeStruct((blocks,) + own_rates.shape, f32),
        pltpu.with_memory_space_constraint(own_rates, pltpu.HBM),
        in_spaces=[pl.ANY],
        scratch=[pltpu.VMEM(own_rates.shape, f32), pltpu.SemaphoreType.DMA],
        flops=COPIES_COST,
    )
    decays = to_chunks(all_to_all(copies, members)).reshape(chunks * order, LANES)

    whole_chunk = own_rates.shape[1] == LANES
    unused = jnp.zeros((order, LANES), f32)
    series, ends = call(
        functools.partial(state_kernel, places, order),
        (
            jax.ShapeDtypeStruct((length * chunks, LANES), f32),
            jax.ShapeDtypeStruct((chunks * 2 * order, LANES), f32),
        ),
        decays,
        own_rates if whole_chunk else unused,
        own_residues if whole_chunk else unused,
        k_proj,
        value_projection,
        flops=2 * order * channels * length,
    )
    local_series, ends = lax.optimization_barrier((series, ends))
    ends = from_chunks(ends.reshape(chunks, 2 * order, LANES), blocks)
    if not whole_chunk:
        ends = ends.at[:, order:].set(weights_of(own_residues, own_rates))
    ends = all_to_all(ends, members)
    weights = to_chunks(ends).reshape(chunks * 2 * order, LANES)
    out_shape = jax.ShapeDtypeStruct((channels, length), jnp.bfloat16)
    out_scratch = [pltpu.VMEM(out_shape.shape, out_shape.dtype), pltpu.SemaphoreType.DMA((chunks,))]
    local, out = call(
        functools.partial(local_kernel, places, order),
        (
            jax.ShapeDtypeStruct((length * chunks, LANES), f32),
            out_shape,
        ),
        decays,
        weights,
        local_series,
        direct_gain.reshape(chunks, LANES),
        q_proj,
        out_spaces=(pltpu.VMEM, pl.ANY),
        scratch=out_scratch,
        flops=4 * order * channels * length,
    )
    starts = call(
        functools.partial(prefix_kernel, length, members),
        jax.ShapeDtypeStruct((blocks,) + own_rates.shape, f32),
        own_rates,
        ends,
    )
    starts = all_to_all(starts, members)
    carry = to_chunks(starts).reshape(chunks * order, LANES)
    return call(
        functools.partial(output_kernel, places, order),
        out_shape,
        decays,
        weights,
        carry,
        local,
        q_proj,
        out,
        out_spaces=pl.ANY,
        aliases={5: 0},
        scratch=[pltpu.VMEM((length * chunks, LANES), f32)] + out_scratch,
        flops=2 * order * channels * length,
    )


def solution(mesh):
    return jax.shard_map(
        functools.partial(shards, mesh.shape["seq"]),
        mesh=mesh,
        in_specs=(
            P("chan", ("groups", "seq")),
            P("chan", ("groups", "seq")),
            P("chan", ("groups", "seq")),
            P(("chan", "seq"), None),
            P(("chan", "seq"), None),
            P("chan"),
        ),
        out_specs=P("chan", ("groups", "seq")),
        check_vma=False,
    )
```

```python
import functools
import jax
import jax.numpy as jnp
from jax import lax
from jax.experimental import pallas as pl
from jax.experimental.pallas import tpu as pltpu
from jax.sharding import PartitionSpec as P

LANES = 128
SUBLANES = 8
UNROLL = 8
COPIES_COST = 10**10
PARTS = 4
VMEM_LIMIT = 32 * 1024 * 1024


def copies_kernel(rate_hbm, copies_ref, rate_ref, sem):
    load = pltpu.make_async_copy(rate_hbm, rate_ref, sem)
    load.start(priority=1)
    load.wait()
    decay = jnp.exp(-rate_ref[...])
    for piece in range(copies_ref.shape[0]):
        copies_ref[piece] = decay


def token_rows(half, length, token):
    row = (half * length + token) * SUBLANES
    return pl.ds(row if isinstance(row, int) else pl.multiple_of(row, SUBLANES), SUBLANES)


def chunk_rows(chunk, length):
    return pl.ds(chunk // SUBLANES * length * SUBLANES + chunk % SUBLANES, length, stride=SUBLANES)


def mode_rows(ref, base, order, per_chunk, chunks, half):
    first = half * SUBLANES * per_chunk + base
    return [ref[pl.ds(first + r, SUBLANES, stride=per_chunk), :] for r in range(order)]


def one_minus_exp(y):
    series = jnp.ones_like(y)
    for k in range(11, 1, -1):
        series = 1.0 - (y * (1.0 / k)) * series
    return jnp.where(y < 0.5, y * series, 1.0 - jnp.exp(-y))


def weights_of(residue, rate):
    return residue * jnp.sqrt(one_minus_exp(2.0 * rate))


def state_kernel(places, order, decays_ref, rate_ref, residue_ref, k_ref, v_ref, series_ref, state_ref):
    chunks, length = len(places), k_ref.shape[1]
    tokens = length // SUBLANES
    halves = chunks // SUBLANES

    def build(chunk):
        rows = pl.ds(places[chunk] * LANES, LANES)
        gated = k_ref[rows, :].astype(jnp.float32) * v_ref[rows, :].astype(jnp.float32)
        series_ref[chunk_rows(chunk, length), :] = gated.T

    weight = weights_of(residue_ref[...], rate_ref[...])
    for chunk in range(chunks):
        state_ref[pl.ds((2 * chunk + 1) * order, order), :] = weight
    for chunk in range(SUBLANES):
        build(chunk)
    for half in range(halves):
        decay = mode_rows(decays_ref, 0, order, order, chunks, half)
        square = [one * one for one in decay]

        def steps(i, state):
            state = list(state)
            for u in range(0, tokens, 2):
                x = series_ref[token_rows(half, length, i * tokens + u), :]
                y = series_ref[token_rows(half, length, i * tokens + u + 1), :]
                for r in range(order):
                    state[r] = square[r] * state[r] + (decay[r] * x + y)
            return tuple(state)

        state = (jnp.zeros((SUBLANES, LANES), jnp.float32),) * order
        if half + 1 < halves:
            for i in range(SUBLANES):
                state = steps(i, state)
                build((half + 1) * SUBLANES + i)
        else:
            state = lax.fori_loop(0, SUBLANES, steps, state)
        for r in range(order):
            state_ref[pl.ds(half * SUBLANES * 2 * order + r, SUBLANES, stride=2 * order), :] = state[r]


def prefix_kernel(length, members, rate_ref, ends_ref, starts_ref, held_ref, sems):
    span_decay = jnp.exp(-float(length) * rate_ref[...])
    carry = jnp.zeros(rate_ref.shape, jnp.float32)
    for block in range(len(members)):
        held_ref[members.index(block)] = carry
        carry = span_decay * carry + ends_ref[members.index(block), : rate_ref.shape[0]]
    part = max(len(members) // PARTS, 1)
    copies = []
    for i in range(0, len(members), part):
        rows = pl.ds(i, part)
        copies.append(pltpu.make_async_copy(held_ref.at[rows], starts_ref.at[rows], sems.at[i // part]))
    for i, copy in enumerate(copies):
        copy.start(priority=i % 2)
    for copy in copies:
        copy.wait()


def tree_sum(terms):
    terms = list(terms)
    while len(terms) > 1:
        terms = [terms[i] + terms[i + 1] if i + 1 < len(terms) else terms[i] for i in range(0, len(terms), 2)]
    return terms[0]


def leaving(chunk, places, gated_ref, out_ref, sems):
    rows = pl.ds(places[chunk] * LANES, LANES)
    return pltpu.make_async_copy(gated_ref.at[rows, :], out_ref.at[rows, :], sems.at[chunk])


def finish(chunk, places, conv_ref, q_ref, gated_ref, out_ref, sems):
    length = conv_ref.shape[0] // len(places)
    rows = pl.ds(places[chunk] * LANES, LANES)
    conv = conv_ref[chunk_rows(chunk, length), :].T
    gated_ref[rows, :] = (q_ref[rows, :].astype(jnp.float32) * conv).astype(jnp.bfloat16)
    leaving(chunk, places, gated_ref, out_ref, sems).start(priority=chunk % 2)


def local_kernel(
    places, order, decays_ref, weights_ref, series_ref, gain_ref, q_ref, conv_ref, out_ref, gated_ref, sems
):
    chunks = len(places)
    length = series_ref.shape[0] // chunks
    for half in range(chunks // SUBLANES):
        decay = mode_rows(decays_ref, 0, order, order, chunks, half)
        weight = mode_rows(weights_ref, order, order, 2 * order, chunks, half)
        own = places[half * SUBLANES : (half + 1) * SUBLANES]
        gain = jnp.concatenate([gain_ref[pl.ds(place, 1), :] for place in own], axis=0)

        def steps(i, state):
            state = list(state)
            for u in range(UNROLL):
                rows = token_rows(half, length, i * UNROLL + u)
                x = series_ref[rows, :]
                for r in range(order):
                    state[r] = decay[r] * state[r] + x
                terms = [weight[r] * state[r] for r in range(order)]
                conv_ref[rows, :] = tree_sum(terms + [gain * x])
            return tuple(state)

        zero = jnp.zeros((SUBLANES, LANES), jnp.float32)
        lax.fori_loop(0, length // UNROLL, steps, (zero,) * order)

    @pl.when(lax.axis_index("seq") == 0)
    def _():
        for chunk in range(chunks):
            finish(chunk, places, conv_ref, q_ref, gated_ref, out_ref, sems)
        for chunk in range(chunks):
            leaving(chunk, places, gated_ref, out_ref, sems).wait()


def output_kernel(
    places, order, decays_ref, weights_ref, carry_ref, local_ref, q_ref, _, out_ref, conv_ref, gated_ref, sems
):
    chunks = len(places)
    length = local_ref.shape[0] // chunks
    tokens = length // SUBLANES

    @pl.when(lax.axis_index("seq") > 0)
    def _():
        for half in range(chunks // SUBLANES):
            decay = mode_rows(decays_ref, 0, order, order, chunks, half)
            weight = mode_rows(weights_ref, order, order, 2 * order, chunks, half)
            carry = mode_rows(carry_ref, 0, order, order, chunks, half)

            def steps(i, fading):
                fading = list(fading)
                for u in range(tokens):
                    rows = token_rows(half, length, i * tokens + u)
                    fading = [decay[r] * fading[r] for r in range(order)]
                    conv_ref[rows, :] = tree_sum(fading + [local_ref[rows, :]])
                return tuple(fading)

            fading = tuple(weight[r] * carry[r] for r in range(order))
            if half == 0:
                lax.fori_loop(0, SUBLANES, steps, fading)
            else:
                for i in range(SUBLANES):
                    fading = steps(i, fading)
                    finish((half - 1) * SUBLANES + i, places, conv_ref, q_ref, gated_ref, out_ref, sems)
        for chunk in range(chunks - SUBLANES, chunks):
            finish(chunk, places, conv_ref, q_ref, gated_ref, out_ref, sems)
        for chunk in range(chunks):
            leaving(chunk, places, gated_ref, out_ref, sems).wait()


def call(kernel, out_shape, *args, in_spaces=None, out_spaces=None, aliases=None, scratch=(), flops=0):
    in_bytes = sum(a.size * a.dtype.itemsize for a in args)
    in_spaces = in_spaces or [pl.ANY if i in (aliases or {}) else pltpu.VMEM for i in range(len(args))]
    out_spaces = out_spaces or jax.tree.map(lambda _: pltpu.VMEM, out_shape)
    return pl.pallas_call(
        kernel,
        out_shape=out_shape,
        in_specs=[pl.BlockSpec(memory_space=space) for space in in_spaces],
        out_specs=jax.tree.map(lambda space: pl.BlockSpec(memory_space=space), out_spaces),
        scratch_shapes=list(scratch),
        input_output_aliases=aliases or {},
        compiler_params=pltpu.CompilerParams(vmem_limit_bytes=VMEM_LIMIT),
        cost_estimate=pl.CostEstimate(flops=flops, bytes_accessed=in_bytes, transcendentals=0),
    )(*args)


def to_chunks(pieces):
    owners, rows, own = pieces.shape
    if own == LANES:
        return pieces
    if own < LANES:
        group = LANES // own
        return pieces.reshape(owners // group, group, rows, own).swapaxes(1, 2).reshape(-1, rows, LANES)
    return pieces.reshape(owners, rows, own // LANES, LANES).swapaxes(1, 2).reshape(-1, rows, LANES)


def from_chunks(pieces, owners):
    chunks, rows, _ = pieces.shape
    own = chunks * LANES // owners
    if own == LANES:
        return pieces
    if own < LANES:
        group = LANES // own
        return pieces.reshape(chunks, rows, group, own).swapaxes(1, 2).reshape(owners, rows, own)
    return pieces.reshape(owners, own // LANES, rows, LANES).swapaxes(1, 2).reshape(owners, rows, own)


def all_to_all(pieces, members):
    return lax.all_to_all(pieces, "seq", split_axis=0, concat_axis=0, axis_index_groups=[members], tiled=True)


def shards(blocks, q_proj, k_proj, value_projection, residues, rates, direct_gain):
    channels, length = q_proj.shape
    order = residues.shape[1]
    chunks = channels // LANES
    f32 = jnp.float32

    members, places = list(range(blocks)), list(range(chunks))
    if blocks == chunks:
        far, middle = blocks // 2, blocks * 11 // 16
        upper = [middle] + [block for block in members[:far - 1:-1] if block != middle]
        members = [block for one in upper for block in (one, one - far)]
        places = list(members)

    own_rates, own_residues = rates.T, residues.T
    copies = call(
        copies_kernel,
        jax.ShapeDtypeStruct((blocks,) + own_rates.shape, f32),
        pltpu.with_memory_space_constraint(own_rates, pltpu.HBM),
        in_spaces=[pl.ANY],
        scratch=[pltpu.VMEM(own_rates.shape, f32), pltpu.SemaphoreType.DMA],
        flops=COPIES_COST,
    )
    decays = to_chunks(all_to_all(copies, members)).reshape(chunks * order, LANES)

    whole_chunk = own_rates.shape[1] == LANES
    unused = jnp.zeros((order, LANES), f32)
    series, ends = call(
        functools.partial(state_kernel, places, order),
        (
            jax.ShapeDtypeStruct((length * chunks, LANES), f32),
            jax.ShapeDtypeStruct((chunks * 2 * order, LANES), f32),
        ),
        decays,
        own_rates if whole_chunk else unused,
        own_residues if whole_chunk else unused,
        k_proj,
        value_projection,
        flops=2 * order * channels * length,
    )
    local_series, ends = lax.optimization_barrier((series, ends))
    ends = from_chunks(ends.reshape(chunks, 2 * order, LANES), blocks)
    if not whole_chunk:
        ends = ends.at[:, order:].set(weights_of(own_residues, own_rates))
    ends = all_to_all(ends, members)
    weights = to_chunks(ends).reshape(chunks * 2 * order, LANES)
    out_shape = jax.ShapeDtypeStruct((channels, length), jnp.bfloat16)
    out_scratch = [pltpu.VMEM(out_shape.shape, out_shape.dtype), pltpu.SemaphoreType.DMA((chunks,))]
    local, out = call(
        functools.partial(local_kernel, places, order),
        (
            jax.ShapeDtypeStruct((length * chunks, LANES), f32),
            out_shape,
        ),
        decays,
        weights,
        local_series,
        direct_gain.reshape(chunks, LANES),
        q_proj,
        out_spaces=(pltpu.VMEM, pl.ANY),
        scratch=out_scratch,
        flops=4 * order * channels * length,
    )
    starts = call(
        functools.partial(prefix_kernel, length, members),
        jax.ShapeDtypeStruct((blocks,) + own_rates.shape, f32),
        own_rates,
        ends,
        out_spaces=pl.ANY,
        scratch=[pltpu.VMEM((blocks,) + own_rates.shape, f32), pltpu.SemaphoreType.DMA((PARTS,))],
    )
    starts = all_to_all(starts, members)
    carry = to_chunks(starts).reshape(chunks * order, LANES)
    return call(
        functools.partial(output_kernel, places, order),
        out_shape,
        decays,
        weights,
        carry,
        local,
        q_proj,
        out,
        out_spaces=pl.ANY,
        aliases={5: 0},
        scratch=[pltpu.VMEM((length * chunks, LANES), f32)] + out_scratch,
        flops=2 * order * channels * length,
    )


def solution(mesh):
    return jax.shard_map(
        functools.partial(shards, mesh.shape["seq"]),
        mesh=mesh,
        in_specs=(
            P("chan", ("groups", "seq")),
            P("chan", ("groups", "seq")),
            P("chan", ("groups", "seq")),
            P(("chan", "seq"), None),
            P(("chan", "seq"), None),
            P("chan"),
        ),
        out_specs=P("chan", ("groups", "seq")),
        check_vma=False,
    )
```

```python
import functools
import jax
import jax.numpy as jnp
from jax import lax
from jax.experimental import pallas as pl
from jax.experimental.pallas import tpu as pltpu
from jax.sharding import PartitionSpec as P

LANES = 128
SUBLANES = 8
UNROLL = 8
COPIES_COST = 10**10
VMEM_LIMIT = 32 * 1024 * 1024


def copies_kernel(rate_hbm, copies_ref, rate_ref, sem):
    load = pltpu.make_async_copy(rate_hbm, rate_ref, sem)
    load.start()
    load.wait()
    decay = jnp.exp(-rate_ref[...])
    for piece in range(copies_ref.shape[0]):
        copies_ref[piece] = decay


def token_rows(half, length, token):
    row = (half * length + token) * SUBLANES
    return pl.ds(row if isinstance(row, int) else pl.multiple_of(row, SUBLANES), SUBLANES)


def chunk_rows(chunk, length):
    return pl.ds(chunk // SUBLANES * length * SUBLANES + chunk % SUBLANES, length, stride=SUBLANES)


def mode_rows(ref, base, order, per_chunk, chunks, half):
    first = half * SUBLANES * per_chunk + base
    return [ref[pl.ds(first + r, SUBLANES, stride=per_chunk), :] for r in range(order)]


def one_minus_exp(y):
    series = jnp.ones_like(y)
    for k in range(11, 1, -1):
        series = 1.0 - (y * (1.0 / k)) * series
    return jnp.where(y < 0.5, y * series, 1.0 - jnp.exp(-y))


def weights_of(residue, rate):
    return residue * jnp.sqrt(one_minus_exp(2.0 * rate))


def state_kernel(places, order, decays_ref, rate_ref, residue_ref, k_ref, v_ref, series_ref, state_ref):
    chunks, length = len(places), k_ref.shape[1]
    tokens = length // SUBLANES
    halves = chunks // SUBLANES

    def build(chunk):
        rows = pl.ds(places[chunk] * LANES, LANES)
        gated = k_ref[rows, :].astype(jnp.float32) * v_ref[rows, :].astype(jnp.float32)
        series_ref[chunk_rows(chunk, length), :] = gated.T

    weight = weights_of(residue_ref[...], rate_ref[...])
    for chunk in range(chunks):
        state_ref[pl.ds((2 * chunk + 1) * order, order), :] = weight
    for chunk in range(SUBLANES):
        build(chunk)
    for half in range(halves):
        decay = mode_rows(decays_ref, 0, order, order, chunks, half)
        square = [one * one for one in decay]

        def steps(i, state):
            state = list(state)
            for u in range(0, tokens, 2):
                x = series_ref[token_rows(half, length, i * tokens + u), :]
                y = series_ref[token_rows(half, length, i * tokens + u + 1), :]
                for r in range(order):
                    state[r] = square[r] * state[r] + (decay[r] * x + y)
            return tuple(state)

        state = (jnp.zeros((SUBLANES, LANES), jnp.float32),) * order
        if half + 1 < halves:
            for i in range(SUBLANES):
                state = steps(i, state)
                build((half + 1) * SUBLANES + i)
        else:
            state = lax.fori_loop(0, SUBLANES, steps, state)
        for r in range(order):
            state_ref[pl.ds(half * SUBLANES * 2 * order + r, SUBLANES, stride=2 * order), :] = state[r]


def prefix_kernel(length, members, rate_ref, ends_ref, starts_ref):
    span_decay = jnp.exp(-float(length) * rate_ref[...])
    carry = jnp.zeros(rate_ref.shape, jnp.float32)
    for block in range(len(members)):
        starts_ref[members.index(block)] = carry
        carry = span_decay * carry + ends_ref[members.index(block), : rate_ref.shape[0]]


def tree_sum(terms):
    terms = list(terms)
    while len(terms) > 1:
        terms = [terms[i] + terms[i + 1] if i + 1 < len(terms) else terms[i] for i in range(0, len(terms), 2)]
    return terms[0]


def leaving(chunk, places, gated_ref, out_ref, sems):
    rows = pl.ds(places[chunk] * LANES, LANES)
    return pltpu.make_async_copy(gated_ref.at[rows, :], out_ref.at[rows, :], sems.at[chunk])


def finish(chunk, places, conv_ref, q_ref, gated_ref, out_ref, sems):
    length = conv_ref.shape[0] // len(places)
    rows = pl.ds(places[chunk] * LANES, LANES)
    conv = conv_ref[chunk_rows(chunk, length), :].T
    gated_ref[rows, :] = (q_ref[rows, :].astype(jnp.float32) * conv).astype(jnp.bfloat16)
    leaving(chunk, places, gated_ref, out_ref, sems).start()


def local_kernel(
    places, order, decays_ref, weights_ref, series_ref, gain_ref, q_ref, conv_ref, dense_ref, out_ref, gated_ref, sems
):
    chunks = len(places)
    length = series_ref.shape[0] // chunks
    for half in range(chunks // SUBLANES):
        decay = mode_rows(decays_ref, 0, order, order, chunks, half)
        weight = mode_rows(weights_ref, order, order, 2 * order, chunks, half)
        for r in range(order):
            dense_ref[half, 0, r] = decay[r]
            dense_ref[half, 1, r] = weight[r]
        own = places[half * SUBLANES : (half + 1) * SUBLANES]
        gain = jnp.concatenate([gain_ref[pl.ds(place, 1), :] for place in own], axis=0)

        def steps(i, state):
            state = list(state)
            for u in range(UNROLL):
                rows = token_rows(half, length, i * UNROLL + u)
                x = series_ref[rows, :]
                for r in range(order):
                    state[r] = decay[r] * state[r] + x
                terms = [weight[r] * state[r] for r in range(order)]
                conv_ref[rows, :] = tree_sum(terms + [gain * x])
            return tuple(state)

        zero = jnp.zeros((SUBLANES, LANES), jnp.float32)
        lax.fori_loop(0, length // UNROLL, steps, (zero,) * order)

    @pl.when(lax.axis_index("seq") == 0)
    def _():
        for chunk in range(chunks):
            finish(chunk, places, conv_ref, q_ref, gated_ref, out_ref, sems)
        for chunk in range(chunks):
            leaving(chunk, places, gated_ref, out_ref, sems).wait()


def output_kernel(
    places, order, dense_ref, carry_ref, local_ref, q_ref, _, out_ref, conv_ref, gated_ref, sems
):
    chunks = len(places)
    length = local_ref.shape[0] // chunks
    tokens = length // SUBLANES

    @pl.when(lax.axis_index("seq") > 0)
    def _():
        for half in range(chunks // SUBLANES):
            decay = [dense_ref[half, 0, r] for r in range(order)]
            weight = [dense_ref[half, 1, r] for r in range(order)]
            carry = mode_rows(carry_ref, 0, order, order, chunks, half)

            def steps(i, fading):
                fading = list(fading)
                for u in range(tokens):
                    rows = token_rows(half, length, i * tokens + u)
                    fading = [decay[r] * fading[r] for r in range(order)]
                    conv_ref[rows, :] = tree_sum(fading + [local_ref[rows, :]])
                return tuple(fading)

            fading = tuple(weight[r] * carry[r] for r in range(order))
            if half == 0:
                lax.fori_loop(0, SUBLANES, steps, fading)
            else:
                for i in range(SUBLANES):
                    fading = steps(i, fading)
                    finish((half - 1) * SUBLANES + i, places, conv_ref, q_ref, gated_ref, out_ref, sems)
        for chunk in range(chunks - SUBLANES, chunks):
            finish(chunk, places, conv_ref, q_ref, gated_ref, out_ref, sems)
        for chunk in range(chunks):
            leaving(chunk, places, gated_ref, out_ref, sems).wait()


def call(kernel, out_shape, *args, in_spaces=None, out_spaces=None, aliases=None, scratch=(), flops=0):
    in_bytes = sum(a.size * a.dtype.itemsize for a in args)
    in_spaces = in_spaces or [pl.ANY if i in (aliases or {}) else pltpu.VMEM for i in range(len(args))]
    out_spaces = out_spaces or jax.tree.map(lambda _: pltpu.VMEM, out_shape)
    return pl.pallas_call(
        kernel,
        out_shape=out_shape,
        in_specs=[pl.BlockSpec(memory_space=space) for space in in_spaces],
        out_specs=jax.tree.map(lambda space: pl.BlockSpec(memory_space=space), out_spaces),
        scratch_shapes=list(scratch),
        input_output_aliases=aliases or {},
        compiler_params=pltpu.CompilerParams(vmem_limit_bytes=VMEM_LIMIT),
        cost_estimate=pl.CostEstimate(flops=flops, bytes_accessed=in_bytes, transcendentals=0),
    )(*args)


def to_chunks(pieces):
    owners, rows, own = pieces.shape
    if own == LANES:
        return pieces
    if own < LANES:
        group = LANES // own
        return pieces.reshape(owners // group, group, rows, own).swapaxes(1, 2).reshape(-1, rows, LANES)
    return pieces.reshape(owners, rows, own // LANES, LANES).swapaxes(1, 2).reshape(-1, rows, LANES)


def from_chunks(pieces, owners):
    chunks, rows, _ = pieces.shape
    own = chunks * LANES // owners
    if own == LANES:
        return pieces
    if own < LANES:
        group = LANES // own
        return pieces.reshape(chunks, rows, group, own).swapaxes(1, 2).reshape(owners, rows, own)
    return pieces.reshape(owners, own // LANES, rows, LANES).swapaxes(1, 2).reshape(owners, rows, own)


def all_to_all(pieces, members):
    return lax.all_to_all(pieces, "seq", split_axis=0, concat_axis=0, axis_index_groups=[members], tiled=True)


def shards(blocks, q_proj, k_proj, value_projection, residues, rates, direct_gain):
    channels, length = q_proj.shape
    order = residues.shape[1]
    chunks = channels // LANES
    f32 = jnp.float32

    members, places = list(range(blocks)), list(range(chunks))
    if blocks == chunks:
        far, middle = blocks // 2, blocks * 11 // 16
        upper = [middle] + [block for block in members[:far - 1:-1] if block != middle]
        members = [block for one in upper for block in (one, one - far)]
        places = list(members)

    own_rates, own_residues = rates.T, residues.T
    copies = call(
        copies_kernel,
        jax.ShapeDtypeStruct((blocks,) + own_rates.shape, f32),
        pltpu.with_memory_space_constraint(own_rates, pltpu.HBM),
        in_spaces=[pl.ANY],
        scratch=[pltpu.VMEM(own_rates.shape, f32), pltpu.SemaphoreType.DMA],
        flops=COPIES_COST,
    )
    decays = to_chunks(all_to_all(copies, members)).reshape(chunks * order, LANES)

    whole_chunk = own_rates.shape[1] == LANES
    unused = jnp.zeros((order, LANES), f32)
    series, ends = call(
        functools.partial(state_kernel, places, order),
        (
            jax.ShapeDtypeStruct((length * chunks, LANES), f32),
            jax.ShapeDtypeStruct((chunks * 2 * order, LANES), f32),
        ),
        decays,
        own_rates if whole_chunk else unused,
        own_residues if whole_chunk else unused,
        k_proj,
        value_projection,
        flops=2 * order * channels * length,
    )
    local_series, ends = lax.optimization_barrier((series, ends))
    ends = from_chunks(ends.reshape(chunks, 2 * order, LANES), blocks)
    if not whole_chunk:
        ends = ends.at[:, order:].set(weights_of(own_residues, own_rates))
    ends = all_to_all(ends, members)
    weights = to_chunks(ends).reshape(chunks * 2 * order, LANES)
    out_shape = jax.ShapeDtypeStruct((channels, length), jnp.bfloat16)
    out_scratch = [pltpu.VMEM(out_shape.shape, out_shape.dtype), pltpu.SemaphoreType.DMA((chunks,))]
    local, dense, out = call(
        functools.partial(local_kernel, places, order),
        (
            jax.ShapeDtypeStruct((length * chunks, LANES), f32),
            jax.ShapeDtypeStruct((chunks // SUBLANES, 2, order, SUBLANES, LANES), f32),
            out_shape,
        ),
        decays,
        weights,
        local_series,
        direct_gain.reshape(chunks, LANES),
        q_proj,
        out_spaces=(pltpu.VMEM, pltpu.VMEM, pl.ANY),
        scratch=out_scratch,
        flops=4 * order * channels * length,
    )
    starts = call(
        functools.partial(prefix_kernel, length, members),
        jax.ShapeDtypeStruct((blocks,) + own_rates.shape, f32),
        own_rates,
        ends,
    )
    starts = all_to_all(starts, members)
    carry = to_chunks(starts).reshape(chunks * order, LANES)
    return call(
        functools.partial(output_kernel, places, order),
        out_shape,
        dense,
        carry,
        local,
        q_proj,
        out,
        out_spaces=pl.ANY,
        aliases={4: 0},
        scratch=[pltpu.VMEM((length * chunks, LANES), f32)] + out_scratch,
        flops=2 * order * channels * length,
    )


def solution(mesh):
    return jax.shard_map(
        functools.partial(shards, mesh.shape["seq"]),
        mesh=mesh,
        in_specs=(
            P("chan", ("groups", "seq")),
            P("chan", ("groups", "seq")),
            P("chan", ("groups", "seq")),
            P(("chan", "seq"), None),
            P(("chan", "seq"), None),
            P("chan"),
        ),
        out_specs=P("chan", ("groups", "seq")),
        check_vma=False,
    )
```

```python
import functools
import jax
import jax.numpy as jnp
from jax import lax
from jax.experimental import pallas as pl
from jax.experimental.pallas import tpu as pltpu
from jax.sharding import PartitionSpec as P

LANES = 128
SUBLANES = 8
UNROLL = 8
COPIES_COST = 10**10
VMEM_LIMIT = 32 * 1024 * 1024


def copies_kernel(rate_hbm, copies_ref, rate_ref, sem):
    load = pltpu.make_async_copy(rate_hbm, rate_ref, sem)
    load.start()
    load.wait()
    decay = jnp.exp(-rate_ref[...])
    for piece in range(copies_ref.shape[0]):
        copies_ref[piece] = decay


def token_rows(half, length, token):
    row = (half * length + token) * SUBLANES
    return pl.ds(row if isinstance(row, int) else pl.multiple_of(row, SUBLANES), SUBLANES)


def chunk_rows(chunk, length):
    return pl.ds(chunk // SUBLANES * length * SUBLANES + chunk % SUBLANES, length, stride=SUBLANES)


def mode_rows(ref, base, order, per_chunk, chunks, half):
    first = half * SUBLANES * per_chunk + base
    return [ref[pl.ds(first + r, SUBLANES, stride=per_chunk), :] for r in range(order)]


def one_minus_exp(y):
    series = jnp.ones_like(y)
    for k in range(11, 1, -1):
        series = 1.0 - (y * (1.0 / k)) * series
    return jnp.where(y < 0.5, y * series, 1.0 - jnp.exp(-y))


def weights_of(residue, rate):
    return residue * jnp.sqrt(one_minus_exp(2.0 * rate))


def state_kernel(places, order, decays_ref, rate_ref, residue_ref, k_ref, v_ref, series_ref, state_ref):
    chunks, length = len(places), k_ref.shape[1]
    tokens = length // SUBLANES
    halves = chunks // SUBLANES

    def build(chunk):
        rows = pl.ds(places[chunk] * LANES, LANES)
        gated = k_ref[rows, :].astype(jnp.float32) * v_ref[rows, :].astype(jnp.float32)
        series_ref[chunk_rows(chunk, length), :] = gated.T

    weight = weights_of(residue_ref[...], rate_ref[...])
    for chunk in range(chunks):
        state_ref[pl.ds((2 * chunk + 1) * order, order), :] = weight
    for chunk in range(SUBLANES):
        build(chunk)
    for half in range(halves):
        decay = mode_rows(decays_ref, 0, order, order, chunks, half)
        square = [one * one for one in decay]

        def steps(i, state):
            state = list(state)
            for u in range(0, tokens, 2):
                x = series_ref[token_rows(half, length, i * tokens + u), :]
                y = series_ref[token_rows(half, length, i * tokens + u + 1), :]
                for r in range(order):
                    state[r] = square[r] * state[r] + (decay[r] * x + y)
            return tuple(state)

        state = (jnp.zeros((SUBLANES, LANES), jnp.float32),) * order
        if half + 1 < halves:
            for i in range(SUBLANES):
                state = steps(i, state)
                build((half + 1) * SUBLANES + i)
        else:
            state = lax.fori_loop(0, SUBLANES, steps, state)
        for r in range(order):
            state_ref[pl.ds(half * SUBLANES * 2 * order + r, SUBLANES, stride=2 * order), :] = state[r]


def prefix_kernel(length, members, rate_ref, ends_ref, starts_ref):
    span_decay = jnp.exp(-float(length) * rate_ref[...])
    carry = jnp.zeros(rate_ref.shape, jnp.float32)
    for block in range(len(members)):
        starts_ref[members.index(block)] = carry
        carry = span_decay * carry + ends_ref[members.index(block), : rate_ref.shape[0]]


def tree_sum(terms):
    terms = list(terms)
    while len(terms) > 1:
        terms = [terms[i] + terms[i + 1] if i + 1 < len(terms) else terms[i] for i in range(0, len(terms), 2)]
    return terms[0]


def leaving(chunk, places, gated_ref, out_ref, sems):
    rows = pl.ds(places[chunk] * LANES, LANES)
    return pltpu.make_async_copy(gated_ref.at[rows, :], out_ref.at[rows, :], sems.at[chunk])


def finish(chunk, places, conv, q_ref, gated_ref, out_ref, sems):
    rows = pl.ds(places[chunk] * LANES, LANES)
    gated_ref[rows, :] = (q_ref[rows, :].astype(jnp.float32) * conv.T).astype(jnp.bfloat16)
    leaving(chunk, places, gated_ref, out_ref, sems).start()


def local_kernel(
    places, order, decays_ref, weights_ref, series_ref, gain_ref, q_ref, conv_ref, dense_ref, out_ref, gated_ref, sems
):
    chunks = len(places)
    length = series_ref.shape[0] // chunks
    for half in range(chunks // SUBLANES):
        decay = mode_rows(decays_ref, 0, order, order, chunks, half)
        weight = mode_rows(weights_ref, order, order, 2 * order, chunks, half)
        for r in range(order):
            dense_ref[half, 0, r] = decay[r]
            dense_ref[half, 1, r] = weight[r]
        own = places[half * SUBLANES : (half + 1) * SUBLANES]
        gain = jnp.concatenate([gain_ref[pl.ds(place, 1), :] for place in own], axis=0)

        def steps(i, state):
            state = list(state)
            for u in range(UNROLL):
                rows = token_rows(half, length, i * UNROLL + u)
                x = series_ref[rows, :]
                for r in range(order):
                    state[r] = decay[r] * state[r] + x
                terms = [weight[r] * state[r] for r in range(order)]
                conv_ref[rows, :] = tree_sum(terms + [gain * x])
            return tuple(state)

        zero = jnp.zeros((SUBLANES, LANES), jnp.float32)
        lax.fori_loop(0, length // UNROLL, steps, (zero,) * order)

    @pl.when(lax.axis_index("seq") == 0)
    def _():
        for chunk in range(chunks):
            finish(chunk, places, conv_ref[chunk_rows(chunk, length), :], q_ref, gated_ref, out_ref, sems)
        for chunk in range(chunks):
            leaving(chunk, places, gated_ref, out_ref, sems).wait()


def output_kernel(
    places, order, dense_ref, carry_ref, local_ref, q_ref, _, out_ref, conv_ref, gated_ref, sems
):
    chunks = len(places)
    length = local_ref.shape[0] // chunks
    tokens = length // SUBLANES

    def send(chunk):
        conv = conv_ref[pl.ds(chunk * length, length), :]
        finish(chunk, places, conv, q_ref, gated_ref, out_ref, sems)

    @pl.when(lax.axis_index("seq") > 0)
    def _():
        for half in range(chunks // SUBLANES):
            decay = [dense_ref[half, 0, r] for r in range(order)]
            weight = [dense_ref[half, 1, r] for r in range(order)]
            carry = mode_rows(carry_ref, 0, order, order, chunks, half)
            fading = [weight[r] * carry[r] for r in range(order)]
            for token in range(length):
                fading = [decay[r] * fading[r] for r in range(order)]
                total = tree_sum(fading + [local_ref[token_rows(half, length, token), :]])
                conv_ref[pl.ds(half * SUBLANES * length + token, SUBLANES, stride=length), :] = total
                if half > 0 and token % tokens == tokens - 1:
                    send((half - 1) * SUBLANES + token // tokens)
        for chunk in range(chunks - SUBLANES, chunks):
            send(chunk)
        for chunk in range(chunks):
            leaving(chunk, places, gated_ref, out_ref, sems).wait()


def call(kernel, out_shape, *args, in_spaces=None, out_spaces=None, aliases=None, scratch=(), flops=0):
    in_bytes = sum(a.size * a.dtype.itemsize for a in args)
    in_spaces = in_spaces or [pl.ANY if i in (aliases or {}) else pltpu.VMEM for i in range(len(args))]
    out_spaces = out_spaces or jax.tree.map(lambda _: pltpu.VMEM, out_shape)
    return pl.pallas_call(
        kernel,
        out_shape=out_shape,
        in_specs=[pl.BlockSpec(memory_space=space) for space in in_spaces],
        out_specs=jax.tree.map(lambda space: pl.BlockSpec(memory_space=space), out_spaces),
        scratch_shapes=list(scratch),
        input_output_aliases=aliases or {},
        compiler_params=pltpu.CompilerParams(vmem_limit_bytes=VMEM_LIMIT),
        cost_estimate=pl.CostEstimate(flops=flops, bytes_accessed=in_bytes, transcendentals=0),
    )(*args)


def to_chunks(pieces):
    owners, rows, own = pieces.shape
    if own == LANES:
        return pieces
    if own < LANES:
        group = LANES // own
        return pieces.reshape(owners // group, group, rows, own).swapaxes(1, 2).reshape(-1, rows, LANES)
    return pieces.reshape(owners, rows, own // LANES, LANES).swapaxes(1, 2).reshape(-1, rows, LANES)


def from_chunks(pieces, owners):
    chunks, rows, _ = pieces.shape
    own = chunks * LANES // owners
    if own == LANES:
        return pieces
    if own < LANES:
        group = LANES // own
        return pieces.reshape(chunks, rows, group, own).swapaxes(1, 2).reshape(owners, rows, own)
    return pieces.reshape(owners, own // LANES, rows, LANES).swapaxes(1, 2).reshape(owners, rows, own)


def all_to_all(pieces, members):
    return lax.all_to_all(pieces, "seq", split_axis=0, concat_axis=0, axis_index_groups=[members], tiled=True)


def shards(blocks, q_proj, k_proj, value_projection, residues, rates, direct_gain):
    channels, length = q_proj.shape
    order = residues.shape[1]
    chunks = channels // LANES
    f32 = jnp.float32

    members, places = list(range(blocks)), list(range(chunks))
    if blocks == chunks:
        far, middle = blocks // 2, blocks * 11 // 16
        upper = [middle] + [block for block in members[:far - 1:-1] if block != middle]
        members = [block for one in upper for block in (one, one - far)]
        places = list(members)

    own_rates, own_residues = rates.T, residues.T
    copies = call(
        copies_kernel,
        jax.ShapeDtypeStruct((blocks,) + own_rates.shape, f32),
        pltpu.with_memory_space_constraint(own_rates, pltpu.HBM),
        in_spaces=[pl.ANY],
        scratch=[pltpu.VMEM(own_rates.shape, f32), pltpu.SemaphoreType.DMA],
        flops=COPIES_COST,
    )
    decays = to_chunks(all_to_all(copies, members)).reshape(chunks * order, LANES)

    whole_chunk = own_rates.shape[1] == LANES
    unused = jnp.zeros((order, LANES), f32)
    series, ends = call(
        functools.partial(state_kernel, places, order),
        (
            jax.ShapeDtypeStruct((length * chunks, LANES), f32),
            jax.ShapeDtypeStruct((chunks * 2 * order, LANES), f32),
        ),
        decays,
        own_rates if whole_chunk else unused,
        own_residues if whole_chunk else unused,
        k_proj,
        value_projection,
        flops=2 * order * channels * length,
    )
    local_series, ends = lax.optimization_barrier((series, ends))
    ends = from_chunks(ends.reshape(chunks, 2 * order, LANES), blocks)
    if not whole_chunk:
        ends = ends.at[:, order:].set(weights_of(own_residues, own_rates))
    ends = all_to_all(ends, members)
    weights = to_chunks(ends).reshape(chunks * 2 * order, LANES)
    out_shape = jax.ShapeDtypeStruct((channels, length), jnp.bfloat16)
    out_scratch = [pltpu.VMEM(out_shape.shape, out_shape.dtype), pltpu.SemaphoreType.DMA((chunks,))]
    local, dense, out = call(
        functools.partial(local_kernel, places, order),
        (
            jax.ShapeDtypeStruct((length * chunks, LANES), f32),
            jax.ShapeDtypeStruct((chunks // SUBLANES, 2, order, SUBLANES, LANES), f32),
            out_shape,
        ),
        decays,
        weights,
        local_series,
        direct_gain.reshape(chunks, LANES),
        q_proj,
        out_spaces=(pltpu.VMEM, pltpu.VMEM, pl.ANY),
        scratch=out_scratch,
        flops=4 * order * channels * length,
    )
    starts = call(
        functools.partial(prefix_kernel, length, members),
        jax.ShapeDtypeStruct((blocks,) + own_rates.shape, f32),
        own_rates,
        ends,
    )
    starts = all_to_all(starts, members)
    carry = to_chunks(starts).reshape(chunks * order, LANES)
    return call(
        functools.partial(output_kernel, places, order),
        out_shape,
        dense,
        carry,
        local,
        q_proj,
        out,
        out_spaces=pl.ANY,
        aliases={4: 0},
        scratch=[pltpu.VMEM((length * chunks, LANES), f32)] + out_scratch,
        flops=2 * order * channels * length,
    )


def solution(mesh):
    return jax.shard_map(
        functools.partial(shards, mesh.shape["seq"]),
        mesh=mesh,
        in_specs=(
            P("chan", ("groups", "seq")),
            P("chan", ("groups", "seq")),
            P("chan", ("groups", "seq")),
            P(("chan", "seq"), None),
            P(("chan", "seq"), None),
            P("chan"),
        ),
        out_specs=P("chan", ("groups", "seq")),
        check_vma=False,
    )
```

```python
import functools
import jax
import jax.numpy as jnp
from jax import lax
from jax.experimental import pallas as pl
from jax.experimental.pallas import tpu as pltpu
from jax.sharding import PartitionSpec as P

LANES = 128
SUBLANES = 8
UNROLL = 8
COPIES_COST = 10**10
FAR_FIRST = (11, 0, 12, 4, 8, 2, 14, 1, 13, 3, 9, 6, 10, 5, 15, 7)
VMEM_LIMIT = 32 * 1024 * 1024


def copies_kernel(rate_hbm, copies_ref, rate_ref, sem):
    load = pltpu.make_async_copy(rate_hbm, rate_ref, sem)
    load.start()
    load.wait()
    decay = jnp.exp(-rate_ref[...])
    for piece in range(copies_ref.shape[0]):
        copies_ref[piece] = decay


def token_rows(half, length, token):
    row = (half * length + token) * SUBLANES
    return pl.ds(row if isinstance(row, int) else pl.multiple_of(row, SUBLANES), SUBLANES)


def chunk_rows(chunk, length):
    return pl.ds(chunk // SUBLANES * length * SUBLANES + chunk % SUBLANES, length, stride=SUBLANES)


def mode_rows(ref, base, order, per_chunk, chunks, half):
    first = half * SUBLANES * per_chunk + base
    return [ref[pl.ds(first + r, SUBLANES, stride=per_chunk), :] for r in range(order)]


def one_minus_exp(y):
    series = jnp.ones_like(y)
    for k in range(11, 1, -1):
        series = 1.0 - (y * (1.0 / k)) * series
    return jnp.where(y < 0.5, y * series, 1.0 - jnp.exp(-y))


def weights_of(residue, rate):
    return residue * jnp.sqrt(one_minus_exp(2.0 * rate))


def state_kernel(places, order, decays_ref, rate_ref, residue_ref, k_ref, v_ref, series_ref, state_ref):
    chunks, length = len(places), k_ref.shape[1]
    tokens = length // SUBLANES
    halves = chunks // SUBLANES

    def build(chunk):
        rows = pl.ds(places[chunk] * LANES, LANES)
        gated = k_ref[rows, :].astype(jnp.float32) * v_ref[rows, :].astype(jnp.float32)
        series_ref[chunk_rows(chunk, length), :] = gated.T

    weight = weights_of(residue_ref[...], rate_ref[...])
    for chunk in range(chunks):
        state_ref[pl.ds((2 * chunk + 1) * order, order), :] = weight
    for chunk in range(SUBLANES):
        build(chunk)
    for half in range(halves):
        decay = mode_rows(decays_ref, 0, order, order, chunks, half)
        square = [one * one for one in decay]

        def steps(i, state):
            state = list(state)
            for u in range(0, tokens, 2):
                x = series_ref[token_rows(half, length, i * tokens + u), :]
                y = series_ref[token_rows(half, length, i * tokens + u + 1), :]
                for r in range(order):
                    state[r] = square[r] * state[r] + (decay[r] * x + y)
            return tuple(state)

        state = (jnp.zeros((SUBLANES, LANES), jnp.float32),) * order
        if half + 1 < halves:
            for i in range(SUBLANES):
                state = steps(i, state)
                build((half + 1) * SUBLANES + i)
        else:
            state = lax.fori_loop(0, SUBLANES, steps, state)
        for r in range(order):
            state_ref[pl.ds(half * SUBLANES * 2 * order + r, SUBLANES, stride=2 * order), :] = state[r]


def prefix_kernel(length, members, rate_ref, ends_ref, starts_ref):
    span_decay = jnp.exp(-float(length) * rate_ref[...])
    carry = jnp.zeros(rate_ref.shape, jnp.float32)
    for block in range(len(members)):
        starts_ref[members.index(block)] = carry
        carry = span_decay * carry + ends_ref[members.index(block), : rate_ref.shape[0]]


def tree_sum(terms):
    terms = list(terms)
    while len(terms) > 1:
        terms = [terms[i] + terms[i + 1] if i + 1 < len(terms) else terms[i] for i in range(0, len(terms), 2)]
    return terms[0]


def leaving(chunk, places, gated_ref, out_ref, sems):
    rows = pl.ds(places[chunk] * LANES, LANES)
    return pltpu.make_async_copy(gated_ref.at[rows, :], out_ref.at[rows, :], sems.at[chunk])


def finish(chunk, places, conv_ref, q_ref, gated_ref, out_ref, sems):
    length = conv_ref.shape[0] // len(places)
    rows = pl.ds(places[chunk] * LANES, LANES)
    conv = conv_ref[chunk_rows(chunk, length), :].T
    gated_ref[rows, :] = (q_ref[rows, :].astype(jnp.float32) * conv).astype(jnp.bfloat16)
    leaving(chunk, places, gated_ref, out_ref, sems).start()


def local_kernel(
    places, order, decays_ref, weights_ref, series_ref, gain_ref, q_ref, conv_ref, dense_ref, out_ref, gated_ref, sems
):
    chunks = len(places)
    length = series_ref.shape[0] // chunks
    for half in range(chunks // SUBLANES):
        decay = mode_rows(decays_ref, 0, order, order, chunks, half)
        weight = mode_rows(weights_ref, order, order, 2 * order, chunks, half)
        for r in range(order):
            dense_ref[half, 0, r] = decay[r]
            dense_ref[half, 1, r] = weight[r]
        own = places[half * SUBLANES : (half + 1) * SUBLANES]
        gain = jnp.concatenate([gain_ref[pl.ds(place, 1), :] for place in own], axis=0)

        def steps(i, state):
            state = list(state)
            for u in range(UNROLL):
                rows = token_rows(half, length, i * UNROLL + u)
                x = series_ref[rows, :]
                for r in range(order):
                    state[r] = decay[r] * state[r] + x
                terms = [weight[r] * state[r] for r in range(order)]
                conv_ref[rows, :] = tree_sum(terms + [gain * x])
            return tuple(state)

        zero = jnp.zeros((SUBLANES, LANES), jnp.float32)
        lax.fori_loop(0, length // UNROLL, steps, (zero,) * order)

    @pl.when(lax.axis_index("seq") == 0)
    def _():
        for chunk in range(chunks):
            finish(chunk, places, conv_ref, q_ref, gated_ref, out_ref, sems)
        for chunk in range(chunks):
            leaving(chunk, places, gated_ref, out_ref, sems).wait()


def output_kernel(
    places, order, dense_ref, carry_ref, local_ref, q_ref, _, out_ref, conv_ref, gated_ref, sems
):
    chunks = len(places)
    length = local_ref.shape[0] // chunks
    tokens = length // SUBLANES

    @pl.when(lax.axis_index("seq") > 0)
    def _():
        for half in range(chunks // SUBLANES):
            decay = [dense_ref[half, 0, r] for r in range(order)]
            weight = [dense_ref[half, 1, r] for r in range(order)]
            carry = mode_rows(carry_ref, 0, order, order, chunks, half)

            def steps(i, fading):
                fading = list(fading)
                for u in range(tokens):
                    rows = token_rows(half, length, i * tokens + u)
                    fading = [decay[r] * fading[r] for r in range(order)]
                    conv_ref[rows, :] = tree_sum(fading + [local_ref[rows, :]])
                return tuple(fading)

            fading = tuple(weight[r] * carry[r] for r in range(order))
            if half == 0:
                lax.fori_loop(0, SUBLANES, steps, fading)
            else:
                for i in range(SUBLANES):
                    fading = steps(i, fading)
                    finish((half - 1) * SUBLANES + i, places, conv_ref, q_ref, gated_ref, out_ref, sems)
        for chunk in range(chunks - SUBLANES, chunks):
            finish(chunk, places, conv_ref, q_ref, gated_ref, out_ref, sems)
        for chunk in range(chunks):
            leaving(chunk, places, gated_ref, out_ref, sems).wait()


def call(kernel, out_shape, *args, in_spaces=None, out_spaces=None, aliases=None, scratch=(), flops=0):
    in_bytes = sum(a.size * a.dtype.itemsize for a in args)
    in_spaces = in_spaces or [pl.ANY if i in (aliases or {}) else pltpu.VMEM for i in range(len(args))]
    out_spaces = out_spaces or jax.tree.map(lambda _: pltpu.VMEM, out_shape)
    return pl.pallas_call(
        kernel,
        out_shape=out_shape,
        in_specs=[pl.BlockSpec(memory_space=space) for space in in_spaces],
        out_specs=jax.tree.map(lambda space: pl.BlockSpec(memory_space=space), out_spaces),
        scratch_shapes=list(scratch),
        input_output_aliases=aliases or {},
        compiler_params=pltpu.CompilerParams(vmem_limit_bytes=VMEM_LIMIT),
        cost_estimate=pl.CostEstimate(flops=flops, bytes_accessed=in_bytes, transcendentals=0),
    )(*args)


def to_chunks(pieces):
    owners, rows, own = pieces.shape
    if own == LANES:
        return pieces
    if own < LANES:
        group = LANES // own
        return pieces.reshape(owners // group, group, rows, own).swapaxes(1, 2).reshape(-1, rows, LANES)
    return pieces.reshape(owners, rows, own // LANES, LANES).swapaxes(1, 2).reshape(-1, rows, LANES)


def from_chunks(pieces, owners):
    chunks, rows, _ = pieces.shape
    own = chunks * LANES // owners
    if own == LANES:
        return pieces
    if own < LANES:
        group = LANES // own
        return pieces.reshape(chunks, rows, group, own).swapaxes(1, 2).reshape(owners, rows, own)
    return pieces.reshape(owners, own // LANES, rows, LANES).swapaxes(1, 2).reshape(owners, rows, own)


def all_to_all(pieces, members):
    return lax.all_to_all(pieces, "seq", split_axis=0, concat_axis=0, axis_index_groups=[members], tiled=True)


def shards(blocks, q_proj, k_proj, value_projection, residues, rates, direct_gain):
    channels, length = q_proj.shape
    order = residues.shape[1]
    chunks = channels // LANES
    f32 = jnp.float32

    members, places = list(range(blocks)), list(range(chunks))
    if blocks == chunks == len(FAR_FIRST):
        members, places = list(FAR_FIRST), list(FAR_FIRST)

    own_rates, own_residues = rates.T, residues.T
    copies = call(
        copies_kernel,
        jax.ShapeDtypeStruct((blocks,) + own_rates.shape, f32),
        pltpu.with_memory_space_constraint(own_rates, pltpu.HBM),
        in_spaces=[pl.ANY],
        scratch=[pltpu.VMEM(own_rates.shape, f32), pltpu.SemaphoreType.DMA],
        flops=COPIES_COST,
    )
    decays = to_chunks(all_to_all(copies, members)).reshape(chunks * order, LANES)

    whole_chunk = own_rates.shape[1] == LANES
    unused = jnp.zeros((order, LANES), f32)
    series, ends = call(
        functools.partial(state_kernel, places, order),
        (
            jax.ShapeDtypeStruct((length * chunks, LANES), f32),
            jax.ShapeDtypeStruct((chunks * 2 * order, LANES), f32),
        ),
        decays,
        own_rates if whole_chunk else unused,
        own_residues if whole_chunk else unused,
        k_proj,
        value_projection,
        flops=2 * order * channels * length,
    )
    local_series, ends = lax.optimization_barrier((series, ends))
    ends = from_chunks(ends.reshape(chunks, 2 * order, LANES), blocks)
    if not whole_chunk:
        ends = ends.at[:, order:].set(weights_of(own_residues, own_rates))
    ends = all_to_all(ends, members)
    weights = to_chunks(ends).reshape(chunks * 2 * order, LANES)
    out_shape = jax.ShapeDtypeStruct((channels, length), jnp.bfloat16)
    out_scratch = [pltpu.VMEM(out_shape.shape, out_shape.dtype), pltpu.SemaphoreType.DMA((chunks,))]
    local, dense, out = call(
        functools.partial(local_kernel, places, order),
        (
            jax.ShapeDtypeStruct((length * chunks, LANES), f32),
            jax.ShapeDtypeStruct((chunks // SUBLANES, 2, order, SUBLANES, LANES), f32),
            out_shape,
        ),
        decays,
        weights,
        local_series,
        direct_gain.reshape(chunks, LANES),
        q_proj,
        out_spaces=(pltpu.VMEM, pltpu.VMEM, pl.ANY),
        scratch=out_scratch,
        flops=4 * order * channels * length,
    )
    starts = call(
        functools.partial(prefix_kernel, length, members),
        jax.ShapeDtypeStruct((blocks,) + own_rates.shape, f32),
        own_rates,
        ends,
    )
    starts = all_to_all(starts, members)
    carry = to_chunks(starts).reshape(chunks * order, LANES)
    return call(
        functools.partial(output_kernel, places, order),
        out_shape,
        dense,
        carry,
        local,
        q_proj,
        out,
        out_spaces=pl.ANY,
        aliases={4: 0},
        scratch=[pltpu.VMEM((length * chunks, LANES), f32)] + out_scratch,
        flops=2 * order * channels * length,
    )


def solution(mesh):
    return jax.shard_map(
        functools.partial(shards, mesh.shape["seq"]),
        mesh=mesh,
        in_specs=(
            P("chan", ("groups", "seq")),
            P("chan", ("groups", "seq")),
            P("chan", ("groups", "seq")),
            P(("chan", "seq"), None),
            P(("chan", "seq"), None),
            P("chan"),
        ),
        out_specs=P("chan", ("groups", "seq")),
        check_vma=False,
    )
```

```python
import functools
import jax
import jax.numpy as jnp
from jax import lax
from jax.experimental import pallas as pl
from jax.experimental.pallas import tpu as pltpu
from jax.sharding import PartitionSpec as P

LANES = 128
SUBLANES = 8
UNROLL = 8
COPIES_COST = 10**10
NEAR_FIRST = (11, 7, 15, 6, 10, 5, 9, 3, 14, 4, 13, 2, 8, 1, 12, 0)
VMEM_LIMIT = 32 * 1024 * 1024


def copies_kernel(rate_hbm, copies_ref, rate_ref, sem):
    load = pltpu.make_async_copy(rate_hbm, rate_ref, sem)
    load.start()
    load.wait()
    decay = jnp.exp(-rate_ref[...])
    for piece in range(copies_ref.shape[0]):
        copies_ref[piece] = decay


def token_rows(half, length, token):
    row = (half * length + token) * SUBLANES
    return pl.ds(row if isinstance(row, int) else pl.multiple_of(row, SUBLANES), SUBLANES)


def chunk_rows(chunk, length):
    return pl.ds(chunk // SUBLANES * length * SUBLANES + chunk % SUBLANES, length, stride=SUBLANES)


def mode_rows(ref, base, order, per_chunk, chunks, half):
    first = half * SUBLANES * per_chunk + base
    return [ref[pl.ds(first + r, SUBLANES, stride=per_chunk), :] for r in range(order)]


def one_minus_exp(y):
    series = jnp.ones_like(y)
    for k in range(11, 1, -1):
        series = 1.0 - (y * (1.0 / k)) * series
    return jnp.where(y < 0.5, y * series, 1.0 - jnp.exp(-y))


def weights_of(residue, rate):
    return residue * jnp.sqrt(one_minus_exp(2.0 * rate))


def state_kernel(places, order, decays_ref, rate_ref, residue_ref, k_ref, v_ref, series_ref, state_ref):
    chunks, length = len(places), k_ref.shape[1]
    tokens = length // SUBLANES
    halves = chunks // SUBLANES

    def build(chunk):
        rows = pl.ds(places[chunk] * LANES, LANES)
        gated = k_ref[rows, :].astype(jnp.float32) * v_ref[rows, :].astype(jnp.float32)
        series_ref[chunk_rows(chunk, length), :] = gated.T

    weight = weights_of(residue_ref[...], rate_ref[...])
    for chunk in range(chunks):
        state_ref[pl.ds((2 * chunk + 1) * order, order), :] = weight
    for chunk in range(SUBLANES):
        build(chunk)
    for half in range(halves):
        decay = mode_rows(decays_ref, 0, order, order, chunks, half)
        square = [one * one for one in decay]

        def steps(i, state):
            state = list(state)
            for u in range(0, tokens, 2):
                x = series_ref[token_rows(half, length, i * tokens + u), :]
                y = series_ref[token_rows(half, length, i * tokens + u + 1), :]
                for r in range(order):
                    state[r] = square[r] * state[r] + (decay[r] * x + y)
            return tuple(state)

        state = (jnp.zeros((SUBLANES, LANES), jnp.float32),) * order
        if half + 1 < halves:
            for i in range(SUBLANES):
                state = steps(i, state)
                build((half + 1) * SUBLANES + i)
        else:
            state = lax.fori_loop(0, SUBLANES, steps, state)
        for r in range(order):
            state_ref[pl.ds(half * SUBLANES * 2 * order + r, SUBLANES, stride=2 * order), :] = state[r]


def prefix_kernel(length, members, rate_ref, ends_ref, starts_ref):
    span_decay = jnp.exp(-float(length) * rate_ref[...])
    carry = jnp.zeros(rate_ref.shape, jnp.float32)
    for block in range(len(members)):
        starts_ref[members.index(block)] = carry
        carry = span_decay * carry + ends_ref[members.index(block), : rate_ref.shape[0]]


def tree_sum(terms):
    terms = list(terms)
    while len(terms) > 1:
        terms = [terms[i] + terms[i + 1] if i + 1 < len(terms) else terms[i] for i in range(0, len(terms), 2)]
    return terms[0]


def leaving(chunk, places, gated_ref, out_ref, sems):
    rows = pl.ds(places[chunk] * LANES, LANES)
    return pltpu.make_async_copy(gated_ref.at[rows, :], out_ref.at[rows, :], sems.at[chunk])


def finish(chunk, places, conv_ref, q_ref, gated_ref, out_ref, sems):
    length = conv_ref.shape[0] // len(places)
    rows = pl.ds(places[chunk] * LANES, LANES)
    conv = conv_ref[chunk_rows(chunk, length), :].T
    gated_ref[rows, :] = (q_ref[rows, :].astype(jnp.float32) * conv).astype(jnp.bfloat16)
    leaving(chunk, places, gated_ref, out_ref, sems).start()


def local_kernel(
    places, order, decays_ref, weights_ref, series_ref, gain_ref, q_ref, conv_ref, dense_ref, out_ref, gated_ref, sems
):
    chunks = len(places)
    length = series_ref.shape[0] // chunks
    for half in range(chunks // SUBLANES):
        decay = mode_rows(decays_ref, 0, order, order, chunks, half)
        weight = mode_rows(weights_ref, order, order, 2 * order, chunks, half)
        for r in range(order):
            dense_ref[half, 0, r] = decay[r]
            dense_ref[half, 1, r] = weight[r]
        own = places[half * SUBLANES : (half + 1) * SUBLANES]
        gain = jnp.concatenate([gain_ref[pl.ds(place, 1), :] for place in own], axis=0)

        def steps(i, state):
            state = list(state)
            for u in range(UNROLL):
                rows = token_rows(half, length, i * UNROLL + u)
                x = series_ref[rows, :]
                for r in range(order):
                    state[r] = decay[r] * state[r] + x
                terms = [weight[r] * state[r] for r in range(order)]
                conv_ref[rows, :] = tree_sum(terms + [gain * x])
            return tuple(state)

        zero = jnp.zeros((SUBLANES, LANES), jnp.float32)
        lax.fori_loop(0, length // UNROLL, steps, (zero,) * order)

    @pl.when(lax.axis_index("seq") == 0)
    def _():
        for chunk in range(chunks):
            finish(chunk, places, conv_ref, q_ref, gated_ref, out_ref, sems)
        for chunk in range(chunks):
            leaving(chunk, places, gated_ref, out_ref, sems).wait()


def output_kernel(
    places, order, dense_ref, carry_ref, local_ref, q_ref, _, out_ref, conv_ref, gated_ref, sems
):
    chunks = len(places)
    length = local_ref.shape[0] // chunks
    tokens = length // SUBLANES

    @pl.when(lax.axis_index("seq") > 0)
    def _():
        for half in range(chunks // SUBLANES):
            decay = [dense_ref[half, 0, r] for r in range(order)]
            weight = [dense_ref[half, 1, r] for r in range(order)]
            carry = mode_rows(carry_ref, 0, order, order, chunks, half)

            def steps(i, fading):
                fading = list(fading)
                for u in range(tokens):
                    rows = token_rows(half, length, i * tokens + u)
                    fading = [decay[r] * fading[r] for r in range(order)]
                    conv_ref[rows, :] = tree_sum(fading + [local_ref[rows, :]])
                return tuple(fading)

            fading = tuple(weight[r] * carry[r] for r in range(order))
            if half == 0:
                lax.fori_loop(0, SUBLANES, steps, fading)
            else:
                for i in range(SUBLANES):
                    fading = steps(i, fading)
                    finish((half - 1) * SUBLANES + i, places, conv_ref, q_ref, gated_ref, out_ref, sems)
        for chunk in range(chunks - SUBLANES, chunks):
            finish(chunk, places, conv_ref, q_ref, gated_ref, out_ref, sems)
        for chunk in range(chunks):
            leaving(chunk, places, gated_ref, out_ref, sems).wait()


def call(kernel, out_shape, *args, in_spaces=None, out_spaces=None, aliases=None, scratch=(), flops=0):
    in_bytes = sum(a.size * a.dtype.itemsize for a in args)
    in_spaces = in_spaces or [pl.ANY if i in (aliases or {}) else pltpu.VMEM for i in range(len(args))]
    out_spaces = out_spaces or jax.tree.map(lambda _: pltpu.VMEM, out_shape)
    return pl.pallas_call(
        kernel,
        out_shape=out_shape,
        in_specs=[pl.BlockSpec(memory_space=space) for space in in_spaces],
        out_specs=jax.tree.map(lambda space: pl.BlockSpec(memory_space=space), out_spaces),
        scratch_shapes=list(scratch),
        input_output_aliases=aliases or {},
        compiler_params=pltpu.CompilerParams(vmem_limit_bytes=VMEM_LIMIT),
        cost_estimate=pl.CostEstimate(flops=flops, bytes_accessed=in_bytes, transcendentals=0),
    )(*args)


def to_chunks(pieces):
    owners, rows, own = pieces.shape
    if own == LANES:
        return pieces
    if own < LANES:
        group = LANES // own
        return pieces.reshape(owners // group, group, rows, own).swapaxes(1, 2).reshape(-1, rows, LANES)
    return pieces.reshape(owners, rows, own // LANES, LANES).swapaxes(1, 2).reshape(-1, rows, LANES)


def from_chunks(pieces, owners):
    chunks, rows, _ = pieces.shape
    own = chunks * LANES // owners
    if own == LANES:
        return pieces
    if own < LANES:
        group = LANES // own
        return pieces.reshape(chunks, rows, group, own).swapaxes(1, 2).reshape(owners, rows, own)
    return pieces.reshape(owners, own // LANES, rows, LANES).swapaxes(1, 2).reshape(owners, rows, own)


def all_to_all(pieces, members):
    return lax.all_to_all(pieces, "seq", split_axis=0, concat_axis=0, axis_index_groups=[members], tiled=True)


def shards(blocks, q_proj, k_proj, value_projection, residues, rates, direct_gain):
    channels, length = q_proj.shape
    order = residues.shape[1]
    chunks = channels // LANES
    f32 = jnp.float32

    members, places = list(range(blocks)), list(range(chunks))
    if blocks == chunks == len(NEAR_FIRST):
        members, places = list(NEAR_FIRST), list(NEAR_FIRST)

    own_rates, own_residues = rates.T, residues.T
    copies = call(
        copies_kernel,
        jax.ShapeDtypeStruct((blocks,) + own_rates.shape, f32),
        pltpu.with_memory_space_constraint(own_rates, pltpu.HBM),
        in_spaces=[pl.ANY],
        scratch=[pltpu.VMEM(own_rates.shape, f32), pltpu.SemaphoreType.DMA],
        flops=COPIES_COST,
    )
    decays = to_chunks(all_to_all(copies, members)).reshape(chunks * order, LANES)

    whole_chunk = own_rates.shape[1] == LANES
    unused = jnp.zeros((order, LANES), f32)
    series, ends = call(
        functools.partial(state_kernel, places, order),
        (
            jax.ShapeDtypeStruct((length * chunks, LANES), f32),
            jax.ShapeDtypeStruct((chunks * 2 * order, LANES), f32),
        ),
        decays,
        own_rates if whole_chunk else unused,
        own_residues if whole_chunk else unused,
        k_proj,
        value_projection,
        flops=2 * order * channels * length,
    )
    local_series, ends = lax.optimization_barrier((series, ends))
    ends = from_chunks(ends.reshape(chunks, 2 * order, LANES), blocks)
    if not whole_chunk:
        ends = ends.at[:, order:].set(weights_of(own_residues, own_rates))
    ends = all_to_all(ends, members)
    weights = to_chunks(ends).reshape(chunks * 2 * order, LANES)
    out_shape = jax.ShapeDtypeStruct((channels, length), jnp.bfloat16)
    out_scratch = [pltpu.VMEM(out_shape.shape, out_shape.dtype), pltpu.SemaphoreType.DMA((chunks,))]
    local, dense, out = call(
        functools.partial(local_kernel, places, order),
        (
            jax.ShapeDtypeStruct((length * chunks, LANES), f32),
            jax.ShapeDtypeStruct((chunks // SUBLANES, 2, order, SUBLANES, LANES), f32),
            out_shape,
        ),
        decays,
        weights,
        local_series,
        direct_gain.reshape(chunks, LANES),
        q_proj,
        out_spaces=(pltpu.VMEM, pltpu.VMEM, pl.ANY),
        scratch=out_scratch,
        flops=4 * order * channels * length,
    )
    starts = call(
        functools.partial(prefix_kernel, length, members),
        jax.ShapeDtypeStruct((blocks,) + own_rates.shape, f32),
        own_rates,
        ends,
    )
    starts = all_to_all(starts, members)
    carry = to_chunks(starts).reshape(chunks * order, LANES)
    return call(
        functools.partial(output_kernel, places, order),
        out_shape,
        dense,
        carry,
        local,
        q_proj,
        out,
        out_spaces=pl.ANY,
        aliases={4: 0},
        scratch=[pltpu.VMEM((length * chunks, LANES), f32)] + out_scratch,
        flops=2 * order * channels * length,
    )


def solution(mesh):
    return jax.shard_map(
        functools.partial(shards, mesh.shape["seq"]),
        mesh=mesh,
        in_specs=(
            P("chan", ("groups", "seq")),
            P("chan", ("groups", "seq")),
            P("chan", ("groups", "seq")),
            P(("chan", "seq"), None),
            P(("chan", "seq"), None),
            P("chan"),
        ),
        out_specs=P("chan", ("groups", "seq")),
        check_vma=False,
    )
```

```python
import functools
import jax
import jax.numpy as jnp
from jax import lax
from jax.experimental import pallas as pl
from jax.experimental.pallas import tpu as pltpu
from jax.sharding import PartitionSpec as P

LANES = 128
SUBLANES = 8
UNROLL = 8
COPIES_COST = 10**10
VMEM_LIMIT = 32 * 1024 * 1024


def copies_kernel(rate_hbm, copies_ref, rate_ref, sem):
    load = pltpu.make_async_copy(rate_hbm, rate_ref, sem)
    load.start()
    load.wait()
    decay = jnp.exp(-rate_ref[...])
    for piece in range(copies_ref.shape[0]):
        copies_ref[piece] = decay


def token_rows(half, length, token):
    row = (half * length + token) * SUBLANES
    return pl.ds(row if isinstance(row, int) else pl.multiple_of(row, SUBLANES), SUBLANES)


def chunk_rows(chunk, length):
    return pl.ds(chunk // SUBLANES * length * SUBLANES + chunk % SUBLANES, length, stride=SUBLANES)


def mode_rows(ref, base, order, per_chunk, chunks, half):
    first = half * SUBLANES * per_chunk + base
    return [ref[pl.ds(first + r, SUBLANES, stride=per_chunk), :] for r in range(order)]


def one_minus_exp(y):
    series = jnp.ones_like(y)
    for k in range(11, 1, -1):
        series = 1.0 - (y * (1.0 / k)) * series
    return jnp.where(y < 0.5, y * series, 1.0 - jnp.exp(-y))


def weights_of(residue, rate):
    return residue * jnp.sqrt(one_minus_exp(2.0 * rate))


def state_kernel(places, order, decays_ref, rate_ref, residue_ref, k_ref, v_ref, series_ref, state_ref):
    chunks, length = len(places), k_ref.shape[1]
    tokens = length // SUBLANES
    halves = chunks // SUBLANES

    def build(chunk):
        rows = pl.ds(places[chunk] * LANES, LANES)
        gated = k_ref[rows, :].astype(jnp.float32) * v_ref[rows, :].astype(jnp.float32)
        series_ref[chunk_rows(chunk, length), :] = gated.T

    weight = weights_of(residue_ref[...], rate_ref[...])
    for chunk in range(chunks):
        state_ref[pl.ds((2 * chunk + 1) * order, order), :] = weight
    for chunk in range(SUBLANES):
        build(chunk)
    for half in range(halves):
        decay = mode_rows(decays_ref, 0, order, order, chunks, half)
        square = [one * one for one in decay]

        def steps(i, state):
            state = list(state)
            for u in range(0, tokens, 2):
                x = series_ref[token_rows(half, length, i * tokens + u), :]
                y = series_ref[token_rows(half, length, i * tokens + u + 1), :]
                for r in range(order):
                    state[r] = square[r] * state[r] + (decay[r] * x + y)
            return tuple(state)

        state = (jnp.zeros((SUBLANES, LANES), jnp.float32),) * order
        if half + 1 < halves:
            for i in range(SUBLANES):
                state = steps(i, state)
                build((half + 1) * SUBLANES + i)
        else:
            state = lax.fori_loop(0, SUBLANES, steps, state)
        for r in range(order):
            state_ref[pl.ds(half * SUBLANES * 2 * order + r, SUBLANES, stride=2 * order), :] = state[r]


def prefix_kernel(length, members, rate_ref, ends_ref, starts_ref):
    span_decay = jnp.exp(-float(length) * rate_ref[...])
    carry = jnp.zeros(rate_ref.shape, jnp.float32)
    for block in range(len(members)):
        starts_ref[members.index(block)] = carry
        carry = span_decay * carry + ends_ref[members.index(block), : rate_ref.shape[0]]


def tree_sum(terms):
    terms = list(terms)
    while len(terms) > 1:
        terms = [terms[i] + terms[i + 1] if i + 1 < len(terms) else terms[i] for i in range(0, len(terms), 2)]
    return terms[0]


def leaving(chunk, places, gated_ref, out_ref, sems):
    rows = pl.ds(places[chunk] * LANES, LANES)
    return pltpu.make_async_copy(gated_ref.at[rows, :], out_ref.at[rows, :], sems.at[chunk])


def finish(chunk, places, conv_ref, q_ref, gated_ref, out_ref, sems):
    length = conv_ref.shape[0] // len(places)
    rows = pl.ds(places[chunk] * LANES, LANES)
    conv = conv_ref[chunk_rows(chunk, length), :].T
    gated_ref[rows, :] = (q_ref[rows, :].astype(jnp.float32) * conv).astype(jnp.bfloat16)
    leaving(chunk, places, gated_ref, out_ref, sems).start()


def local_kernel(
    places, order, decays_ref, weights_ref, series_ref, gain_ref, q_ref, conv_ref, dense_ref, gate_ref, out_ref,
    gated_ref, sems
):
    chunks = len(places)
    length = series_ref.shape[0] // chunks
    for half in range(chunks // SUBLANES):
        decay = mode_rows(decays_ref, 0, order, order, chunks, half)
        weight = mode_rows(weights_ref, order, order, 2 * order, chunks, half)
        for r in range(order):
            dense_ref[half, 0, r] = decay[r]
            dense_ref[half, 1, r] = weight[r]
        own = places[half * SUBLANES : (half + 1) * SUBLANES]
        gain = jnp.concatenate([gain_ref[pl.ds(place, 1), :] for place in own], axis=0)

        def steps(i, state):
            state = list(state)
            for u in range(UNROLL):
                rows = token_rows(half, length, i * UNROLL + u)
                x = series_ref[rows, :]
                for r in range(order):
                    state[r] = decay[r] * state[r] + x
                terms = [weight[r] * state[r] for r in range(order)]
                conv_ref[rows, :] = tree_sum(terms + [gain * x])
            return tuple(state)

        zero = jnp.zeros((SUBLANES, LANES), jnp.float32)
        lax.fori_loop(0, length // UNROLL, steps, (zero,) * order)

    first = lax.axis_index("seq") == 0

    @pl.when(first)
    def _():
        for chunk in range(chunks):
            finish(chunk, places, conv_ref, q_ref, gated_ref, out_ref, sems)
        for chunk in range(chunks):
            leaving(chunk, places, gated_ref, out_ref, sems).wait()

    @pl.when(jnp.logical_not(first))
    def _():
        for chunk, place in enumerate(places):
            q = q_ref[pl.ds(place * LANES, LANES), :].astype(jnp.float32)
            gate_ref[chunk_rows(chunk, length), :] = q.T


def output_kernel(
    places, order, dense_ref, carry_ref, local_ref, gate_ref, _, out_ref, conv_ref, gated_ref, sems
):
    chunks = len(places)
    length = local_ref.shape[0] // chunks
    tokens = length // SUBLANES

    def send(chunk):
        rows = pl.ds(places[chunk] * LANES, LANES)
        gated_ref[rows, :] = conv_ref[chunk_rows(chunk, length), :].astype(jnp.bfloat16).T
        leaving(chunk, places, gated_ref, out_ref, sems).start()

    @pl.when(lax.axis_index("seq") > 0)
    def _():
        for half in range(chunks // SUBLANES):
            decay = [dense_ref[half, 0, r] for r in range(order)]
            weight = [dense_ref[half, 1, r] for r in range(order)]
            carry = mode_rows(carry_ref, 0, order, order, chunks, half)

            def steps(i, fading):
                fading = list(fading)
                for u in range(tokens):
                    rows = token_rows(half, length, i * tokens + u)
                    fading = [decay[r] * fading[r] for r in range(order)]
                    conv_ref[rows, :] = gate_ref[rows, :] * tree_sum(fading + [local_ref[rows, :]])
                return tuple(fading)

            fading = tuple(weight[r] * carry[r] for r in range(order))
            if half == 0:
                lax.fori_loop(0, SUBLANES, steps, fading)
            else:
                for i in range(SUBLANES):
                    fading = steps(i, fading)
                    send((half - 1) * SUBLANES + i)
        for chunk in range(chunks - SUBLANES, chunks):
            send(chunk)
        for chunk in range(chunks):
            leaving(chunk, places, gated_ref, out_ref, sems).wait()


def call(kernel, out_shape, *args, in_spaces=None, out_spaces=None, aliases=None, scratch=(), flops=0):
    in_bytes = sum(a.size * a.dtype.itemsize for a in args)
    in_spaces = in_spaces or [pl.ANY if i in (aliases or {}) else pltpu.VMEM for i in range(len(args))]
    out_spaces = out_spaces or jax.tree.map(lambda _: pltpu.VMEM, out_shape)
    return pl.pallas_call(
        kernel,
        out_shape=out_shape,
        in_specs=[pl.BlockSpec(memory_space=space) for space in in_spaces],
        out_specs=jax.tree.map(lambda space: pl.BlockSpec(memory_space=space), out_spaces),
        scratch_shapes=list(scratch),
        input_output_aliases=aliases or {},
        compiler_params=pltpu.CompilerParams(vmem_limit_bytes=VMEM_LIMIT),
        cost_estimate=pl.CostEstimate(flops=flops, bytes_accessed=in_bytes, transcendentals=0),
    )(*args)


def to_chunks(pieces):
    owners, rows, own = pieces.shape
    if own == LANES:
        return pieces
    if own < LANES:
        group = LANES // own
        return pieces.reshape(owners // group, group, rows, own).swapaxes(1, 2).reshape(-1, rows, LANES)
    return pieces.reshape(owners, rows, own // LANES, LANES).swapaxes(1, 2).reshape(-1, rows, LANES)


def from_chunks(pieces, owners):
    chunks, rows, _ = pieces.shape
    own = chunks * LANES // owners
    if own == LANES:
        return pieces
    if own < LANES:
        group = LANES // own
        return pieces.reshape(chunks, rows, group, own).swapaxes(1, 2).reshape(owners, rows, own)
    return pieces.reshape(owners, own // LANES, rows, LANES).swapaxes(1, 2).reshape(owners, rows, own)


def all_to_all(pieces, members):
    return lax.all_to_all(pieces, "seq", split_axis=0, concat_axis=0, axis_index_groups=[members], tiled=True)


def shards(blocks, q_proj, k_proj, value_projection, residues, rates, direct_gain):
    channels, length = q_proj.shape
    order = residues.shape[1]
    chunks = channels // LANES
    f32 = jnp.float32

    members, places = list(range(blocks)), list(range(chunks))
    if blocks == chunks:
        far, middle = blocks // 2, blocks * 11 // 16
        upper = [middle] + [block for block in members[:far - 1:-1] if block != middle]
        members = [block for one in upper for block in (one, one - far)]
        places = list(members)

    own_rates, own_residues = rates.T, residues.T
    copies = call(
        copies_kernel,
        jax.ShapeDtypeStruct((blocks,) + own_rates.shape, f32),
        pltpu.with_memory_space_constraint(own_rates, pltpu.HBM),
        in_spaces=[pl.ANY],
        scratch=[pltpu.VMEM(own_rates.shape, f32), pltpu.SemaphoreType.DMA],
        flops=COPIES_COST,
    )
    decays = to_chunks(all_to_all(copies, members)).reshape(chunks * order, LANES)

    whole_chunk = own_rates.shape[1] == LANES
    unused = jnp.zeros((order, LANES), f32)
    series, ends = call(
        functools.partial(state_kernel, places, order),
        (
            jax.ShapeDtypeStruct((length * chunks, LANES), f32),
            jax.ShapeDtypeStruct((chunks * 2 * order, LANES), f32),
        ),
        decays,
        own_rates if whole_chunk else unused,
        own_residues if whole_chunk else unused,
        k_proj,
        value_projection,
        flops=2 * order * channels * length,
    )
    local_series, ends = lax.optimization_barrier((series, ends))
    ends = from_chunks(ends.reshape(chunks, 2 * order, LANES), blocks)
    if not whole_chunk:
        ends = ends.at[:, order:].set(weights_of(own_residues, own_rates))
    ends = all_to_all(ends, members)
    weights = to_chunks(ends).reshape(chunks * 2 * order, LANES)
    out_shape = jax.ShapeDtypeStruct((channels, length), jnp.bfloat16)
    out_scratch = [pltpu.VMEM(out_shape.shape, out_shape.dtype), pltpu.SemaphoreType.DMA((chunks,))]
    local, dense, gate, out = call(
        functools.partial(local_kernel, places, order),
        (
            jax.ShapeDtypeStruct((length * chunks, LANES), f32),
            jax.ShapeDtypeStruct((chunks // SUBLANES, 2, order, SUBLANES, LANES), f32),
            jax.ShapeDtypeStruct((length * chunks, LANES), f32),
            out_shape,
        ),
        decays,
        weights,
        local_series,
        direct_gain.reshape(chunks, LANES),
        q_proj,
        out_spaces=(pltpu.VMEM, pltpu.VMEM, pltpu.VMEM, pl.ANY),
        scratch=out_scratch,
        flops=4 * order * channels * length,
    )
    starts = call(
        functools.partial(prefix_kernel, length, members),
        jax.ShapeDtypeStruct((blocks,) + own_rates.shape, f32),
        own_rates,
        ends,
    )
    starts = all_to_all(starts, members)
    carry = to_chunks(starts).reshape(chunks * order, LANES)
    return call(
        functools.partial(output_kernel, places, order),
        out_shape,
        dense,
        carry,
        local,
        gate,
        out,
        out_spaces=pl.ANY,
        aliases={4: 0},
        scratch=[pltpu.VMEM((length * chunks, LANES), f32)] + out_scratch,
        flops=2 * order * channels * length,
    )


def solution(mesh):
    return jax.shard_map(
        functools.partial(shards, mesh.shape["seq"]),
        mesh=mesh,
        in_specs=(
            P("chan", ("groups", "seq")),
            P("chan", ("groups", "seq")),
            P("chan", ("groups", "seq")),
            P(("chan", "seq"), None),
            P(("chan", "seq"), None),
            P("chan"),
        ),
        out_specs=P("chan", ("groups", "seq")),
        check_vma=False,
    )
```

```python
import functools
import jax
import jax.numpy as jnp
from jax import lax
from jax.experimental import pallas as pl
from jax.experimental.pallas import tpu as pltpu
from jax.sharding import PartitionSpec as P

LANES = 128
SUBLANES = 8
UNROLL = 8
COPIES_COST = 10**10
VMEM_LIMIT = 32 * 1024 * 1024


def copies_kernel(rate_hbm, copies_ref, rate_ref, sem):
    load = pltpu.make_async_copy(rate_hbm, rate_ref, sem)
    load.start()
    load.wait()
    decay = jnp.exp(-rate_ref[...])
    for piece in range(copies_ref.shape[0]):
        copies_ref[piece] = decay


def token_rows(half, length, token):
    row = (half * length + token) * SUBLANES
    return pl.ds(row if isinstance(row, int) else pl.multiple_of(row, SUBLANES), SUBLANES)


def chunk_rows(chunk, length):
    return pl.ds(chunk // SUBLANES * length * SUBLANES + chunk % SUBLANES, length, stride=SUBLANES)


def mode_rows(ref, base, order, per_chunk, chunks, half):
    first = half * SUBLANES * per_chunk + base
    return [ref[pl.ds(first + r, SUBLANES, stride=per_chunk), :] for r in range(order)]


def one_minus_exp(y):
    series = jnp.ones_like(y)
    for k in range(11, 1, -1):
        series = 1.0 - (y * (1.0 / k)) * series
    return jnp.where(y < 0.5, y * series, 1.0 - jnp.exp(-y))


def weights_of(residue, rate):
    return residue * jnp.sqrt(one_minus_exp(2.0 * rate))


def state_kernel(places, order, decays_ref, rate_ref, residue_ref, k_ref, v_ref, series_ref, state_ref):
    chunks, length = len(places), k_ref.shape[1]
    tokens = length // SUBLANES
    halves = chunks // SUBLANES

    def build(chunk):
        rows = pl.ds(places[chunk] * LANES, LANES)
        gated = k_ref[rows, :].astype(jnp.float32) * v_ref[rows, :].astype(jnp.float32)
        series_ref[chunk_rows(chunk, length), :] = gated.T

    weight = weights_of(residue_ref[...], rate_ref[...])
    for chunk in range(chunks):
        state_ref[pl.ds((2 * chunk + 1) * order, order), :] = weight
    for chunk in range(SUBLANES):
        build(chunk)
    for half in range(halves):
        decay = mode_rows(decays_ref, 0, order, order, chunks, half)
        square = [one * one for one in decay]

        def steps(i, state):
            state = list(state)
            for u in range(0, tokens, 2):
                x = series_ref[token_rows(half, length, i * tokens + u), :]
                y = series_ref[token_rows(half, length, i * tokens + u + 1), :]
                for r in range(order):
                    state[r] = square[r] * state[r] + (decay[r] * x + y)
            return tuple(state)

        state = (jnp.zeros((SUBLANES, LANES), jnp.float32),) * order
        if half + 1 < halves:
            for i in range(SUBLANES):
                state = steps(i, state)
                build((half + 1) * SUBLANES + i)
        else:
            state = lax.fori_loop(0, SUBLANES, steps, state)
        for r in range(order):
            state_ref[pl.ds(half * SUBLANES * 2 * order + r, SUBLANES, stride=2 * order), :] = state[r]


def prefix_kernel(length, members, rate_ref, ends_ref, starts_ref):
    span_decay = jnp.exp(-float(length) * rate_ref[...])
    carry = jnp.zeros(rate_ref.shape, jnp.float32)
    for block in range(len(members)):
        starts_ref[members.index(block)] = carry
        carry = span_decay * carry + ends_ref[members.index(block), : rate_ref.shape[0]]


def tree_sum(terms):
    terms = list(terms)
    while len(terms) > 1:
        terms = [terms[i] + terms[i + 1] if i + 1 < len(terms) else terms[i] for i in range(0, len(terms), 2)]
    return terms[0]


def leaving(chunk, places, gated_ref, out_ref, sems):
    rows = pl.ds(places[chunk] * LANES, LANES)
    return pltpu.make_async_copy(gated_ref.at[rows, :], out_ref.at[rows, :], sems.at[chunk])


def finish(chunk, places, conv_ref, q_ref, gated_ref, out_ref, sems, start=True):
    length = conv_ref.shape[0] // len(places)
    rows = pl.ds(places[chunk] * LANES, LANES)
    conv = conv_ref[chunk_rows(chunk, length), :].T
    gated_ref[rows, :] = (q_ref[rows, :].astype(jnp.float32) * conv).astype(jnp.bfloat16)
    if start:
        leaving(chunk, places, gated_ref, out_ref, sems).start()


def local_kernel(
    places, order, decays_ref, weights_ref, series_ref, gain_ref, q_ref, conv_ref, dense_ref, out_ref, gated_ref, sems
):
    chunks = len(places)
    length = series_ref.shape[0] // chunks
    for half in range(chunks // SUBLANES):
        decay = mode_rows(decays_ref, 0, order, order, chunks, half)
        weight = mode_rows(weights_ref, order, order, 2 * order, chunks, half)
        for r in range(order):
            dense_ref[half, 0, r] = decay[r]
            dense_ref[half, 1, r] = weight[r]
        own = places[half * SUBLANES : (half + 1) * SUBLANES]
        gain = jnp.concatenate([gain_ref[pl.ds(place, 1), :] for place in own], axis=0)

        def steps(i, state):
            state = list(state)
            for u in range(UNROLL):
                rows = token_rows(half, length, i * UNROLL + u)
                x = series_ref[rows, :]
                for r in range(order):
                    state[r] = decay[r] * state[r] + x
                terms = [weight[r] * state[r] for r in range(order)]
                conv_ref[rows, :] = tree_sum(terms + [gain * x])
            return tuple(state)

        zero = jnp.zeros((SUBLANES, LANES), jnp.float32)
        lax.fori_loop(0, length // UNROLL, steps, (zero,) * order)

    @pl.when(lax.axis_index("seq") == 0)
    def _():
        for chunk in range(chunks):
            finish(chunk, places, conv_ref, q_ref, gated_ref, out_ref, sems)
        for chunk in range(chunks):
            leaving(chunk, places, gated_ref, out_ref, sems).wait()


def output_kernel(
    places, order, dense_ref, carry_ref, local_ref, q_ref, _, out_ref, conv_ref, gated_ref, sems
):
    chunks = len(places)
    length = local_ref.shape[0] // chunks
    tokens = length // SUBLANES

    @pl.when(lax.axis_index("seq") > 0)
    def _():
        for half in range(chunks // SUBLANES):
            decay = [dense_ref[half, 0, r] for r in range(order)]
            weight = [dense_ref[half, 1, r] for r in range(order)]
            carry = mode_rows(carry_ref, 0, order, order, chunks, half)

            def steps(i, fading):
                fading = list(fading)
                for u in range(tokens):
                    rows = token_rows(half, length, i * tokens + u)
                    fading = [decay[r] * fading[r] for r in range(order)]
                    conv_ref[rows, :] = tree_sum(fading + [local_ref[rows, :]])
                return tuple(fading)

            fading = tuple(weight[r] * carry[r] for r in range(order))
            if half == 0:
                lax.fori_loop(0, SUBLANES, steps, fading)
            else:
                for i in range(SUBLANES):
                    fading = steps(i, fading)
                    if i > 0:
                        leaving((half - 1) * SUBLANES + i - 1, places, gated_ref, out_ref, sems).start()
                    finish((half - 1) * SUBLANES + i, places, conv_ref, q_ref, gated_ref, out_ref, sems, False)
                leaving(half * SUBLANES - 1, places, gated_ref, out_ref, sems).start()
        for chunk in range(chunks - SUBLANES, chunks):
            finish(chunk, places, conv_ref, q_ref, gated_ref, out_ref, sems)
        for chunk in range(chunks):
            leaving(chunk, places, gated_ref, out_ref, sems).wait()


def call(kernel, out_shape, *args, in_spaces=None, out_spaces=None, aliases=None, scratch=(), flops=0):
    in_bytes = sum(a.size * a.dtype.itemsize for a in args)
    in_spaces = in_spaces or [pl.ANY if i in (aliases or {}) else pltpu.VMEM for i in range(len(args))]
    out_spaces = out_spaces or jax.tree.map(lambda _: pltpu.VMEM, out_shape)
    return pl.pallas_call(
        kernel,
        out_shape=out_shape,
        in_specs=[pl.BlockSpec(memory_space=space) for space in in_spaces],
        out_specs=jax.tree.map(lambda space: pl.BlockSpec(memory_space=space), out_spaces),
        scratch_shapes=list(scratch),
        input_output_aliases=aliases or {},
        compiler_params=pltpu.CompilerParams(vmem_limit_bytes=VMEM_LIMIT),
        cost_estimate=pl.CostEstimate(flops=flops, bytes_accessed=in_bytes, transcendentals=0),
    )(*args)


def to_chunks(pieces):
    owners, rows, own = pieces.shape
    if own == LANES:
        return pieces
    if own < LANES:
        group = LANES // own
        return pieces.reshape(owners // group, group, rows, own).swapaxes(1, 2).reshape(-1, rows, LANES)
    return pieces.reshape(owners, rows, own // LANES, LANES).swapaxes(1, 2).reshape(-1, rows, LANES)


def from_chunks(pieces, owners):
    chunks, rows, _ = pieces.shape
    own = chunks * LANES // owners
    if own == LANES:
        return pieces
    if own < LANES:
        group = LANES // own
        return pieces.reshape(chunks, rows, group, own).swapaxes(1, 2).reshape(owners, rows, own)
    return pieces.reshape(owners, own // LANES, rows, LANES).swapaxes(1, 2).reshape(owners, rows, own)


def all_to_all(pieces, members):
    return lax.all_to_all(pieces, "seq", split_axis=0, concat_axis=0, axis_index_groups=[members], tiled=True)


def shards(blocks, q_proj, k_proj, value_projection, residues, rates, direct_gain):
    channels, length = q_proj.shape
    order = residues.shape[1]
    chunks = channels // LANES
    f32 = jnp.float32

    members, places = list(range(blocks)), list(range(chunks))
    if blocks == chunks:
        far, middle = blocks // 2, blocks * 11 // 16
        upper = [middle] + [block for block in members[:far - 1:-1] if block != middle]
        members = [block for one in upper for block in (one, one - far)]
        places = list(members)

    own_rates, own_residues = rates.T, residues.T
    copies = call(
        copies_kernel,
        jax.ShapeDtypeStruct((blocks,) + own_rates.shape, f32),
        pltpu.with_memory_space_constraint(own_rates, pltpu.HBM),
        in_spaces=[pl.ANY],
        scratch=[pltpu.VMEM(own_rates.shape, f32), pltpu.SemaphoreType.DMA],
        flops=COPIES_COST,
    )
    decays = to_chunks(all_to_all(copies, members)).reshape(chunks * order, LANES)

    whole_chunk = own_rates.shape[1] == LANES
    unused = jnp.zeros((order, LANES), f32)
    series, ends = call(
        functools.partial(state_kernel, places, order),
        (
            jax.ShapeDtypeStruct((length * chunks, LANES), f32),
            jax.ShapeDtypeStruct((chunks * 2 * order, LANES), f32),
        ),
        decays,
        own_rates if whole_chunk else unused,
        own_residues if whole_chunk else unused,
        k_proj,
        value_projection,
        flops=2 * order * channels * length,
    )
    local_series, ends = lax.optimization_barrier((series, ends))
    ends = from_chunks(ends.reshape(chunks, 2 * order, LANES), blocks)
    if not whole_chunk:
        ends = ends.at[:, order:].set(weights_of(own_residues, own_rates))
    ends = all_to_all(ends, members)
    weights = to_chunks(ends).reshape(chunks * 2 * order, LANES)
    out_shape = jax.ShapeDtypeStruct((channels, length), jnp.bfloat16)
    out_scratch = [pltpu.VMEM(out_shape.shape, out_shape.dtype), pltpu.SemaphoreType.DMA((chunks,))]
    local, dense, out = call(
        functools.partial(local_kernel, places, order),
        (
            jax.ShapeDtypeStruct((length * chunks, LANES), f32),
            jax.ShapeDtypeStruct((chunks // SUBLANES, 2, order, SUBLANES, LANES), f32),
            out_shape,
        ),
        decays,
        weights,
        local_series,
        direct_gain.reshape(chunks, LANES),
        q_proj,
        out_spaces=(pltpu.VMEM, pltpu.VMEM, pl.ANY),
        scratch=out_scratch,
        flops=4 * order * channels * length,
    )
    starts = call(
        functools.partial(prefix_kernel, length, members),
        jax.ShapeDtypeStruct((blocks,) + own_rates.shape, f32),
        own_rates,
        ends,
    )
    starts = all_to_all(starts, members)
    carry = to_chunks(starts).reshape(chunks * order, LANES)
    return call(
        functools.partial(output_kernel, places, order),
        out_shape,
        dense,
        carry,
        local,
        q_proj,
        out,
        out_spaces=pl.ANY,
        aliases={4: 0},
        scratch=[pltpu.VMEM((length * chunks, LANES), f32)] + out_scratch,
        flops=2 * order * channels * length,
    )


def solution(mesh):
    return jax.shard_map(
        functools.partial(shards, mesh.shape["seq"]),
        mesh=mesh,
        in_specs=(
            P("chan", ("groups", "seq")),
            P("chan", ("groups", "seq")),
            P("chan", ("groups", "seq")),
            P(("chan", "seq"), None),
            P(("chan", "seq"), None),
            P("chan"),
        ),
        out_specs=P("chan", ("groups", "seq")),
        check_vma=False,
    )
```

```python
import functools
import jax
import jax.numpy as jnp
from jax import lax
from jax.experimental import pallas as pl
from jax.experimental.pallas import tpu as pltpu
from jax.sharding import PartitionSpec as P

LANES = 128
SUBLANES = 8
UNROLL = 8
COPIES_COST = 10**10
VMEM_LIMIT = 32 * 1024 * 1024


def copies_kernel(rate_hbm, copies_ref, rate_ref, sem):
    load = pltpu.make_async_copy(rate_hbm, rate_ref, sem)
    load.start()
    load.wait()
    decay = jnp.exp(-rate_ref[...])
    for piece in range(copies_ref.shape[0]):
        copies_ref[piece] = decay


def token_rows(half, length, token):
    row = (half * length + token) * SUBLANES
    return pl.ds(row if isinstance(row, int) else pl.multiple_of(row, SUBLANES), SUBLANES)


def chunk_rows(chunk, length):
    return pl.ds(chunk // SUBLANES * length * SUBLANES + chunk % SUBLANES, length, stride=SUBLANES)


def mode_rows(ref, base, order, per_chunk, chunks, half):
    first = half * SUBLANES * per_chunk + base
    return [ref[pl.ds(first + r, SUBLANES, stride=per_chunk), :] for r in range(order)]


def one_minus_exp(y):
    series = jnp.ones_like(y)
    for k in range(11, 1, -1):
        series = 1.0 - (y * (1.0 / k)) * series
    return jnp.where(y < 0.5, y * series, 1.0 - jnp.exp(-y))


def weights_of(residue, rate):
    return residue * jnp.sqrt(one_minus_exp(2.0 * rate))


def state_kernel(places, order, decays_ref, rate_ref, residue_ref, k_ref, v_ref, series_ref, state_ref):
    chunks, length = len(places), k_ref.shape[1]
    tokens = length // SUBLANES
    halves = chunks // SUBLANES

    def build(chunk):
        rows = pl.ds(places[chunk] * LANES, LANES)
        gated = k_ref[rows, :].astype(jnp.float32) * v_ref[rows, :].astype(jnp.float32)
        series_ref[chunk_rows(chunk, length), :] = gated.T

    weight = weights_of(residue_ref[...], rate_ref[...])
    for chunk in range(chunks):
        state_ref[pl.ds((2 * chunk + 1) * order, order), :] = weight
    for chunk in range(SUBLANES):
        build(chunk)
    for half in range(halves):
        decay = mode_rows(decays_ref, 0, order, order, chunks, half)
        square = [one * one for one in decay]

        def steps(i, state):
            state = list(state)
            for u in range(0, tokens, 2):
                x = series_ref[token_rows(half, length, i * tokens + u), :]
                y = series_ref[token_rows(half, length, i * tokens + u + 1), :]
                for r in range(order):
                    state[r] = square[r] * state[r] + (decay[r] * x + y)
            return tuple(state)

        state = (jnp.zeros((SUBLANES, LANES), jnp.float32),) * order
        for i in range(SUBLANES):
            state = steps(i, state)
            if half + 1 < halves:
                build((half + 1) * SUBLANES + i)
        for r in range(order):
            state_ref[pl.ds(half * SUBLANES * 2 * order + r, SUBLANES, stride=2 * order), :] = state[r]


def prefix_kernel(length, members, rate_ref, ends_ref, starts_ref):
    span_decay = jnp.exp(-float(length) * rate_ref[...])
    carry = jnp.zeros(rate_ref.shape, jnp.float32)
    for block in range(len(members)):
        starts_ref[members.index(block)] = carry
        carry = span_decay * carry + ends_ref[members.index(block), : rate_ref.shape[0]]


def tree_sum(terms):
    terms = list(terms)
    while len(terms) > 1:
        terms = [terms[i] + terms[i + 1] if i + 1 < len(terms) else terms[i] for i in range(0, len(terms), 2)]
    return terms[0]


def leaving(chunk, places, gated_ref, out_ref, sems):
    rows = pl.ds(places[chunk] * LANES, LANES)
    return pltpu.make_async_copy(gated_ref.at[rows, :], out_ref.at[rows, :], sems.at[chunk])


def finish(chunk, places, conv_ref, q_ref, gated_ref, out_ref, sems):
    length = conv_ref.shape[0] // len(places)
    rows = pl.ds(places[chunk] * LANES, LANES)
    conv = conv_ref[chunk_rows(chunk, length), :].T
    gated_ref[rows, :] = (q_ref[rows, :].astype(jnp.float32) * conv).astype(jnp.bfloat16)
    leaving(chunk, places, gated_ref, out_ref, sems).start()


def local_kernel(
    places, order, decays_ref, weights_ref, series_ref, gain_ref, q_ref, conv_ref, dense_ref, out_ref, gated_ref, sems
):
    chunks = len(places)
    length = series_ref.shape[0] // chunks
    for half in range(chunks // SUBLANES):
        decay = mode_rows(decays_ref, 0, order, order, chunks, half)
        weight = mode_rows(weights_ref, order, order, 2 * order, chunks, half)
        for r in range(order):
            dense_ref[half, 0, r] = decay[r]
            dense_ref[half, 1, r] = weight[r]
        own = places[half * SUBLANES : (half + 1) * SUBLANES]
        gain = jnp.concatenate([gain_ref[pl.ds(place, 1), :] for place in own], axis=0)

        def steps(i, state):
            state = list(state)
            for u in range(UNROLL):
                rows = token_rows(half, length, i * UNROLL + u)
                x = series_ref[rows, :]
                for r in range(order):
                    state[r] = decay[r] * state[r] + x
                terms = [weight[r] * state[r] for r in range(order)]
                conv_ref[rows, :] = tree_sum(terms + [gain * x])
            return tuple(state)

        zero = jnp.zeros((SUBLANES, LANES), jnp.float32)
        lax.fori_loop(0, length // UNROLL, steps, (zero,) * order)

    @pl.when(lax.axis_index("seq") == 0)
    def _():
        for chunk in range(chunks):
            finish(chunk, places, conv_ref, q_ref, gated_ref, out_ref, sems)
        for chunk in range(chunks):
            leaving(chunk, places, gated_ref, out_ref, sems).wait()


def output_kernel(
    places, order, dense_ref, carry_ref, local_ref, q_ref, _, out_ref, conv_ref, gated_ref, sems
):
    chunks = len(places)
    length = local_ref.shape[0] // chunks
    tokens = length // SUBLANES

    @pl.when(lax.axis_index("seq") > 0)
    def _():
        for half in range(chunks // SUBLANES):
            decay = [dense_ref[half, 0, r] for r in range(order)]
            weight = [dense_ref[half, 1, r] for r in range(order)]
            carry = mode_rows(carry_ref, 0, order, order, chunks, half)

            def steps(i, fading):
                fading = list(fading)
                for u in range(tokens):
                    rows = token_rows(half, length, i * tokens + u)
                    fading = [decay[r] * fading[r] for r in range(order)]
                    conv_ref[rows, :] = tree_sum(fading + [local_ref[rows, :]])
                return tuple(fading)

            fading = tuple(weight[r] * carry[r] for r in range(order))
            if half == 0:
                lax.fori_loop(0, SUBLANES, steps, fading)
            else:
                for i in range(SUBLANES):
                    fading = steps(i, fading)
                    finish((half - 1) * SUBLANES + i, places, conv_ref, q_ref, gated_ref, out_ref, sems)
        for chunk in range(chunks - SUBLANES, chunks):
            finish(chunk, places, conv_ref, q_ref, gated_ref, out_ref, sems)
        for chunk in range(chunks):
            leaving(chunk, places, gated_ref, out_ref, sems).wait()


def call(kernel, out_shape, *args, in_spaces=None, out_spaces=None, aliases=None, scratch=(), flops=0):
    in_bytes = sum(a.size * a.dtype.itemsize for a in args)
    in_spaces = in_spaces or [pl.ANY if i in (aliases or {}) else pltpu.VMEM for i in range(len(args))]
    out_spaces = out_spaces or jax.tree.map(lambda _: pltpu.VMEM, out_shape)
    return pl.pallas_call(
        kernel,
        out_shape=out_shape,
        in_specs=[pl.BlockSpec(memory_space=space) for space in in_spaces],
        out_specs=jax.tree.map(lambda space: pl.BlockSpec(memory_space=space), out_spaces),
        scratch_shapes=list(scratch),
        input_output_aliases=aliases or {},
        compiler_params=pltpu.CompilerParams(vmem_limit_bytes=VMEM_LIMIT),
        cost_estimate=pl.CostEstimate(flops=flops, bytes_accessed=in_bytes, transcendentals=0),
    )(*args)


def to_chunks(pieces):
    owners, rows, own = pieces.shape
    if own == LANES:
        return pieces
    if own < LANES:
        group = LANES // own
        return pieces.reshape(owners // group, group, rows, own).swapaxes(1, 2).reshape(-1, rows, LANES)
    return pieces.reshape(owners, rows, own // LANES, LANES).swapaxes(1, 2).reshape(-1, rows, LANES)


def from_chunks(pieces, owners):
    chunks, rows, _ = pieces.shape
    own = chunks * LANES // owners
    if own == LANES:
        return pieces
    if own < LANES:
        group = LANES // own
        return pieces.reshape(chunks, rows, group, own).swapaxes(1, 2).reshape(owners, rows, own)
    return pieces.reshape(owners, own // LANES, rows, LANES).swapaxes(1, 2).reshape(owners, rows, own)


def all_to_all(pieces, members):
    return lax.all_to_all(pieces, "seq", split_axis=0, concat_axis=0, axis_index_groups=[members], tiled=True)


def shards(blocks, q_proj, k_proj, value_projection, residues, rates, direct_gain):
    channels, length = q_proj.shape
    order = residues.shape[1]
    chunks = channels // LANES
    f32 = jnp.float32

    members, places = list(range(blocks)), list(range(chunks))
    if blocks == chunks:
        far, middle = blocks // 2, blocks * 11 // 16
        upper = [middle] + [block for block in members[:far - 1:-1] if block != middle]
        members = [block for one in upper for block in (one, one - far)]
        places = list(members)

    own_rates, own_residues = rates.T, residues.T
    copies = call(
        copies_kernel,
        jax.ShapeDtypeStruct((blocks,) + own_rates.shape, f32),
        pltpu.with_memory_space_constraint(own_rates, pltpu.HBM),
        in_spaces=[pl.ANY],
        scratch=[pltpu.VMEM(own_rates.shape, f32), pltpu.SemaphoreType.DMA],
        flops=COPIES_COST,
    )
    decays = to_chunks(all_to_all(copies, members)).reshape(chunks * order, LANES)

    whole_chunk = own_rates.shape[1] == LANES
    unused = jnp.zeros((order, LANES), f32)
    series, ends = call(
        functools.partial(state_kernel, places, order),
        (
            jax.ShapeDtypeStruct((length * chunks, LANES), f32),
            jax.ShapeDtypeStruct((chunks * 2 * order, LANES), f32),
        ),
        decays,
        own_rates if whole_chunk else unused,
        own_residues if whole_chunk else unused,
        k_proj,
        value_projection,
        flops=2 * order * channels * length,
    )
    local_series, ends = lax.optimization_barrier((series, ends))
    ends = from_chunks(ends.reshape(chunks, 2 * order, LANES), blocks)
    if not whole_chunk:
        ends = ends.at[:, order:].set(weights_of(own_residues, own_rates))
    ends = all_to_all(ends, members)
    weights = to_chunks(ends).reshape(chunks * 2 * order, LANES)
    out_shape = jax.ShapeDtypeStruct((channels, length), jnp.bfloat16)
    out_scratch = [pltpu.VMEM(out_shape.shape, out_shape.dtype), pltpu.SemaphoreType.DMA((chunks,))]
    local, dense, out = call(
        functools.partial(local_kernel, places, order),
        (
            jax.ShapeDtypeStruct((length * chunks, LANES), f32),
            jax.ShapeDtypeStruct((chunks // SUBLANES, 2, order, SUBLANES, LANES), f32),
            out_shape,
        ),
        decays,
        weights,
        local_series,
        direct_gain.reshape(chunks, LANES),
        q_proj,
        out_spaces=(pltpu.VMEM, pltpu.VMEM, pl.ANY),
        scratch=out_scratch,
        flops=4 * order * channels * length,
    )
    starts = call(
        functools.partial(prefix_kernel, length, members),
        jax.ShapeDtypeStruct((blocks,) + own_rates.shape, f32),
        own_rates,
        ends,
    )
    starts = all_to_all(starts, members)
    carry = to_chunks(starts).reshape(chunks * order, LANES)
    return call(
        functools.partial(output_kernel, places, order),
        out_shape,
        dense,
        carry,
        local,
        q_proj,
        out,
        out_spaces=pl.ANY,
        aliases={4: 0},
        scratch=[pltpu.VMEM((length * chunks, LANES), f32)] + out_scratch,
        flops=2 * order * channels * length,
    )


def solution(mesh):
    return jax.shard_map(
        functools.partial(shards, mesh.shape["seq"]),
        mesh=mesh,
        in_specs=(
            P("chan", ("groups", "seq")),
            P("chan", ("groups", "seq")),
            P("chan", ("groups", "seq")),
            P(("chan", "seq"), None),
            P(("chan", "seq"), None),
            P("chan"),
        ),
        out_specs=P("chan", ("groups", "seq")),
        check_vma=False,
    )
```
